32 devices in a mesh: items: 8 (over y, x, core), band: 4 (over z).
Axes of the slice: x: 2, y: 2, z: 4, core: 2. Of those that a mesh axis runs over, the one named last changes fastest.
Arguments:
- tokens: bfloat16 [640, 64, 768], P('band', 'items'), may hold values from -6 to 6
- lengths: int32 [64], P('items'), may hold values from 257 to 577, as said below
- norm_attn: float32 [768], replicated, may hold values from 0.5 to 1.5
- w_query: bfloat16 [768, 768], replicated, may hold values from -0.21875 to 0.21875
- w_key: bfloat16 [768, 768], replicated, may hold values from -0.21875 to 0.21875
- w_value: bfloat16 [768, 768], replicated, may hold values from -0.21875 to 0.21875
- w_out: bfloat16 [768, 768], replicated, may hold values from -0.875 to 0.875
- norm_ffn: float32 [768], replicated, may hold values from 0.5 to 1.5
- w_gate: bfloat16 [768, 2048], replicated, may hold values from -0.21875 to 0.21875
- w_up: bfloat16 [768, 2048], replicated, may hold values from -0.21875 to 0.21875
- w_down: bfloat16 [2048, 768], replicated, may hold values from -0.125 to 0.125
- cotangent: bfloat16 [640, 64, 768], P('band', 'items'), may hold values from -6 to 6
Outputs:
- output: bfloat16 [640, 64, 768], P('band', 'items')
- grad_tokens: bfloat16 [640, 64, 768], P('band', 'items')
- grad_norm_attn: float32 [768], P(('items', 'band'))
- grad_w_query: float32 [768, 768], P(('items', 'band'))
- grad_w_key: float32 [768, 768], P(('items', 'band'))
- grad_w_value: float32 [768, 768], P(('items', 'band'))
- grad_w_out: float32 [768, 768], P(('items', 'band'))
- grad_norm_ffn: float32 [768], P(('items', 'band'))
- grad_w_gate: float32 [768, 2048], P(('items', 'band'))
- grad_w_up: float32 [768, 2048], P(('items', 'band'))
- grad_w_down: float32 [2048, 768], P(('items', 'band'))
The draws below stay inside these ranges and needn't reach their ends.
Inputs may be any that keep to these rules, and one draw needn't show every extreme that they name: `lengths`: each item has 257 or 577 real tokens; every aligned group of 8 items holds both values.
All inputs are finite; a program needn't handle non-finite values.
Results may differ from the reference program's by a relative error of at most 0.018.
Values may be sent and summed in bfloat16 or wider, within the bound.
A program may use at most 320 MiB of HBM per device.

```python
import jax
import jax.numpy as jnp
from jax import lax

D = 768
HEADS = 12
HEAD_DIM = 64
FF = 2048
SEQ = 640
LONG = 577
SHORT = 257
ITEMS_DEV = 8
ITEMS = 64


def draw_lengths(key, part):
    key = jax.random.fold_in(key, 11)
    key_pick, key_force = jax.random.split(key)
    picked = jax.random.randint(key_pick, (ITEMS,), 0, 2)
    group_count = ITEMS // ITEMS_DEV
    forced = jax.random.randint(key_force, (group_count,), 0, ITEMS_DEV)
    forced_all = jnp.repeat(forced, ITEMS_DEV, total_repeat_length=ITEMS)
    slot = jnp.arange(ITEMS) % ITEMS_DEV
    make_long = (slot == forced_all) | (picked == 1) & (slot != (forced_all + 1) % ITEMS_DEV)
    return jnp.where(make_long, LONG, SHORT).astype(jnp.int32)


def shard_levels(stream_key, extent, cuts, smallest, largest):
    loudness = 1.0
    for axis_at, blocks in cuts:
        heights = jax.random.uniform(jax.random.fold_in(jax.random.fold_in(stream_key, 6), axis_at), (blocks,), jnp.float32, smallest / len(cuts), largest / len(cuts))
        loudness = loudness * jnp.repeat(jnp.exp(heights), extent[axis_at] // blocks).reshape((-1,) + (1,) * (len(extent) - 1 - axis_at))
    return loudness


def normal_values(own_key, shape, spread, limit, shards=(), held_as=jnp.bfloat16):
    drawn = spread * jax.random.normal(own_key, shape, jnp.float32)
    if shards:
        drawn = drawn * shard_levels(own_key, shape, shards, -0.22, 0.18)
    return jnp.clip(drawn, -limit, limit).astype(held_as)


def setup_inputs(seed: int = 0) -> dict:
    key_of = jax.random.split(jax.random.key(seed), 13)
    return {
        "tokens": normal_values(key_of[0], (SEQ, ITEMS, D), 1.0, 6.0, ((0, 4), (1, 8))),
        "lengths": draw_lengths(jax.random.fold_in(key_of[12], 71), 0),
        "norm_attn": jnp.clip(1.0 + 0.1 * jax.random.normal(key_of[2], (D,), jnp.float32), 0.5, 1.5),
        "w_query": normal_values(key_of[3], (D, D), D ** -0.5, 0.21875),
        "w_key": normal_values(key_of[4], (D, D), D ** -0.5, 0.21875),
        "w_value": normal_values(key_of[5], (D, D), D ** -0.5, 0.21875),
        "w_out": normal_values(key_of[6], (D, D), (D // 16) ** -0.5, 0.875),
        "norm_ffn": jnp.clip(1.0 + 0.1 * jax.random.normal(key_of[7], (D,), jnp.float32), 0.5, 1.5),
        "w_gate": normal_values(key_of[8], (D, FF), D ** -0.5, 0.21875),
        "w_up": normal_values(key_of[9], (D, FF), D ** -0.5, 0.21875),
        "w_down": normal_values(key_of[10], (FF, D), FF ** -0.5, 0.125),
        "cotangent": normal_values(key_of[11], (SEQ, ITEMS, D), 1.0, 6.0, ((0, 4), (1, 8))),
    }


EPS = 1e-05
NEG = -1e+30
ROPE_BASE = 10000.0

@jax.custom_vjp
def low(v):
    return lax.optimization_barrier(v.astype(jnp.bfloat16)).astype(jnp.float32)

@jax.custom_vjp
def low_back(v):
    return v

def low_keep(v):
    return (low(v), None)

def low_pass(kept, grad):
    return (grad,)

def back_keep(v):
    return (v, None)

def back_low(kept, grad):
    return (low(grad),)
low.defvjp(low_keep, low_pass)
low_back.defvjp(back_keep, back_low)

def rope_tables(positions, head_size):
    half_dim = head_size // 2
    frequency = jnp.exp(-jnp.log(ROPE_BASE) * (2.0 * jnp.arange(half_dim, dtype=jnp.float32) / head_size))
    angles = positions.astype(jnp.float32)[:, None] * frequency[None, :]
    return (jnp.cos(angles), jnp.sin(angles))

def rotate(vector, cos_table, sin_table):
    half_dim = vector.shape[-1] // 2
    lower_half = vector[..., :half_dim]
    upper_half = vector[..., half_dim:]
    return jnp.concatenate([lower_half * cos_table - upper_half * sin_table, lower_half * sin_table + upper_half * cos_table], -1)

def layer_item(inputs, length, weights):
    norm_attn, w_query, w_key, w_value, w_out, norm_ffn, w_gate, w_up, w_down = weights
    highest = lax.Precision.HIGHEST
    seq_len = inputs.shape[0]
    positions = jnp.arange(seq_len).astype(jnp.int32)
    cos_table, sin_table = rope_tables(positions, HEAD_DIM)
    cos_table = cos_table[:, None, :]
    sin_table = sin_table[:, None, :]
    head_shape = (seq_len, HEADS, HEAD_DIM)
    inv_one = lax.rsqrt(lax.optimization_barrier(jnp.mean(inputs * inputs, -1, keepdims=True)) + EPS)
    normed = low(inputs * inv_one * norm_attn)
    queries = low(rotate(low_back(jnp.dot(normed, w_query, precision=highest)).reshape(head_shape), cos_table, sin_table))
    key_rows = low(rotate(low_back(jnp.dot(normed, w_key, precision=highest)).reshape(head_shape), cos_table, sin_table))
    values = low_back(low(jnp.dot(normed, w_value, precision=highest))).reshape(head_shape)
    scores = low_back(jnp.einsum('qhd,khd->hqk', queries, key_rows, precision=highest) * HEAD_DIM ** (-0.5))
    allowed = ((positions[None, :] <= positions[:, None]) & (positions[None, :] < length))[None]
    scores = jnp.where(allowed, scores, NEG)
    row_top = lax.optimization_barrier(jnp.max(scores, -1, keepdims=True))
    exp_scores = jnp.where(allowed, jnp.exp(scores - row_top), 0.0)
    attn_prob = exp_scores / lax.optimization_barrier(jnp.sum(exp_scores, -1, keepdims=True))
    attended = jnp.einsum('hqk,khd->qhd', low(attn_prob), values, precision=highest).reshape(seq_len, HEADS * HEAD_DIM)
    resid = inputs + low_back(jnp.dot(low_back(low(attended)), w_out, precision=highest))
    inv_two = lax.rsqrt(lax.optimization_barrier(jnp.mean(resid * resid, -1, keepdims=True)) + EPS)
    normed_two = low(resid * inv_two * norm_ffn)
    gate_pre = low_back(jnp.dot(normed_two, w_gate, precision=highest))
    upward = low_back(jnp.dot(normed_two, w_up, precision=highest))
    hidden = low(jax.nn.silu(gate_pre) * upward)
    return resid + jnp.dot(hidden, w_down, precision=highest)

def reference(tokens, lengths, norm_attn, w_query, w_key, w_value, w_out, norm_ffn, w_gate, w_up, w_down, cotangent):
    weights = (norm_attn.astype(jnp.float32), w_query.astype(jnp.float32), w_key.astype(jnp.float32), w_value.astype(jnp.float32), w_out.astype(jnp.float32), norm_ffn.astype(jnp.float32), w_gate.astype(jnp.float32), w_up.astype(jnp.float32), w_down.astype(jnp.float32))
    inputs = jnp.transpose(tokens.astype(jnp.float32), (1, 0, 2))

    def forward(all_inputs, all_weights):
        item_layer = jax.checkpoint(layer_item)
        return lax.map(lambda paired: item_layer(paired[0], paired[1], all_weights), (all_inputs, lengths))
    result_rows, pullback = jax.vjp(forward, inputs, weights)
    grad_inputs, grad_weights = pullback(jnp.transpose(cotangent.astype(jnp.float32), (1, 0, 2)))
    output = jnp.transpose(result_rows, (1, 0, 2)).astype(jnp.bfloat16)
    grad_tokens = jnp.transpose(grad_inputs, (1, 0, 2)).astype(jnp.bfloat16)
    return (output, grad_tokens, grad_weights[0], grad_weights[1], grad_weights[2], grad_weights[3], grad_weights[4], grad_weights[5], grad_weights[6], grad_weights[7], grad_weights[8])
```

```python
import functools

import jax
import jax.numpy as jnp
from jax import lax
from jax.experimental import pallas as pl
from jax.experimental.pallas import tpu as pltpu
from jax.sharding import PartitionSpec as P

HEAD_DIM = 64
HALF = HEAD_DIM // 2
EPS = 1e-05
NEG = -1e30
ROPE_BASE = 10000.0
LOG2E = 1.4426950408889634
SCALE = HEAD_DIM**-0.5
BLOCK = 256
F32 = jnp.float32
LOW = jnp.bfloat16


def dot_nn(left, right):
    return lax.dot_general(left, right, (((1,), (0,)), ((), ())), preferred_element_type=F32)


def dot_nt(left, right):
    return lax.dot_general(left, right, (((1,), (1,)), ((), ())), preferred_element_type=F32)


def dot_tn(left, right):
    return lax.dot_general(left, right, (((0,), (0,)), ((), ())), preferred_element_type=F32)


def vmem(count):
    return [pl.BlockSpec(memory_space=pltpu.VMEM)] * count


def smem():
    return pl.BlockSpec(memory_space=pltpu.SMEM)


def params(mib):
    return pltpu.CompilerParams(vmem_limit_bytes=mib * 2**20)


def log2_of(number):
    return number.bit_length() - 1


def split_kernel(items, chunk, band_items_ref, rows_ref, *outs):
    size = items * chunk
    row = lax.broadcasted_iota(jnp.int32, (size, size), 0)
    col = lax.broadcasted_iota(jnp.int32, (size, size), 1)
    item = (row >> log2_of(chunk)) + band_items_ref[0]
    item = jnp.where(item >= items, item - items, item)
    order = jnp.where(col == (row & (chunk - 1)) * items + item, 1.0, 0.0).astype(LOW)
    for block in range(rows_ref.shape[0] // size):
        moved = dot_nn(order, rows_ref[block * size : (block + 1) * size, :]).astype(LOW)
        for at, out in enumerate(outs):
            out[block * chunk : (block + 1) * chunk, :] = moved[at * chunk : (at + 1) * chunk]


def split_items(array, band, bands):
    band_rows, items, width = array.shape
    chunk = 32 if band_rows % 32 == 0 else 16
    per = items // bands
    return pl.pallas_call(
        functools.partial(split_kernel, items, chunk),
        name="split_items",
        out_shape=[jax.ShapeDtypeStruct((band_rows, width), LOW)] * items,
        in_specs=[smem()] + vmem(1),
        out_specs=vmem(items),
        compiler_params=params(32),
    )(jnp.reshape(band * per, (1,)), array.reshape(band_rows * items, width))


def merge_kernel(items, per, chunk, band_ref, *refs):
    ins, out = refs[:-1], refs[-1]
    size, bands = items * chunk, items // per
    row = lax.broadcasted_iota(jnp.int32, (size, size), 0)
    col = lax.broadcasted_iota(jnp.int32, (size, size), 1)
    number = col >> log2_of(chunk)
    source = band_ref[0] - (number >> log2_of(per))
    source = jnp.where(source < 0, source + bands, source)
    item = source * per + (number & (per - 1))
    order = jnp.where(row == (col & (chunk - 1)) * items + item, 1.0, 0.0).astype(LOW)
    for block in range(out.shape[0] // size):
        parts = jnp.concatenate([part[block * chunk : (block + 1) * chunk, :] for part in ins], 0)
        out[block * size : (block + 1) * size, :] = dot_nn(order, parts).astype(LOW)


def merge_items(parts, band, bands):
    items = len(parts)
    band_rows, width = parts[0].shape
    chunk = 32 if band_rows % 32 == 0 else 16
    return pl.pallas_call(
        functools.partial(merge_kernel, items, items // bands, chunk),
        name="merge_items",
        out_shape=jax.ShapeDtypeStruct((band_rows * items, width), LOW),
        in_specs=[smem()] + vmem(items),
        out_specs=vmem(1)[0],
        compiler_params=params(32),
    )(jnp.reshape(band, (1,)), *parts).reshape(band_rows, items, width)


def band_start(band, shift, bands, band_rows):
    return pl.multiple_of(lax.rem(band + shift + bands, bands) * band_rows, band_rows)


def exchange(parts, bands, per, item):
    kept = [parts[item]]
    for shift in range(1, bands):
        kept.append(
            lax.ppermute(
                parts[shift * per + item], "band", [(i, (i + shift) % bands) for i in range(bands)]
            )
        )
    return kept


def rope(vector, cos, sin):
    parts = []
    for at in range(0, vector.shape[0], HEAD_DIM):
        lower, upper = vector[at : at + HALF], vector[at + HALF : at + HEAD_DIM]
        parts += [lower * cos - upper * sin, lower * sin + upper * cos]
    return jnp.concatenate(parts, 0)


def query_blocks(seq):
    return [(start, min(start + BLOCK, seq)) for start in range(0, seq, BLOCK)]


def limits(start, stop, length):
    position = start + lax.broadcasted_iota(jnp.int32, (1, stop - start), 1)
    return jnp.minimum(position, length - 1)


def score_parts(keys, queries, start, stop, length):
    parts = []
    if start:
        parts.append((0, BLOCK, dot_tn(keys[:, :BLOCK], queries)))
    first = min(start, BLOCK)
    late = dot_tn(keys[:, first:stop], queries)
    position = first + lax.broadcasted_iota(jnp.int32, late.shape, 0)
    late = jnp.where(position <= limits(start, stop, length), late, NEG)
    parts.append((first, stop, late))
    return parts


def norm_rows(inputs):
    return lax.rsqrt(jnp.mean(inputs * inputs, -1, keepdims=True) + EPS)


def attend_kernel(bands, scalars, *refs):
    chunks, refs = refs[:bands], refs[bands:]
    weights, gain, cos, sin, x, query, key, value, attended_t, attended, log_total, normed = refs
    seq, width = x.shape
    band_rows = seq // bands
    band, length = scalars[0], scalars[1]
    for shift, chunk in enumerate(chunks):
        x[pl.ds(band_start(band, -shift, bands, band_rows), band_rows), :] = chunk[...]
    tile = 128
    for at in range(0, seq, tile):
        inputs = x[at : at + tile, :].astype(F32)
        normed[at : at + tile, :] = (inputs * norm_rows(inputs) * gain[...]).astype(LOW)

    project = 256

    def project_tile(at, _):
        rows = pl.ds(pl.multiple_of(at * project, project), project)
        for part, out, scaled in ((0, query, SCALE * LOG2E), (1, key, 1.0)):
            source = pl.ds(pl.multiple_of(part * width + at * project, project), project)
            out[rows, :] = (rope(dot_nt(weights[source, :], normed[...]), cos[...], sin[...]) * scaled).astype(LOW)
        source = pl.ds(pl.multiple_of(2 * width + at * project, project), project)
        value[rows, :] = dot_nt(weights[source, :], normed[...]).astype(LOW)
        return 0

    lax.fori_loop(0, width // project, project_tile, 0)

    def head(at, _):
        for which in range(2):
            number = at * 2 + which
            rows = pl.ds(pl.multiple_of(number * HEAD_DIM, HEAD_DIM), HEAD_DIM)
            keys, values = key[rows, :], value[rows, :]
            for start, stop in query_blocks(seq):
                parts = score_parts(keys, query[rows, start:stop], start, stop, length)
                top = functools.reduce(jnp.maximum, [jnp.max(s, 0, keepdims=True) for _, _, s in parts])
                total = jnp.zeros_like(top)
                acc = jnp.zeros((HEAD_DIM, stop - start), F32)
                for first, last, scores in parts:
                    prob = jnp.exp2(scores - top)
                    total += jnp.sum(prob, 0, keepdims=True)
                    acc += dot_nn(values[:, first:last], prob.astype(LOW))
                attended_t[rows, start:stop] = (acc / total).astype(LOW)
                log_total[number, :, start:stop] = top + jnp.log2(total)
        return 0

    lax.fori_loop(0, width // HEAD_DIM // 2, head, 0)
    for at in range(0, width, project):
        attended[:, at : at + project] = attended_t[at : at + project, :].T


def attend(chunks, scalars, weights_t, gain, cos, sin):
    bands = len(chunks)
    band_rows, width = chunks[0].shape
    seq = bands * band_rows
    low_t = jax.ShapeDtypeStruct((width, seq), LOW)
    low = jax.ShapeDtypeStruct((seq, width), LOW)
    pairs = seq * seq * width
    return pl.pallas_call(
        functools.partial(attend_kernel, bands),
        name="attend",
        out_shape=[low, low_t, low_t, low_t, low_t, low, jax.ShapeDtypeStruct((width // HEAD_DIM, 1, seq), F32)],
        in_specs=[smem()] + vmem(bands + 4),
        out_specs=vmem(7),
        scratch_shapes=[pltpu.VMEM((seq, width), LOW)],
        compiler_params=params(48),
        cost_estimate=pl.CostEstimate(
            flops=6 * seq * width * width + 12 * pairs, bytes_accessed=20 * seq * width, transcendentals=0
        ),
    )(scalars, *chunks, weights_t, gain, cos, sin)


def feed_kernel(bands, follows, scalars, *refs):
    chunks, refs = refs[:bands], refs[bands:]
    x, attended, attended_t, w_out, gain, w_gate, w_up, w_down = refs[:8]
    refs = refs[8:]
    prev = None
    if follows:
        prev, refs = refs[:5], refs[5:]
    outs, refs = refs[:bands], refs[bands:]
    grad_resid_low, grad_attended_t, g_gate, g_up, g_down, g_out, g_norm = refs[:7]
    cot, resid, normed, normed_t, out_acc, back_acc = refs[7:]
    seq, width = x.shape
    band_rows = seq // bands
    band = scalars[0]
    step = pl.program_id(0)
    tile = 128

    @pl.when(step == 0)
    def _():
        for shift, chunk in enumerate(chunks):
            cot[pl.ds(band_start(band, -shift, bands, band_rows), band_rows), :] = chunk[...]
        for at in range(0, seq, tile):
            rows = slice(at, at + tile)
            total = x[rows, :].astype(F32) + dot_nn(attended[rows, :], w_out[...])
            resid[rows, :] = total
            out_acc[rows, :] = total
            low = (total * norm_rows(total) * gain[...]).astype(LOW)
            normed[rows, :] = low
            normed_t[:, rows] = low.T
        back_acc[...] = jnp.zeros_like(back_acc)

    gate = dot_nn(normed[...], w_gate[...])
    upward = dot_nn(normed[...], w_up[...])
    grad_hidden = dot_nt(cot[...], w_down[...])
    sig = 0.5 * jnp.tanh(0.5 * gate) + 0.5
    silu = gate * sig
    hidden = (silu * upward).astype(LOW)
    grad_gate = (grad_hidden * upward * (sig + silu * (1.0 - sig))).astype(LOW)
    grad_upward = (grad_hidden * silu).astype(LOW)
    out_acc[...] += dot_nn(hidden, w_down[...])
    back_acc[...] += dot_nt(grad_gate, w_gate[...]) + dot_nt(grad_upward, w_up[...])

    def put(out, at, grad):
        if follows:
            grad += prev[at][...].astype(F32)
        out[...] = grad.astype(LOW)

    put(g_down, 2, dot_nn(hidden.T, cot[...]))
    put(g_gate, 0, dot_nn(normed_t[...], grad_gate))
    put(g_up, 1, dot_nn(normed_t[...], grad_upward))

    @pl.when(step == pl.num_programs(0) - 1)
    def _():
        norm_sum = jnp.zeros((1, width), F32)
        for at in range(0, seq, tile):
            rows = slice(at, at + tile)
            total, incoming = resid[rows, :], back_acc[rows, :]
            inv = norm_rows(total)
            scaled = total * inv
            norm_sum += jnp.sum(incoming * scaled, 0, keepdims=True)
            weighted = incoming * gain[...]
            grad = cot[rows, :].astype(F32) + inv * (
                weighted - scaled * jnp.mean(weighted * scaled, -1, keepdims=True)
            )
            grad_resid_low[rows, :] = grad.astype(LOW)
        if follows:
            norm_sum += prev[4][...]
        g_norm[...] = norm_sum
        grad_attended_t[...] = dot_nt(w_out[...], grad_resid_low[...]).astype(LOW)
        put(g_out, 3, dot_nn(attended_t[...], grad_resid_low[...]))
        for shift, out in enumerate(outs):
            out[...] = out_acc[pl.ds(band_start(band, shift, bands, band_rows), band_rows), :].astype(LOW)


def feed(chunks, scalars, x, attended, attended_t, w_out, gain, w_gate, w_up, w_down, prev):
    bands = len(chunks)
    seq, width = x.shape
    ff = w_gate.shape[1]
    wide = 512
    whole = lambda *shape: pl.BlockSpec(shape, lambda i: (0,) * len(shape))
    columns = pl.BlockSpec((width, wide), lambda i: (0, i))
    rows = pl.BlockSpec((wide, width), lambda i: (i, 0))
    grad_specs = [columns, columns, rows, whole(width, width), whole(1, width)]
    band_rows = seq // bands
    return pl.pallas_call(
        functools.partial(feed_kernel, bands, prev is not None),
        name="feed",
        grid=(ff // wide,),
        out_shape=[jax.ShapeDtypeStruct((band_rows, width), LOW)] * bands
        + [
            jax.ShapeDtypeStruct((seq, width), LOW),
            jax.ShapeDtypeStruct((width, seq), LOW),
            jax.ShapeDtypeStruct((width, ff), LOW),
            jax.ShapeDtypeStruct((width, ff), LOW),
            jax.ShapeDtypeStruct((ff, width), LOW),
            jax.ShapeDtypeStruct((width, width), LOW),
            jax.ShapeDtypeStruct((1, width), F32),
        ],
        in_specs=[smem()]
        + [whole(band_rows, width)] * bands
        + [whole(seq, width), whole(seq, width), whole(width, seq), whole(width, width), whole(1, width)]
        + [columns, columns, rows]
        + (grad_specs if prev is not None else []),
        out_specs=[whole(band_rows, width)] * bands + [whole(seq, width), whole(width, seq)] + grad_specs,
        scratch_shapes=[
            pltpu.VMEM((seq, width), LOW),
            pltpu.VMEM((seq, width), F32),
            pltpu.VMEM((seq, width), LOW),
            pltpu.VMEM((width, seq), LOW),
            pltpu.VMEM((seq, width), F32),
            pltpu.VMEM((seq, width), F32),
        ],
        compiler_params=params(60),
        cost_estimate=pl.CostEstimate(
            flops=18 * seq * width * ff + 6 * seq * width * width, bytes_accessed=12 * width * ff, transcendentals=0
        ),
    )(scalars, *chunks, x, attended, attended_t, w_out, gain, w_gate, w_up, w_down, *(prev or ()))


def back_kernel(bands, follows, scalars, *refs):
    x, grad_resid, grad_attended, attended, query, key, value, log_total, w_query, w_key, w_value = refs[:11]
    gain, cos, sin = refs[11:14]
    refs = refs[14:]
    prev = None
    if follows:
        prev, refs = refs[:2], refs[2:]
    outs, refs = refs[:bands], refs[bands:]
    g_weights, g_norm, grads, normed_t, back = refs
    seq, width = x.shape
    band_rows = seq // bands
    band, length = scalars[0], scalars[1]
    blocks = query_blocks(seq)

    def head(at, _):
        for which in range(2):
            number = at * 2 + which
            rows = pl.ds(pl.multiple_of(number * HEAD_DIM, HEAD_DIM), HEAD_DIM)
            keys, values = key[rows, :], value[rows, :]
            delta_all = jnp.sum(grad_attended[rows, :].astype(F32) * attended[rows, :].astype(F32), 0, keepdims=True)
            key_grads = [0.0] * len(blocks)
            value_grads = [0.0] * len(blocks)
            for start, stop in blocks:
                queries, incoming = query[rows, start:stop], grad_attended[rows, start:stop]
                total = log_total[number, :, start:stop]
                delta = delta_all[:, start:stop]
                query_grad = 0.0
                for first, last, scores in score_parts(keys, queries, start, stop, length):
                    prob = jnp.exp2(scores - total)
                    grad_prob = dot_tn(values[:, first:last], incoming)
                    grad_score = (prob * (grad_prob - delta)).astype(LOW)
                    query_grad += dot_nn(keys[:, first:last], grad_score)
                    key_grad = dot_nt(queries, grad_score)
                    value_grad = dot_nt(incoming, prob.astype(LOW))
                    for piece, (low, high) in enumerate(blocks):
                        if first <= low and high <= last:
                            key_grads[piece] += key_grad[:, low - first : high - first]
                            value_grads[piece] += value_grad[:, low - first : high - first]
                grads[rows, start:stop] = (
                    rope(query_grad, cos[:, start:stop], -sin[:, start:stop]) * SCALE
                ).astype(LOW)
            for (start, stop), key_grad, value_grad in zip(blocks, key_grads, value_grads):
                at_key = pl.ds(pl.multiple_of(width + number * HEAD_DIM, HEAD_DIM), HEAD_DIM)
                at_value = pl.ds(pl.multiple_of(2 * width + number * HEAD_DIM, HEAD_DIM), HEAD_DIM)
                grads[at_key, start:stop] = (
                    rope(key_grad, cos[:, start:stop], -sin[:, start:stop]) * (1.0 / LOG2E)
                ).astype(LOW)
                grads[at_value, start:stop] = value_grad.astype(LOW)
        return 0

    lax.fori_loop(0, width // HEAD_DIM // 2, head, 0)

    tile = 128
    for at in range(0, seq, tile):
        inputs = x[at : at + tile, :].astype(F32)
        normed_t[:, at : at + tile] = (inputs * norm_rows(inputs) * gain[...]).astype(LOW).T
    project = 256
    for at in range(0, width, project):
        rows = slice(at, at + project)
        total = dot_nn(w_query[rows, :], grads[:width, :])
        total += dot_nn(w_key[rows, :], grads[width : 2 * width, :])
        total += dot_nn(w_value[rows, :], grads[2 * width :, :])
        back[:, rows] = total.T
        for part in range(3):
            grad = dot_nt(normed_t[rows, :], grads[part * width : (part + 1) * width, :])
            columns = slice(part * width, (part + 1) * width)
            if follows:
                grad += prev[0][rows, columns].astype(F32)
            g_weights[rows, columns] = grad.astype(LOW)
    norm_sum = jnp.zeros((1, width), F32)
    for at in range(0, seq, tile):
        rows = slice(at, at + tile)
        inputs, incoming = x[rows, :].astype(F32), back[rows, :]
        inv = norm_rows(inputs)
        scaled = inputs * inv
        norm_sum += jnp.sum(incoming * scaled, 0, keepdims=True)
        weighted = incoming * gain[...]
        back[rows, :] = grad_resid[rows, :].astype(F32) + inv * (
            weighted - scaled * jnp.mean(weighted * scaled, -1, keepdims=True)
        )
    if follows:
        norm_sum += prev[1][...]
    g_norm[...] = norm_sum
    for shift, out in enumerate(outs):
        out[...] = back[pl.ds(band_start(band, shift, bands, band_rows), band_rows), :].astype(LOW)


def back_attend(bands, scalars, x, grad_resid, grad_attended_t, attended_t, query, key, value, log_total, weights, gain, cos, sin, prev):
    seq, width = x.shape
    band_rows = seq // bands
    pairs = seq * seq * width
    args = [x, grad_resid, grad_attended_t, attended_t, query, key, value, log_total, *weights, gain, cos, sin, *(prev or ())]
    return pl.pallas_call(
        functools.partial(back_kernel, bands, prev is not None),
        name="back_attend",
        out_shape=[jax.ShapeDtypeStruct((band_rows, width), LOW)] * bands
        + [jax.ShapeDtypeStruct((width, 3 * width), LOW), jax.ShapeDtypeStruct((1, width), F32)],
        in_specs=[smem()] + vmem(len(args)),
        out_specs=vmem(bands + 2),
        scratch_shapes=[
            pltpu.VMEM((3 * width, seq), LOW),
            pltpu.VMEM((width, seq), LOW),
            pltpu.VMEM((seq, width), F32),
        ],
        compiler_params=params(48),
        cost_estimate=pl.CostEstimate(
            flops=12 * seq * width * width + 30 * pairs, bytes_accessed=24 * seq * width, transcendentals=0
        ),
    )(scalars, *args)


def rope_tables(seq):
    frequency = jnp.exp(-jnp.log(ROPE_BASE) * (2.0 * jnp.arange(HALF, dtype=F32) / HEAD_DIM))
    angles = frequency[:, None] * jnp.arange(seq, dtype=jnp.int32).astype(F32)[None, :]
    return jnp.cos(angles), jnp.sin(angles)


def per_device(
    bands,
    tokens,
    lengths,
    norm_attn,
    w_query,
    w_key,
    w_value,
    w_out,
    norm_ffn,
    w_gate,
    w_up,
    w_down,
    cotangent,
):
    band_rows, items, width = tokens.shape
    per = items // bands
    seq = bands * band_rows
    band = lax.axis_index("band")
    token_parts = split_items(tokens, band, bands)
    x_chunks = [exchange(token_parts, bands, per, item) for item in range(per)]
    cot_parts = split_items(cotangent, band, bands)
    cot_chunks = [exchange(cot_parts, bands, per, item) for item in range(per)]
    cos, sin = rope_tables(seq)
    gain_attn, gain_ffn = norm_attn.reshape(1, width), norm_ffn.reshape(1, width)
    weights_t = jnp.concatenate([w_query.T, w_key.T, w_value.T], 0)
    scalars = [
        jnp.stack([band, lax.dynamic_index_in_dim(lengths, band * per + item, keepdims=False)]).astype(jnp.int32)
        for item in range(per)
    ]
    fronts = [attend(x_chunks[i], scalars[i], weights_t, gain_attn, cos, sin) for i in range(per)]
    feeds, prev = [], None
    for i in range(per):
        x, _, _, _, attended_t, attended, _ = fronts[i]
        feeds.append(
            feed(cot_chunks[i], scalars[i], x, attended, attended_t, w_out, gain_ffn, w_gate, w_up, w_down, prev)
        )
        prev = feeds[-1][bands + 2 :]
    out_parts = [f[:bands] for f in feeds]
    g_gate, g_up, g_down, g_out, g_norm_ffn = prev
    backs, prev = [], None
    for i in range(per):
        x, query, key, value, attended_t, _, log_total = fronts[i]
        grad_resid, grad_attended_t = feeds[i][bands : bands + 2]
        backs.append(
            back_attend(
                bands, scalars[i], x, grad_resid, grad_attended_t, attended_t, query, key, value, log_total,
                (w_query, w_key, w_value), gain_attn, cos, sin, prev,
            )
        )
        prev = backs[-1][bands:]
    g_weights, g_norm_attn = prev

    def home(parts):
        came = [exchange([parts[i][k] for k in range(bands)], bands, 1, 0) for i in range(per)]
        return merge_items([came[j][k] for k in range(bands) for j in range(per)], band, bands)

    output = home(out_parts)
    grad_tokens = home([b[:bands] for b in backs])
    axes = ("items", "band")
    gains = jnp.concatenate([g_norm_attn.T, g_norm_ffn.T], 1)
    feed_sum = lax.psum_scatter(jnp.concatenate([g_gate, g_up], 1), axes, scatter_dimension=0, tiled=True).astype(F32)
    down_sum = lax.psum_scatter(g_down, axes, scatter_dimension=0, tiled=True).astype(F32)
    rest = jnp.concatenate([g_weights, g_out, gains.astype(LOW)], 1)
    rest_sum = lax.psum_scatter(rest, axes, scatter_dimension=0, tiled=True).astype(F32)
    ff = w_gate.shape[1]
    return (
        output,
        grad_tokens,
        rest_sum[:, 4 * width],
        rest_sum[:, :width],
        rest_sum[:, width : 2 * width],
        rest_sum[:, 2 * width : 3 * width],
        rest_sum[:, 3 * width : 4 * width],
        rest_sum[:, 4 * width + 1],
        feed_sum[:, :ff],
        feed_sum[:, ff:],
        down_sum,
    )


def solution(mesh):
    split = P("band", "items", None)
    rows = P(("items", "band"), None)
    flat = P(("items", "band"))
    return jax.shard_map(
        functools.partial(per_device, mesh.shape["band"]),
        mesh=mesh,
        in_specs=(split, P("items")) + (P(),) * 9 + (split,),
        out_specs=(split, split, flat, rows, rows, rows, rows, flat, rows, rows, rows),
        check_vma=False,
    )
```

```python
import functools

import jax
import jax.numpy as jnp
import numpy as np
from jax import lax
from jax.experimental import pallas as pl
from jax.experimental.pallas import tpu as pltpu
from jax.sharding import PartitionSpec as P

HEAD_DIM = 64
HALF = HEAD_DIM // 2
EPS = 1e-05
NEG = -1e30
ROPE_BASE = 10000.0
LOG2E = 1.4426950408889634
SCALE = HEAD_DIM**-0.5
BLOCK = 256
F32 = jnp.float32
LOW = jnp.bfloat16
MESH = pl.DeviceIdType.MESH


def dot_nn(left, right):
    return lax.dot_general(left, right, (((1,), (0,)), ((), ())), preferred_element_type=F32)


def dot_nt(left, right):
    return lax.dot_general(left, right, (((1,), (1,)), ((), ())), preferred_element_type=F32)


def dot_tn(left, right):
    return lax.dot_general(left, right, (((0,), (0,)), ((), ())), preferred_element_type=F32)


def vmem(count):
    return [pl.BlockSpec(memory_space=pltpu.VMEM)] * count


def smem():
    return pl.BlockSpec(memory_space=pltpu.SMEM)


def params(mib):
    return pltpu.CompilerParams(vmem_limit_bytes=mib * 2**20)


def log2_of(number):
    return number.bit_length() - 1


def split_order(items, chunk, first):
    size = items * chunk
    row = lax.broadcasted_iota(jnp.int32, (size, size), 0)
    col = lax.broadcasted_iota(jnp.int32, (size, size), 1)
    item = (row >> log2_of(chunk)) + first
    item = jnp.where(item >= items, item - items, item)
    return jnp.where(col == (row & (chunk - 1)) * items + item, 1.0, 0.0).astype(LOW)


def merge_kernel(items, per, chunk, band_ref, *refs):
    ins, out = refs[:-1], refs[-1]
    size, bands = items * chunk, items // per
    row = lax.broadcasted_iota(jnp.int32, (size, size), 0)
    col = lax.broadcasted_iota(jnp.int32, (size, size), 1)
    number = col >> log2_of(chunk)
    source = band_ref[0] - (number >> log2_of(per))
    source = jnp.where(source < 0, source + bands, source)
    item = source * per + (number & (per - 1))
    order = jnp.where(row == (col & (chunk - 1)) * items + item, 1.0, 0.0).astype(LOW)
    for block in range(out.shape[0] // size):
        parts = jnp.concatenate([part[block * chunk : (block + 1) * chunk, :] for part in ins], 0)
        out[block * size : (block + 1) * size, :] = dot_nn(order, parts).astype(LOW)


def merge_items(parts, band, bands):
    items = len(parts)
    band_rows, width = parts[0].shape
    chunk = 32 if band_rows % 32 == 0 else 16
    return pl.pallas_call(
        functools.partial(merge_kernel, items, items // bands, chunk),
        name="merge_items",
        out_shape=jax.ShapeDtypeStruct((band_rows * items, width), LOW),
        in_specs=[smem()] + vmem(items),
        out_specs=vmem(1)[0],
        compiler_params=params(32),
    )(jnp.reshape(band, (1,)), *parts).reshape(band_rows, items, width)


def band_start(band, shift, bands, band_rows):
    return pl.multiple_of(lax.rem(band + shift + bands, bands) * band_rows, band_rows)


def exchange(parts, bands, per, item):
    kept = [parts[item]]
    for shift in range(1, bands):
        kept.append(
            lax.ppermute(
                parts[shift * per + item], "band", [(i, (i + shift) % bands) for i in range(bands)]
            )
        )
    return kept


def rope(vector, cos, sin):
    parts = []
    for at in range(0, vector.shape[0], HEAD_DIM):
        lower, upper = vector[at : at + HALF], vector[at + HALF : at + HEAD_DIM]
        parts += [lower * cos - upper * sin, lower * sin + upper * cos]
    return jnp.concatenate(parts, 0)


def query_blocks(seq):
    return [(start, min(start + BLOCK, seq)) for start in range(0, seq, BLOCK)]


def limits(start, stop, length):
    position = start + lax.broadcasted_iota(jnp.int32, (1, stop - start), 1)
    return jnp.minimum(position, length - 1)


def score_parts(keys, queries, start, stop, length):
    parts = []
    if start:
        parts.append((0, BLOCK, dot_tn(keys[:, :BLOCK], queries)))
    first = min(start, BLOCK)
    late = dot_tn(keys[:, first:stop], queries)
    position = first + lax.broadcasted_iota(jnp.int32, late.shape, 0)
    late = jnp.where(position <= limits(start, stop, length), late, NEG)
    parts.append((first, stop, late))
    return parts


def norm_rows(inputs):
    return lax.rsqrt(jnp.mean(inputs * inputs, -1, keepdims=True) + EPS)


def attend_item(length, x, weights, gain, cos, sin, query, key, value, attended_t, attended, log_total, normed, ready):
    seq, width = x.shape
    tile = 128
    for at in range(0, seq, tile):
        inputs = x[at : at + tile, :].astype(F32)
        normed[at : at + tile, :] = (inputs * norm_rows(inputs) * gain[...]).astype(LOW)

    project = 256

    def project_tile(at, _):
        rows = pl.ds(pl.multiple_of(at * project, project), project)
        for part, out, scaled in ((0, query, SCALE * LOG2E), (1, key, 1.0)):
            source = pl.ds(pl.multiple_of(part * width + at * project, project), project)
            out[rows, :] = (rope(dot_nt(weights[source, :], normed[...]), cos[...], sin[...]) * scaled).astype(LOW)
        source = pl.ds(pl.multiple_of(2 * width + at * project, project), project)
        value[rows, :] = dot_nt(weights[source, :], normed[...]).astype(LOW)
        return 0

    lax.fori_loop(0, width // project, project_tile, 0)
    ready()

    def head(at, _):
        for which in range(2):
            number = at * 2 + which
            rows = pl.ds(pl.multiple_of(number * HEAD_DIM, HEAD_DIM), HEAD_DIM)
            keys, values = key[rows, :], value[rows, :]
            for start, stop in query_blocks(seq):
                parts = score_parts(keys, query[rows, start:stop], start, stop, length)
                top = functools.reduce(jnp.maximum, [jnp.max(s, 0, keepdims=True) for _, _, s in parts])
                total = jnp.zeros_like(top)
                acc = jnp.zeros((HEAD_DIM, stop - start), F32)
                for first, last, scores in parts:
                    prob = jnp.exp2(scores - top)
                    total += jnp.sum(prob, 0, keepdims=True)
                    acc += dot_nn(values[:, first:last], prob.astype(LOW))
                attended_t[rows, start:stop] = (acc / total).astype(LOW)
                log_total[number, :, start:stop] = top + jnp.log2(total)
        return 0

    lax.fori_loop(0, width // HEAD_DIM // 2, head, 0)
    for at in range(0, width, project):
        attended[:, at : at + project] = attended_t[at : at + project, :].T


def feed_item(follows, x, attended, attended_t, cot, weights, gain, grads, g_norm, out, grad_attended_t, scratch):
    w_out, w_gate, w_up, w_down = weights
    g_out, g_gate, g_up, g_down = grads
    normed, normed_t, resid, out_acc, back_acc = scratch
    seq, width = x.shape
    tile, wide = 128, 512

    def put(ref, at, grad):
        if follows:
            grad += ref[at].astype(F32)
        ref[at] = grad.astype(LOW)

    for at in range(0, seq, tile):
        rows = slice(at, at + tile)
        total = x[rows, :].astype(F32) + dot_nn(attended[rows, :], w_out[...])
        resid[rows, :] = total
        out_acc[rows, :] = total
        low = (total * norm_rows(total) * gain[...]).astype(LOW)
        normed[rows, :] = low
        normed_t[:, rows] = low.T
    back_acc[...] = jnp.zeros_like(back_acc)

    def chunk(step, _):
        span = pl.ds(pl.multiple_of(step * wide, wide), wide)
        gate = dot_nn(normed[...], w_gate[:, span])
        upward = dot_nn(normed[...], w_up[:, span])
        grad_hidden = dot_nt(cot[...], w_down[span, :])
        sig = 0.5 * jnp.tanh(0.5 * gate) + 0.5
        silu = gate * sig
        hidden = (silu * upward).astype(LOW)
        grad_gate = (grad_hidden * upward * (sig + silu * (1.0 - sig))).astype(LOW)
        grad_upward = (grad_hidden * silu).astype(LOW)
        out_acc[...] += dot_nn(hidden, w_down[span, :])
        back_acc[...] += dot_nt(grad_gate, w_gate[:, span]) + dot_nt(grad_upward, w_up[:, span])
        put(g_down, (span, slice(None)), dot_nn(hidden.T, cot[...]))
        put(g_gate, (slice(None), span), dot_nn(normed_t[...], grad_gate))
        put(g_up, (slice(None), span), dot_nn(normed_t[...], grad_upward))
        return 0

    lax.fori_loop(0, w_gate.shape[1] // wide, chunk, 0)
    norm_sum = jnp.zeros((1, width), F32)
    for at in range(0, seq, tile):
        rows = slice(at, at + tile)
        out[rows, :] = out_acc[rows, :].astype(LOW)
        total, incoming = resid[rows, :], back_acc[rows, :]
        inv = norm_rows(total)
        scaled = total * inv
        norm_sum += jnp.sum(incoming * scaled, 0, keepdims=True)
        weighted = incoming * gain[...]
        grad = cot[rows, :].astype(F32) + inv * (weighted - scaled * jnp.mean(weighted * scaled, -1, keepdims=True))
        cot[rows, :] = grad.astype(LOW)
    g_norm[...] = g_norm[...] + norm_sum if follows else norm_sum
    grad_attended_t[...] = dot_nt(w_out[...], cot[...]).astype(LOW)
    put(g_out, (slice(None), slice(None)), dot_nn(attended_t[...], cot[...]))


class Copies:
    def __init__(self, local, send, receive, bands):
        self.local, self.send, self.receive = local, send, receive
        self.at, self.link, self.bands = 0, 0, bands
        self.band, self.items = lax.axis_index("band"), lax.axis_index("items")

    def start(self, source, target):
        copy = pltpu.make_async_copy(source, target, self.local.at[self.at])
        self.at += 1
        copy.start()
        return copy

    def other(self, shift):
        return lax.rem(self.band + shift + self.bands, self.bands)

    def greet(self):
        barrier = pltpu.get_barrier_semaphore()
        for shift in range(1, self.bands):
            pl.semaphore_signal(barrier, inc=1, device_id=(self.items, self.other(shift)), device_id_type=MESH)
        pl.semaphore_wait(barrier, self.bands - 1)

    def remote(self, source, target, arrival, device):
        ends = []
        for place in (target, arrival):
            ends.append(
                pltpu.make_async_remote_copy(
                    src_ref=source,
                    dst_ref=place,
                    send_sem=self.send.at[self.link],
                    recv_sem=self.receive.at[self.link],
                    device_id=device,
                    device_id_type=MESH,
                )
            )
        self.link += 1
        ends[0].start()
        return ends


def front_kernel(
    bands, per, lengths, tokens, cotangent, gain_attn, gain_ffn, cos, sin,
    w_query, w_key, w_value, w_out, w_gate, w_up, w_down,
    x_to, query_to, key_to, value_to, attended_t_to, log_total, grad_resid_to, grad_attended_t_to, out_to, home,
    g_gate_to, g_up_to, g_down_to, g_out_to, g_norm,
    weights_t, out_s, gate_s, up_s, down_s, g_gate, g_up, g_down, g_out,
    x, attended, attended_t, cot, query, key, value, grad_attended_t, normed, normed_t, resid, out_acc, back_acc,
    token_send, cot_send, local, send, receive,
):
    seq, width = x.shape[1:]
    band_rows, items = seq // bands, bands * per
    copies = Copies(local, send, receive, bands)
    band = copies.band
    loads = [copies.start(w_query, g_down.at[pl.ds(0, width)]), copies.start(w_key, g_down.at[pl.ds(width, width)])]
    loads.append(copies.start(w_value, g_out))
    late = [copies.start(a, b) for a, b in ((w_out, out_s), (w_gate, gate_s), (w_up, up_s), (w_down, down_s))]
    copies.greet()

    def own_rows(shift):
        return pl.ds(pl.multiple_of(copies.other(shift) * band_rows, band_rows), band_rows)

    chunk = 32 if band_rows % 32 == 0 else 16
    size = items * chunk
    order = split_order(items, chunk, band * per)

    def split(source, kept, sent):
        for block in range(band_rows // chunk):
            moved = dot_nn(order, source[block * size : (block + 1) * size, :]).astype(LOW)
            rows = pl.ds(pl.multiple_of(band * band_rows + block * chunk, 16), chunk)
            for at in range(items):
                part = moved[at * chunk : (at + 1) * chunk]
                if at < per:
                    kept[at, rows, :] = part
                else:
                    sent[at - per, block * chunk : (block + 1) * chunk, :] = part

    def scatter(sent, kept, item):
        return [
            copies.remote(
                sent.at[(shift - 1) * per + item],
                kept.at[item, own_rows(0)],
                kept.at[item, own_rows(-shift)],
                (copies.items, copies.other(shift)),
            )
            for shift in range(1, bands)
        ]

    split(tokens, x, token_send)
    token_links = [scatter(token_send, x, item) for item in range(per)]
    for part, source in enumerate((g_down.at[pl.ds(0, width)], g_down.at[pl.ds(width, width)], g_out)):
        loads[part].wait()
        for at in range(0, width, 256):
            weights_t[part * width + at : part * width + at + 256, :] = source[:, at : at + 256].T
    split(cotangent, cot, cot_send)
    cot_links, saves, home_links = [], [], []

    for item in range(per):
        for _, arrival in token_links[item]:
            arrival.wait_recv()
        cot_links.append(scatter(cot_send, cot, item))
        saved = [copies.start(x.at[item], x_to.at[item])]
        if item:
            for save in saves[-1][1:]:
                save.wait()

        def ready():
            for source, target in ((query, query_to), (key, key_to), (value, value_to)):
                saved.append(copies.start(source, target.at[item]))

        attend_item(
            lengths[band * per + item], x.at[item], weights_t, gain_attn, cos, sin, query, key, value,
            attended_t.at[item], attended.at[item], log_total.at[item], normed, ready,
        )
        saves.append(saved)
    waits = [save for save in saves[-1][1:]] + [saved[0] for saved in saves]
    for load in late:
        load.wait()
    grads = (g_out, g_gate, g_up, g_down)
    for item in range(per):
        for _, arrival in cot_links[item]:
            arrival.wait_recv()
        if item:
            dependent.wait()
        feed_item(
            item > 0, x.at[item], attended.at[item], attended_t.at[item], cot.at[item],
            (out_s, gate_s, up_s, down_s), gain_ffn, grads, g_norm, attended.at[item], grad_attended_t,
            (normed, normed_t, resid, out_acc, back_acc),
        )
        dependent = copies.start(grad_attended_t, grad_attended_t_to.at[item])
        waits.append(copies.start(attended_t.at[item], attended_t_to.at[item]))
        waits.append(copies.start(cot.at[item], grad_resid_to.at[item]))
        if item < per - 1:
            waits.append(copies.start(attended.at[item, own_rows(0)], home.at[item]))
            for shift in range(1, bands):
                slot = home.at[shift * (per - 1) + item]
                home_links.append(
                    copies.remote(attended.at[item, own_rows(shift)], slot, slot, (copies.items, copies.other(shift)))
                )
        else:
            waits.append(copies.start(attended.at[item], out_to))
    waits.append(dependent)
    waits += [copies.start(a, b) for a, b in ((g_gate, g_gate_to), (g_up, g_up_to), (g_down, g_down_to), (g_out, g_out_to))]
    for wait in waits:
        wait.wait()
    for links in token_links + cot_links + [home_links]:
        for started, _ in links:
            started.wait_send()
    for _, arrival in home_links:
        arrival.wait_recv()


def front(bands, lengths, tokens, cotangent, gains, tables, weights):
    band_rows, items, width = tokens.shape
    per, seq, ff = items // bands, bands * band_rows, weights[4].shape[1]
    rows, columns = (seq, width), (width, seq)
    many = lambda shape: jax.ShapeDtypeStruct((per,) + shape, LOW)
    low = lambda shape: jax.ShapeDtypeStruct(shape, LOW)
    scratch = lambda *shape: pltpu.VMEM(shape, LOW)
    full = lambda *shape: pltpu.VMEM(shape, F32)
    outside = pl.BlockSpec(memory_space=pl.ANY)
    inside = pl.BlockSpec(memory_space=pltpu.VMEM)
    home = max(bands * (per - 1), 1)
    local = 7 + per * 8 + bands + 8
    links = (bands - 1) * per * 3
    return pl.pallas_call(
        functools.partial(front_kernel, bands, per),
        name="front",
        out_shape=[many(rows)] + [many(columns)] * 4
        + [jax.ShapeDtypeStruct((per, width // HEAD_DIM, 1, seq), F32), many(rows), many(columns), low(rows)]
        + [low((home, band_rows, width)), low((width, ff)), low((width, ff)), low((ff, width)), low((width, width))]
        + [jax.ShapeDtypeStruct((1, width), F32)],
        in_specs=[smem()] + [inside] * 6 + [outside] * 7,
        out_specs=[outside] * 5 + [inside] + [outside] * 8 + [inside],
        scratch_shapes=[
            scratch(3 * width, width), scratch(width, width), scratch(width, ff), scratch(width, ff), scratch(ff, width),
            scratch(width, ff), scratch(width, ff), scratch(ff, width), scratch(width, width),
            scratch(per, seq, width), scratch(per, seq, width), scratch(per, width, seq), scratch(per, seq, width),
            scratch(width, seq), scratch(width, seq), scratch(width, seq), scratch(width, seq),
            scratch(seq, width), scratch(width, seq), full(seq, width), full(seq, width), full(seq, width),
            scratch(items - per, band_rows, width), scratch(items - per, band_rows, width),
            pltpu.SemaphoreType.DMA((local,)), pltpu.SemaphoreType.DMA((links,)), pltpu.SemaphoreType.DMA((links,)),
        ],
        compiler_params=pltpu.CompilerParams(
            vmem_limit_bytes=62 * 2**20, collective_id=0, has_side_effects=True
        ),
    )(
        lengths, tokens.reshape(band_rows * items, width), cotangent.reshape(band_rows * items, width),
        *gains, *tables, *weights,
    )


def back_kernel(bands, follows, scalars, *refs):
    x, grad_resid, grad_attended, attended, query, key, value, log_total, w_query, w_key, w_value = refs[:11]
    gain, cos, sin = refs[11:14]
    refs = refs[14:]
    prev = None
    if follows:
        prev, refs = refs[:2], refs[2:]
    outs, refs = refs[:bands], refs[bands:]
    g_weights, g_norm, grads, normed_t, back = refs
    seq, width = x.shape
    band_rows = seq // bands
    band, length = scalars[0], scalars[1]
    blocks = query_blocks(seq)

    def head(at, _):
        for which in range(2):
            number = at * 2 + which
            rows = pl.ds(pl.multiple_of(number * HEAD_DIM, HEAD_DIM), HEAD_DIM)
            keys, values = key[rows, :], value[rows, :]
            delta_all = jnp.sum(grad_attended[rows, :].astype(F32) * attended[rows, :].astype(F32), 0, keepdims=True)
            key_grads = [0.0] * len(blocks)
            value_grads = [0.0] * len(blocks)
            for start, stop in blocks:
                queries, incoming = query[rows, start:stop], grad_attended[rows, start:stop]
                total = log_total[number, :, start:stop]
                delta = delta_all[:, start:stop]
                query_grad = 0.0
                for first, last, scores in score_parts(keys, queries, start, stop, length):
                    prob = jnp.exp2(scores - total)
                    grad_prob = dot_tn(values[:, first:last], incoming)
                    grad_score = (prob * (grad_prob - delta)).astype(LOW)
                    query_grad += dot_nn(keys[:, first:last], grad_score)
                    key_grad = dot_nt(queries, grad_score)
                    value_grad = dot_nt(incoming, prob.astype(LOW))
                    for piece, (low, high) in enumerate(blocks):
                        if first <= low and high <= last:
                            key_grads[piece] += key_grad[:, low - first : high - first]
                            value_grads[piece] += value_grad[:, low - first : high - first]
                grads[rows, start:stop] = (
                    rope(query_grad, cos[:, start:stop], -sin[:, start:stop]) * SCALE
                ).astype(LOW)
            for (start, stop), key_grad, value_grad in zip(blocks, key_grads, value_grads):
                at_key = pl.ds(pl.multiple_of(width + number * HEAD_DIM, HEAD_DIM), HEAD_DIM)
                at_value = pl.ds(pl.multiple_of(2 * width + number * HEAD_DIM, HEAD_DIM), HEAD_DIM)
                grads[at_key, start:stop] = (
                    rope(key_grad, cos[:, start:stop], -sin[:, start:stop]) * (1.0 / LOG2E)
                ).astype(LOW)
                grads[at_value, start:stop] = value_grad.astype(LOW)
        return 0

    lax.fori_loop(0, width // HEAD_DIM // 2, head, 0)

    tile = 128
    for at in range(0, seq, tile):
        inputs = x[at : at + tile, :].astype(F32)
        normed_t[:, at : at + tile] = (inputs * norm_rows(inputs) * gain[...]).astype(LOW).T
    project = 256
    for at in range(0, width, project):
        rows = slice(at, at + project)
        total = dot_nn(w_query[rows, :], grads[:width, :])
        total += dot_nn(w_key[rows, :], grads[width : 2 * width, :])
        total += dot_nn(w_value[rows, :], grads[2 * width :, :])
        back[:, rows] = total.T
        for part in range(3):
            grad = dot_nt(normed_t[rows, :], grads[part * width : (part + 1) * width, :])
            columns = slice(part * width, (part + 1) * width)
            if follows:
                grad += prev[0][rows, columns].astype(F32)
            g_weights[rows, columns] = grad.astype(LOW)
    norm_sum = jnp.zeros((1, width), F32)
    for at in range(0, seq, tile):
        rows = slice(at, at + tile)
        inputs, incoming = x[rows, :].astype(F32), back[rows, :]
        inv = norm_rows(inputs)
        scaled = inputs * inv
        norm_sum += jnp.sum(incoming * scaled, 0, keepdims=True)
        weighted = incoming * gain[...]
        back[rows, :] = grad_resid[rows, :].astype(F32) + inv * (
            weighted - scaled * jnp.mean(weighted * scaled, -1, keepdims=True)
        )
    if follows:
        norm_sum += prev[1][...]
    g_norm[...] = norm_sum
    for shift, out in enumerate(outs):
        out[...] = back[pl.ds(band_start(band, shift, bands, band_rows), band_rows), :].astype(LOW)


def back_attend(bands, scalars, x, grad_resid, grad_attended_t, attended_t, query, key, value, log_total, weights, gain, cos, sin, prev):
    seq, width = x.shape
    band_rows = seq // bands
    pairs = seq * seq * width
    args = [x, grad_resid, grad_attended_t, attended_t, query, key, value, log_total, *weights, gain, cos, sin, *(prev or ())]
    return pl.pallas_call(
        functools.partial(back_kernel, bands, prev is not None),
        name="back_attend",
        out_shape=[jax.ShapeDtypeStruct((band_rows, width), LOW)] * bands
        + [jax.ShapeDtypeStruct((width, 3 * width), LOW), jax.ShapeDtypeStruct((1, width), F32)],
        in_specs=[smem()] + vmem(len(args)),
        out_specs=vmem(bands + 2),
        scratch_shapes=[
            pltpu.VMEM((3 * width, seq), LOW),
            pltpu.VMEM((width, seq), LOW),
            pltpu.VMEM((seq, width), F32),
        ],
        compiler_params=params(48),
        cost_estimate=pl.CostEstimate(
            flops=12 * seq * width * width + 30 * pairs, bytes_accessed=24 * seq * width, transcendentals=0
        ),
    )(scalars, *args)


def rope_tables(seq):
    frequency = np.exp(-np.log(ROPE_BASE) * (2.0 * np.arange(HALF) / HEAD_DIM))
    angles = frequency[:, None] * np.arange(seq)[None, :]
    return jnp.asarray(np.cos(angles), F32), jnp.asarray(np.sin(angles), F32)


def per_device(
    bands,
    tokens,
    lengths,
    norm_attn,
    w_query,
    w_key,
    w_value,
    w_out,
    norm_ffn,
    w_gate,
    w_up,
    w_down,
    cotangent,
):
    band_rows, items, width = tokens.shape
    per = items // bands
    seq = bands * band_rows
    band = lax.axis_index("band")
    cos, sin = rope_tables(seq)
    gain_attn, gain_ffn = norm_attn.reshape(1, width), norm_ffn.reshape(1, width)
    scalars = [
        jnp.stack([band, lax.dynamic_index_in_dim(lengths, band * per + item, keepdims=False)]).astype(jnp.int32)
        for item in range(per)
    ]
    (
        x, query, key, value, attended_t, log_total, grad_resid, grad_attended_t, out_last, home_early,
        g_gate, g_up, g_down, g_out, g_norm_ffn,
    ) = front(
        bands, lengths, tokens, cotangent, (gain_attn, gain_ffn), (cos, sin),
        (w_query, w_key, w_value, w_out, w_gate, w_up, w_down),
    )
    backs, prev = [], None
    for i in range(per):
        backs.append(
            back_attend(
                bands, scalars[i], x[i], grad_resid[i], grad_attended_t[i], attended_t[i], query[i], key[i], value[i], log_total[i],
                (w_query, w_key, w_value), gain_attn, cos, sin, prev,
            )
        )
        prev = backs[-1][bands:]
    g_weights, g_norm_attn = prev

    def home(parts):
        came = [exchange([parts[i][k] for k in range(bands)], bands, 1, 0) for i in range(per)]
        return merge_items([came[j][k] for k in range(bands) for j in range(per)], band, bands)

    def last_part(shift):
        return lax.dynamic_slice_in_dim(out_last, band_start(band, shift, bands, band_rows), band_rows, 0)

    came = exchange([last_part(k) for k in range(bands)], bands, 1, 0)
    early = [[home_early[k * (per - 1) + j] for j in range(per - 1)] for k in range(bands)]
    output = merge_items([part for k in range(bands) for part in early[k] + [came[k]]], band, bands)
    grad_tokens = home([b[:bands] for b in backs])
    axes = ("items", "band")
    gains = jnp.concatenate([g_norm_attn.T, g_norm_ffn.T], 1)
    feed_sum = lax.psum_scatter(jnp.concatenate([g_gate, g_up], 1), axes, scatter_dimension=0, tiled=True).astype(F32)
    down_sum = lax.psum_scatter(g_down, axes, scatter_dimension=0, tiled=True).astype(F32)
    rest = jnp.concatenate([g_weights, g_out, gains.astype(LOW)], 1)
    rest_sum = lax.psum_scatter(rest, axes, scatter_dimension=0, tiled=True).astype(F32)
    ff = w_gate.shape[1]
    return (
        output,
        grad_tokens,
        rest_sum[:, 4 * width],
        rest_sum[:, :width],
        rest_sum[:, width : 2 * width],
        rest_sum[:, 2 * width : 3 * width],
        rest_sum[:, 3 * width : 4 * width],
        rest_sum[:, 4 * width + 1],
        feed_sum[:, :ff],
        feed_sum[:, ff:],
        down_sum,
    )


def solution(mesh):
    split = P("band", "items", None)
    rows = P(("items", "band"), None)
    flat = P(("items", "band"))
    return jax.shard_map(
        functools.partial(per_device, mesh.shape["band"]),
        mesh=mesh,
        in_specs=(split, P("items")) + (P(),) * 9 + (split,),
        out_specs=(split, split, flat, rows, rows, rows, rows, flat, rows, rows, rows),
        check_vma=False,
    )
```

```python
import functools

import jax
import jax.numpy as jnp
import numpy as np
from jax import lax
from jax.experimental import pallas as pl
from jax.experimental.pallas import tpu as pltpu
from jax.sharding import PartitionSpec as P

HEAD_DIM = 64
HALF = HEAD_DIM // 2
EPS = 1e-05
NEG = -1e30
ROPE_BASE = 10000.0
LOG2E = 1.4426950408889634
SCALE = HEAD_DIM**-0.5
BLOCK = 256
F32 = jnp.float32
LOW = jnp.bfloat16
MESH = pl.DeviceIdType.MESH


def dot_nn(left, right):
    return lax.dot_general(left, right, (((1,), (0,)), ((), ())), preferred_element_type=F32)


def dot_nt(left, right):
    return lax.dot_general(left, right, (((1,), (1,)), ((), ())), preferred_element_type=F32)


def dot_tn(left, right):
    return lax.dot_general(left, right, (((0,), (0,)), ((), ())), preferred_element_type=F32)


def vmem(count):
    return [pl.BlockSpec(memory_space=pltpu.VMEM)] * count


def smem():
    return pl.BlockSpec(memory_space=pltpu.SMEM)


def params(mib):
    return pltpu.CompilerParams(vmem_limit_bytes=mib * 2**20)


def log2_of(number):
    return number.bit_length() - 1


def split_order(items, chunk, first):
    size = items * chunk
    row = lax.broadcasted_iota(jnp.int32, (size, size), 0)
    col = lax.broadcasted_iota(jnp.int32, (size, size), 1)
    item = (row >> log2_of(chunk)) + first
    item = jnp.where(item >= items, item - items, item)
    return jnp.where(col == (row & (chunk - 1)) * items + item, 1.0, 0.0).astype(LOW)


def merge_kernel(items, per, chunk, band_ref, *refs):
    ins, out = refs[:-1], refs[-1]
    size, bands = items * chunk, items // per
    row = lax.broadcasted_iota(jnp.int32, (size, size), 0)
    col = lax.broadcasted_iota(jnp.int32, (size, size), 1)
    number = col >> log2_of(chunk)
    source = band_ref[0] - (number >> log2_of(per))
    source = jnp.where(source < 0, source + bands, source)
    item = source * per + (number & (per - 1))
    order = jnp.where(row == (col & (chunk - 1)) * items + item, 1.0, 0.0).astype(LOW)
    for block in range(out.shape[0] // size):
        parts = jnp.concatenate([part[block * chunk : (block + 1) * chunk, :] for part in ins], 0)
        out[block * size : (block + 1) * size, :] = dot_nn(order, parts).astype(LOW)


def merge_items(parts, band, bands):
    items = len(parts)
    band_rows, width = parts[0].shape
    chunk = 32 if band_rows % 32 == 0 else 16
    return pl.pallas_call(
        functools.partial(merge_kernel, items, items // bands, chunk),
        name="merge_items",
        out_shape=jax.ShapeDtypeStruct((band_rows * items, width), LOW),
        in_specs=[smem()] + vmem(items),
        out_specs=vmem(1)[0],
        compiler_params=params(32),
    )(jnp.reshape(band, (1,)), *parts).reshape(band_rows, items, width)


def rope(vector, cos, sin):
    parts = []
    for at in range(0, vector.shape[0], HEAD_DIM):
        lower, upper = vector[at : at + HALF], vector[at + HALF : at + HEAD_DIM]
        parts += [lower * cos - upper * sin, lower * sin + upper * cos]
    return jnp.concatenate(parts, 0)


def query_blocks(seq):
    return [(start, min(start + BLOCK, seq)) for start in range(0, seq, BLOCK)]


def limits(start, stop, length):
    position = start + lax.broadcasted_iota(jnp.int32, (1, stop - start), 1)
    return jnp.minimum(position, length - 1)


def score_parts(keys, queries, start, stop, length):
    parts = []
    if start:
        parts.append((0, BLOCK, dot_tn(keys[:, :BLOCK], queries)))
    first = min(start, BLOCK)
    late = dot_tn(keys[:, first:stop], queries)
    position = first + lax.broadcasted_iota(jnp.int32, late.shape, 0)
    late = jnp.where(position <= limits(start, stop, length), late, NEG)
    parts.append((first, stop, late))
    return parts


def norm_rows(inputs):
    return lax.rsqrt(jnp.mean(inputs * inputs, -1, keepdims=True) + EPS)


def attend_item(length, x, weights, gain, cos, sin, query, key, value, attended_t, attended, log_total, normed, ready):
    seq, width = x.shape
    tile = 128
    for at in range(0, seq, tile):
        inputs = x[at : at + tile, :].astype(F32)
        normed[at : at + tile, :] = (inputs * norm_rows(inputs) * gain[...]).astype(LOW)

    project = 256

    def project_tile(at, _):
        rows = pl.ds(pl.multiple_of(at * project, project), project)
        for part, out, scaled in ((0, query, SCALE * LOG2E), (1, key, 1.0)):
            source = pl.ds(pl.multiple_of(part * width + at * project, project), project)
            out[rows, :] = (rope(dot_nt(weights[source, :], normed[...]), cos[...], sin[...]) * scaled).astype(LOW)
        source = pl.ds(pl.multiple_of(2 * width + at * project, project), project)
        value[rows, :] = dot_nt(weights[source, :], normed[...]).astype(LOW)
        return 0

    lax.fori_loop(0, width // project, project_tile, 0)
    ready()

    def head(at, _):
        for which in range(2):
            number = at * 2 + which
            rows = pl.ds(pl.multiple_of(number * HEAD_DIM, HEAD_DIM), HEAD_DIM)
            keys, values = key[rows, :], value[rows, :]
            for start, stop in query_blocks(seq):
                parts = score_parts(keys, query[rows, start:stop], start, stop, length)
                top = functools.reduce(jnp.maximum, [jnp.max(s, 0, keepdims=True) for _, _, s in parts])
                total = jnp.zeros_like(top)
                acc = jnp.zeros((HEAD_DIM, stop - start), F32)
                for first, last, scores in parts:
                    prob = jnp.exp2(scores - top)
                    total += jnp.sum(prob, 0, keepdims=True)
                    acc += dot_nn(values[:, first:last], prob.astype(LOW))
                attended_t[rows, start:stop] = (acc / total).astype(LOW)
                log_total[number, :, start:stop] = top + jnp.log2(total)
        return 0

    lax.fori_loop(0, width // HEAD_DIM // 2, head, 0)
    for at in range(0, width, project):
        attended[:, at : at + project] = attended_t[at : at + project, :].T


def feed_item(follows, x, attended, attended_t, cot, weights, gain, grads, g_norm, out, grad_attended_t, scratch):
    w_out, w_gate, w_up, w_down = weights
    g_out, g_gate, g_up, g_down = grads
    normed, normed_t, resid, out_acc, back_acc = scratch
    seq, width = x.shape
    tile, wide = 128, 512

    def put(ref, at, grad):
        if follows:
            grad += ref[at].astype(F32)
        ref[at] = grad.astype(LOW)

    for at in range(0, seq, tile):
        rows = slice(at, at + tile)
        total = x[rows, :].astype(F32) + dot_nn(attended[rows, :], w_out[...])
        resid[rows, :] = total
        out_acc[rows, :] = total
        low = (total * norm_rows(total) * gain[...]).astype(LOW)
        normed[rows, :] = low
        normed_t[:, rows] = low.T
    back_acc[...] = jnp.zeros_like(back_acc)

    def chunk(step, _):
        span = pl.ds(pl.multiple_of(step * wide, wide), wide)
        gate = dot_nn(normed[...], w_gate[:, span])
        upward = dot_nn(normed[...], w_up[:, span])
        grad_hidden = dot_nt(cot[...], w_down[span, :])
        sig = 0.5 * jnp.tanh(0.5 * gate) + 0.5
        silu = gate * sig
        hidden = (silu * upward).astype(LOW)
        grad_gate = (grad_hidden * upward * (sig + silu * (1.0 - sig))).astype(LOW)
        grad_upward = (grad_hidden * silu).astype(LOW)
        out_acc[...] += dot_nn(hidden, w_down[span, :])
        back_acc[...] += dot_nt(grad_gate, w_gate[:, span]) + dot_nt(grad_upward, w_up[:, span])
        put(g_down, (span, slice(None)), dot_nn(hidden.T, cot[...]))
        put(g_gate, (slice(None), span), dot_nn(normed_t[...], grad_gate))
        put(g_up, (slice(None), span), dot_nn(normed_t[...], grad_upward))
        return 0

    lax.fori_loop(0, w_gate.shape[1] // wide, chunk, 0)
    norm_sum = jnp.zeros((1, width), F32)
    for at in range(0, seq, tile):
        rows = slice(at, at + tile)
        out[rows, :] = out_acc[rows, :].astype(LOW)
        total, incoming = resid[rows, :], back_acc[rows, :]
        inv = norm_rows(total)
        scaled = total * inv
        norm_sum += jnp.sum(incoming * scaled, 0, keepdims=True)
        weighted = incoming * gain[...]
        grad = cot[rows, :].astype(F32) + inv * (weighted - scaled * jnp.mean(weighted * scaled, -1, keepdims=True))
        cot[rows, :] = grad.astype(LOW)
    g_norm[...] = g_norm[...] + norm_sum if follows else norm_sum
    grad_attended_t[...] = dot_nt(w_out[...], cot[...]).astype(LOW)
    put(g_out, (slice(None), slice(None)), dot_nn(attended_t[...], cot[...]))


class Copies:
    def __init__(self, local, send, receive, bands):
        self.local, self.send, self.receive = local, send, receive
        self.at, self.link, self.bands = 0, 0, bands
        self.band, self.items = lax.axis_index("band"), lax.axis_index("items")

    def start(self, source, target):
        copy = pltpu.make_async_copy(source, target, self.local.at[self.at])
        self.at += 1
        copy.start()
        return copy

    def other(self, shift):
        return lax.rem(self.band + shift + self.bands, self.bands)

    def greet(self, axis=0):
        barrier = pltpu.get_barrier_semaphore()
        others = [(self.items, self.other(shift)) for shift in range(1, self.bands)]
        if axis:
            others += [(flipped(self.items, at), self.band) for at in range(log2_of(axis))]
        for other in others:
            pl.semaphore_signal(barrier, inc=1, device_id=other, device_id_type=MESH)
        pl.semaphore_wait(barrier, len(others))

    def remote(self, source, target, arrival, device):
        ends = []
        for place in (target, arrival):
            ends.append(
                pltpu.make_async_remote_copy(
                    src_ref=source,
                    dst_ref=place,
                    send_sem=self.send.at[self.link],
                    recv_sem=self.receive.at[self.link],
                    device_id=device,
                    device_id_type=MESH,
                )
            )
        self.link += 1
        ends[0].start()
        return ends


def front_kernel(
    bands, per, lengths, tokens, cotangent, gain_attn, gain_ffn, cos, sin,
    w_query, w_key, w_value, w_out, w_gate, w_up, w_down,
    x_to, query_to, key_to, value_to, attended_t_to, log_total, grad_resid_to, grad_attended_t_to, out_to, home,
    g_gate_to, g_up_to, g_down_to, g_out_to, g_norm,
    weights_t, out_s, gate_s, up_s, down_s, g_gate, g_up, g_down, g_out,
    x, attended, attended_t, cot, query, key, value, grad_attended_t, normed, normed_t, resid, out_acc, back_acc,
    token_send, cot_send, local, send, receive,
):
    seq, width = x.shape[1:]
    band_rows, items = seq // bands, bands * per
    copies = Copies(local, send, receive, bands)
    band = copies.band
    loads = [copies.start(w_query, g_down.at[pl.ds(0, width)]), copies.start(w_key, g_down.at[pl.ds(width, width)])]
    loads.append(copies.start(w_value, g_out))
    late = [copies.start(a, b) for a, b in ((w_out, out_s), (w_gate, gate_s), (w_up, up_s), (w_down, down_s))]
    copies.greet()

    def own_rows(shift):
        return pl.ds(pl.multiple_of(copies.other(shift) * band_rows, band_rows), band_rows)

    chunk = 32 if band_rows % 32 == 0 else 16
    size = items * chunk
    order = split_order(items, chunk, band * per)

    def split(source, kept, sent):
        for block in range(band_rows // chunk):
            moved = dot_nn(order, source[block * size : (block + 1) * size, :]).astype(LOW)
            rows = pl.ds(pl.multiple_of(band * band_rows + block * chunk, 16), chunk)
            for at in range(items):
                part = moved[at * chunk : (at + 1) * chunk]
                if at < per:
                    kept[at, rows, :] = part
                else:
                    sent[at - per, block * chunk : (block + 1) * chunk, :] = part

    def scatter(sent, kept, item):
        return [
            copies.remote(
                sent.at[(shift - 1) * per + item],
                kept.at[item, own_rows(0)],
                kept.at[item, own_rows(-shift)],
                (copies.items, copies.other(shift)),
            )
            for shift in range(1, bands)
        ]

    split(tokens, x, token_send)
    token_links = [scatter(token_send, x, item) for item in range(per)]
    for part, source in enumerate((g_down.at[pl.ds(0, width)], g_down.at[pl.ds(width, width)], g_out)):
        loads[part].wait()
        for at in range(0, width, 256):
            weights_t[part * width + at : part * width + at + 256, :] = source[:, at : at + 256].T
    split(cotangent, cot, cot_send)
    cot_links, saves, home_links = [], [], []

    for item in range(per):
        for _, arrival in token_links[item]:
            arrival.wait_recv()
        cot_links.append(scatter(cot_send, cot, item))
        saved = [copies.start(x.at[item], x_to.at[item])]
        if item:
            for save in saves[-1][1:]:
                save.wait()

        def ready():
            for source, target in ((query, query_to), (key, key_to), (value, value_to)):
                saved.append(copies.start(source, target.at[item]))

        attend_item(
            lengths[band * per + item], x.at[item], weights_t, gain_attn, cos, sin, query, key, value,
            attended_t.at[item], attended.at[item], log_total.at[item], normed, ready,
        )
        saves.append(saved)
    waits = [save for save in saves[-1][1:]] + [saved[0] for saved in saves]
    for load in late:
        load.wait()
    grads = (g_out, g_gate, g_up, g_down)
    for item in range(per):
        for _, arrival in cot_links[item]:
            arrival.wait_recv()
        if item:
            dependent.wait()
        feed_item(
            item > 0, x.at[item], attended.at[item], attended_t.at[item], cot.at[item],
            (out_s, gate_s, up_s, down_s), gain_ffn, grads, g_norm, attended.at[item], grad_attended_t,
            (normed, normed_t, resid, out_acc, back_acc),
        )
        dependent = copies.start(grad_attended_t, grad_attended_t_to.at[item])
        waits.append(copies.start(attended_t.at[item], attended_t_to.at[item]))
        waits.append(copies.start(cot.at[item], grad_resid_to.at[item]))
        if item < per - 1:
            waits.append(copies.start(attended.at[item, own_rows(0)], home.at[item]))
            for shift in range(1, bands):
                slot = home.at[shift * (per - 1) + item]
                home_links.append(
                    copies.remote(attended.at[item, own_rows(shift)], slot, slot, (copies.items, copies.other(shift)))
                )
        else:
            waits.append(copies.start(attended.at[item], out_to))
    waits.append(dependent)
    waits += [copies.start(a, b) for a, b in ((g_gate, g_gate_to), (g_up, g_up_to), (g_down, g_down_to), (g_out, g_out_to))]
    for wait in waits:
        wait.wait()
    for links in token_links + cot_links + [home_links]:
        for started, _ in links:
            started.wait_send()
    for _, arrival in home_links:
        arrival.wait_recv()


def front(bands, lengths, tokens, cotangent, gains, tables, weights):
    band_rows, items, width = tokens.shape
    per, seq, ff = items // bands, bands * band_rows, weights[4].shape[1]
    rows, columns = (seq, width), (width, seq)
    many = lambda shape: jax.ShapeDtypeStruct((per,) + shape, LOW)
    low = lambda shape: jax.ShapeDtypeStruct(shape, LOW)
    scratch = lambda *shape: pltpu.VMEM(shape, LOW)
    full = lambda *shape: pltpu.VMEM(shape, F32)
    outside = pl.BlockSpec(memory_space=pl.ANY)
    inside = pl.BlockSpec(memory_space=pltpu.VMEM)
    home = max(bands * (per - 1), 1)
    local = 7 + per * 8 + bands + 8
    links = (bands - 1) * per * 3
    return pl.pallas_call(
        functools.partial(front_kernel, bands, per),
        name="front",
        out_shape=[many(rows)] + [many(columns)] * 4
        + [jax.ShapeDtypeStruct((per, width // HEAD_DIM, 1, seq), F32), many(rows), many(columns), low(rows)]
        + [low((home, band_rows, width)), low((width, ff)), low((width, ff)), low((ff, width)), low((width, width))]
        + [jax.ShapeDtypeStruct((1, width), F32)],
        in_specs=[smem()] + [inside] * 6 + [outside] * 7,
        out_specs=[outside] * 5 + [inside] + [outside] * 8 + [inside],
        scratch_shapes=[
            scratch(3 * width, width), scratch(width, width), scratch(width, ff), scratch(width, ff), scratch(ff, width),
            scratch(width, ff), scratch(width, ff), scratch(ff, width), scratch(width, width),
            scratch(per, seq, width), scratch(per, seq, width), scratch(per, width, seq), scratch(per, seq, width),
            scratch(width, seq), scratch(width, seq), scratch(width, seq), scratch(width, seq),
            scratch(seq, width), scratch(width, seq), full(seq, width), full(seq, width), full(seq, width),
            scratch(items - per, band_rows, width), scratch(items - per, band_rows, width),
            pltpu.SemaphoreType.DMA((local,)), pltpu.SemaphoreType.DMA((links,)), pltpu.SemaphoreType.DMA((links,)),
        ],
        compiler_params=pltpu.CompilerParams(
            vmem_limit_bytes=62 * 2**20, collective_id=0, has_side_effects=True
        ),
    )(
        lengths, tokens.reshape(band_rows * items, width), cotangent.reshape(band_rows * items, width),
        *gains, *tables, *weights,
    )


def back_item(
    follows, length, x, grad_resid, grad_attended, attended, query, key, value, log_total, weights, gain, cos, sin,
    g_weights, g_norm, grads, normed_t, back, tick,
):
    w_query, w_key, w_value = weights
    seq, width = x.shape
    blocks = query_blocks(seq)

    def head(at, _):
        tick(at)
        for which in range(2):
            number = at * 2 + which
            rows = pl.ds(pl.multiple_of(number * HEAD_DIM, HEAD_DIM), HEAD_DIM)
            keys, values = key[rows, :], value[rows, :]
            delta_all = jnp.sum(grad_attended[rows, :].astype(F32) * attended[rows, :].astype(F32), 0, keepdims=True)
            key_grads = [0.0] * len(blocks)
            value_grads = [0.0] * len(blocks)
            for start, stop in blocks:
                queries, incoming = query[rows, start:stop], grad_attended[rows, start:stop]
                total = log_total[number, :, start:stop]
                delta = delta_all[:, start:stop]
                query_grad = 0.0
                for first, last, scores in score_parts(keys, queries, start, stop, length):
                    prob = jnp.exp2(scores - total)
                    grad_prob = dot_tn(values[:, first:last], incoming)
                    grad_score = (prob * (grad_prob - delta)).astype(LOW)
                    query_grad += dot_nn(keys[:, first:last], grad_score)
                    key_grad = dot_nt(queries, grad_score)
                    value_grad = dot_nt(incoming, prob.astype(LOW))
                    for piece, (low, high) in enumerate(blocks):
                        if first <= low and high <= last:
                            key_grads[piece] += key_grad[:, low - first : high - first]
                            value_grads[piece] += value_grad[:, low - first : high - first]
                grads[rows, start:stop] = (
                    rope(query_grad, cos[:, start:stop], -sin[:, start:stop]) * SCALE
                ).astype(LOW)
            for (start, stop), key_grad, value_grad in zip(blocks, key_grads, value_grads):
                at_key = pl.ds(pl.multiple_of(width + number * HEAD_DIM, HEAD_DIM), HEAD_DIM)
                at_value = pl.ds(pl.multiple_of(2 * width + number * HEAD_DIM, HEAD_DIM), HEAD_DIM)
                grads[at_key, start:stop] = (
                    rope(key_grad, cos[:, start:stop], -sin[:, start:stop]) * (1.0 / LOG2E)
                ).astype(LOW)
                grads[at_value, start:stop] = value_grad.astype(LOW)
        return 0

    lax.fori_loop(0, width // HEAD_DIM // 2, head, 0)

    tile = 128
    for at in range(0, seq, tile):
        inputs = x[at : at + tile, :].astype(F32)
        normed_t[:, at : at + tile] = (inputs * norm_rows(inputs) * gain[...]).astype(LOW).T
    project = 256
    for at in range(0, width, project):
        rows = slice(at, at + project)
        total = dot_nn(w_query[rows, :], grads[:width, :])
        total += dot_nn(w_key[rows, :], grads[width : 2 * width, :])
        total += dot_nn(w_value[rows, :], grads[2 * width :, :])
        back[:, rows] = total.T
        for part in range(3):
            grad = dot_nt(normed_t[rows, :], grads[part * width : (part + 1) * width, :])
            columns = slice(part * width, (part + 1) * width)
            if follows:
                grad += g_weights[rows, columns].astype(F32)
            g_weights[rows, columns] = grad.astype(LOW)
    norm_sum = jnp.zeros((1, width), F32)
    for at in range(0, seq, tile):
        rows = slice(at, at + tile)
        inputs, incoming = x[rows, :].astype(F32), back[rows, :]
        inv = norm_rows(inputs)
        scaled = inputs * inv
        norm_sum += jnp.sum(incoming * scaled, 0, keepdims=True)
        weighted = incoming * gain[...]
        grad = grad_resid[rows, :].astype(F32) + inv * (
            weighted - scaled * jnp.mean(weighted * scaled, -1, keepdims=True)
        )
        grad_resid[rows, :] = grad.astype(LOW)
    g_norm[...] = g_norm[...] + norm_sum if follows else norm_sum


def bit(number, at):
    return lax.rem(lax.div(number, 2**at), 2)


def flipped(number, at):
    return number + (1 - 2 * bit(number, at)) * 2**at


def replaced(number, bits, choice):
    for order, at in enumerate(bits):
        number = number + ((choice >> order & 1) - bit(number, at)) * 2**at
    return number


def sum_orders(axis):
    later = list(range(1, log2_of(axis)))
    return [0] + later, [0] + later[::-1]


def sum_lanes(axis, stage, columns):
    left, right = sum_orders(axis)
    half = columns // 2
    if stage == 0:
        return [(left[0], left[1:], 0, columns)]
    return [(left[stage], left[stage + 1 :], 0, half), (right[stage], right[stage + 1 :], half, half)]


def band_shape(axis, bands, shape):
    rows = shape[0] // axis // bands
    return (rows, shape[1]) if rows % 16 == 0 else (2 * rows, shape[1] // 2)


def sum_scratch(axis, bands, shape):
    low = lambda *dims: pltpu.VMEM(dims, LOW)
    out = []
    for stage in range(log2_of(axis)):
        for _, bits, _, columns in sum_lanes(axis, stage, shape[1]):
            out.append(low(2 ** len(bits), shape[0] // axis, columns))
    part = band_shape(axis, bands, shape)
    out.append(low(bands, *part))
    for stage in range(log2_of(bands)):
        out.append(low(bands >> stage + 1, *part))
    return out


def sum_links(axis, bands):
    return axis // 2 + 2 * (axis // 2 - 1) + bands - 1


class Summing:
    def __init__(self, copies, axis, arrays, scratch, outs):
        self.copies, self.axis, self.arrays, self.outs = copies, axis, arrays, outs
        self.count = log2_of(axis)
        self.stages = self.count + log2_of(copies.bands)
        each = len(scratch) // len(arrays)
        self.scratch = [list(scratch[at * each : (at + 1) * each]) for at in range(len(arrays))]
        self.flights = {}
        self.sent = []

    def buffers(self, at, stage):
        taken = self.scratch[at]
        if stage < self.count:
            first = 0 if stage == 0 else 2 * stage - 1
            return taken[first : first + (1 if stage == 0 else 2)]
        return taken[2 * self.count + stage - self.count : 2 * self.count + stage - self.count + 1]

    def piece(self, array, number, first, columns):
        rows = array.shape[0] // self.axis
        return array.at[pl.ds(pl.multiple_of(number * rows, rows), rows), pl.ds(first, columns)]

    def begin(self, stage):
        me, band = self.copies.items, self.copies.band
        flights = []
        for at, array in enumerate(self.arrays):
            if stage < self.count:
                lanes = sum_lanes(self.axis, stage, array.shape[1])
                for (axis_bit, bits, first, columns), came in zip(lanes, self.buffers(at, stage)):
                    other = flipped(me, axis_bit)
                    for choice in range(2 ** len(bits)):
                        sent = self.piece(array, replaced(other, bits, choice), first, columns)
                        kept = self.piece(array, replaced(me, bits, choice), first, columns)
                        links = self.copies.remote(sent, came.at[choice], came.at[choice], (other, band))
                        flights.append((links, kept, came.at[choice]))
            else:
                band_bit = stage - self.count
                bits = list(range(band_bit + 1, log2_of(self.copies.bands)))
                parts, came = self.scratch[at][2 * self.count - 1], self.buffers(at, stage)[0]
                other = flipped(band, band_bit)
                for choice in range(2 ** len(bits)):
                    sent, kept = parts.at[replaced(other, bits, choice)], parts.at[replaced(band, bits, choice)]
                    links = self.copies.remote(sent, came.at[choice], came.at[choice], (me, other))
                    flights.append((links, kept, came.at[choice]))
        self.flights[stage] = flights
        self.sent += [links[0] for links, _, _ in flights]

    def end(self, stage):
        for links, _, _ in self.flights[stage]:
            links[1].wait_recv()
        last = stage == self.stages - 1
        for at, (_, kept, came) in enumerate(self.flights[stage]):
            if last:
                total = kept[...].astype(F32) + came[...].astype(F32)
                out = self.outs[at]
                rows, half = out.shape[0], total.shape[1]
                if total.shape[0] == rows:
                    out[...] = total
                else:
                    out[:, :half] = total[:rows]
                    out[:, half:] = total[rows:]
                continue
            tile = 16

            def add(step, _, kept=kept, came=came):
                rows = pl.ds(pl.multiple_of(step * tile, tile), tile)
                kept[rows, :] = (kept[rows, :].astype(F32) + came[rows, :].astype(F32)).astype(LOW)
                return 0

            lax.fori_loop(0, kept.shape[0] // tile, add, 0)
        if stage == self.count - 1:
            self.stack()

    def stack(self):
        bands = self.copies.bands
        for at, array in enumerate(self.arrays):
            parts = self.scratch[at][2 * self.count - 1]
            whole = self.piece(array, self.copies.items, 0, array.shape[1])
            rows = whole.shape[0] // bands
            if parts.shape[1] == rows:
                for number in range(bands):
                    parts[number] = whole[number * rows : (number + 1) * rows, :]
                continue
            half = array.shape[1] // 2
            left, right = whole[:, :half].astype(F32), whole[:, half:].astype(F32)
            for number in range(bands):
                span = slice(number * rows, (number + 1) * rows)
                parts[number] = jnp.concatenate([left[span], right[span]], 0).astype(LOW)

    def close(self):
        for link in self.sent:
            link.wait_send()


def rear_kernel(
    bands, per, axis, lengths, gain, cos, sin, log_total, g_norm_ffn, *refs
):
    fused = axis > 0
    x_from, query_from, key_from, value_from, attended_t_from, grad_resid_from, grad_attended_t_from = refs[:7]
    out_last, w_query_from, w_key_from, w_value_from, *g_feed_from = refs[7:15]
    refs = refs[15:]
    home_last, home_grad, *outs = refs[: 2 + (6 if fused else 2)]
    refs = refs[2 + (6 if fused else 2) :]
    x, query, key, value, attended_t, grad_resid, grad_attended_t, w_query, w_key, w_value = refs[:10]
    g_weights, grads, normed_t, back, g_norm, local, send, receive = refs[10:18]
    refs = refs[18:]
    seq, width = x.shape[1:]
    band_rows, items = seq // bands, bands * per
    copies = Copies(local, send, receive, bands)
    band = copies.band
    loads = []
    for item in range(per):
        loads.append(
            [
                copies.start(source.at[item], target.at[item])
                for source, target in (
                    (query_from, query), (key_from, key), (value_from, value), (attended_t_from, attended_t),
                    (grad_attended_t_from, grad_attended_t), (x_from, x), (grad_resid_from, grad_resid),
                )
            ]
        )
        if item == 0:
            loads[0] += [
                copies.start(w_query_from, w_query), copies.start(w_key_from, w_key), copies.start(w_value_from, w_value)
            ]
            if fused:
                g_feed = refs[:4]
                feed_loads = [copies.start(a, b) for a, b in zip(g_feed_from, g_feed)]
    copies.greet(axis)
    if fused:
        each = len(sum_scratch(axis, bands, (axis * bands * 16, 256)))
        feed_sum = Summing(copies, axis, g_feed, refs[4 : 4 + 4 * each], outs[:4])
        rest_sum = Summing(copies, axis, [g_weights], refs[4 + 4 * each :], outs[4:5])

    def own_rows(shift):
        return pl.ds(pl.multiple_of(copies.other(shift) * band_rows, band_rows), band_rows)

    def go_home(source, home, slots, item):
        kept = copies.start(source.at[own_rows(0)], home.at[item])
        links = []
        for shift in range(1, bands):
            slot = home.at[shift * slots + item]
            links.append(
                copies.remote(source.at[own_rows(shift)], slot, slot, (copies.items, copies.other(shift)))
            )
        return kept, links

    flights = [go_home(out_last, home_last, 1, 0)]
    if fused:
        for load in feed_loads:
            load.wait()
        feed_sum.begin(0)
    for item in range(per):
        for load in loads[item]:
            load.wait()

        def tick(at, item=item):
            if not fused:
                return
            for place, action in progress.get(item, {}).items():
                pl.when(at == place)(action)

        progress = {}
        back_item(
            item > 0, lengths[band * per + item], x.at[item], grad_resid.at[item], grad_attended_t.at[item],
            attended_t.at[item], query.at[item], key.at[item], value.at[item], log_total.at[item],
            (w_query, w_key, w_value), gain, cos, sin, g_weights, g_norm, grads, normed_t, back, tick,
        )
        flights.append(go_home(grad_resid.at[item], home_grad, per, item))
        if fused and item < per - 1:
            feed_sum.end(item)
            feed_sum.begin(item + 1)
    if fused:
        lanes = 128
        pad = jnp.zeros((lanes - 1, width), F32)
        for at, sums in enumerate((g_norm, g_norm_ffn)):
            spread = jnp.concatenate([sums[...], pad], 0).T
            g_weights[:, 3 * width + at * lanes : 3 * width + (at + 1) * lanes] = spread.astype(LOW)
        rest_sum.begin(0)
        begun = per - 1
        for stage in range(rest_sum.stages):
            if begun < feed_sum.stages:
                feed_sum.end(begun)
                begun += 1
                if begun < feed_sum.stages:
                    feed_sum.begin(begun)
            rest_sum.end(stage)
            if stage + 1 < rest_sum.stages:
                rest_sum.begin(stage + 1)
        while begun < feed_sum.stages:
            feed_sum.end(begun)
            begun += 1
            if begun < feed_sum.stages:
                feed_sum.begin(begun)
        feed_sum.close()
        rest_sum.close()
    else:
        outs[0][...] = g_weights[...]
        outs[1][...] = g_norm[...]
    for kept, links in flights:
        kept.wait()
        for started, arrival in links:
            started.wait_send()
            arrival.wait_recv()


def rear(bands, axis, lengths, gain, tables, kept, out_last, weights, g_feed, g_norm_ffn):
    x, query, key, value, attended_t, log_total, grad_resid, grad_attended_t = kept
    per, seq, width = x.shape
    band_rows, items = seq // bands, bands * per
    fused = axis > 0
    low = lambda *shape: jax.ShapeDtypeStruct(shape, LOW)
    scratch = lambda *shape: pltpu.VMEM(shape, LOW)
    outside = pl.BlockSpec(memory_space=pl.ANY)
    inside = pl.BlockSpec(memory_space=pltpu.VMEM)
    rest = (width, 3 * width + 256) if fused else (width, 3 * width)
    out_shape = [low(bands, band_rows, width), low(items, band_rows, width)]
    sums = []
    links = 3 * (bands - 1) * (per + 1)
    if fused:
        shapes = [g.shape for g in g_feed] + [rest]
        out_shape += [jax.ShapeDtypeStruct((s[0] // axis // bands, s[1]), F32) for s in shapes]
        out_shape += [jax.ShapeDtypeStruct((1, width), F32)]
        sums = [scratch(*s) for s in shapes[:-1]]
        for shape in shapes:
            sums += sum_scratch(axis, bands, shape)
        links += len(shapes) * sum_links(axis, bands)
    else:
        out_shape += [low(*rest), jax.ShapeDtypeStruct((1, width), F32)]
    local = 8 * per + 3 + 4 + per + 1
    return pl.pallas_call(
        functools.partial(rear_kernel, bands, per, axis),
        name="rear",
        out_shape=out_shape,
        in_specs=[smem()] + [inside] * 5 + [outside] * 15,
        out_specs=[outside] * 2 + [inside] * (len(out_shape) - 2),
        scratch_shapes=[
            scratch(per, seq, width), scratch(per, width, seq), scratch(per, width, seq), scratch(per, width, seq),
            scratch(per, width, seq), scratch(per, seq, width), scratch(per, width, seq),
            scratch(width, width), scratch(width, width), scratch(width, width),
            scratch(*rest), scratch(3 * width, seq), scratch(width, seq), pltpu.VMEM((seq, width), F32),
            pltpu.VMEM((1, width), F32),
            pltpu.SemaphoreType.DMA((local,)), pltpu.SemaphoreType.DMA((links,)), pltpu.SemaphoreType.DMA((links,)),
        ]
        + sums,
        compiler_params=pltpu.CompilerParams(vmem_limit_bytes=62 * 2**20, collective_id=1, has_side_effects=True),
    )(
        lengths, gain, *tables, log_total, g_norm_ffn, x, query, key, value, attended_t, grad_resid, grad_attended_t,
        out_last, *weights, *g_feed,
    )


def rope_tables(seq):
    frequency = np.exp(-np.log(ROPE_BASE) * (2.0 * np.arange(HALF) / HEAD_DIM))
    angles = frequency[:, None] * np.arange(seq)[None, :]
    return jnp.asarray(np.cos(angles), F32), jnp.asarray(np.sin(angles), F32)


def per_device(
    bands,
    axis,
    tokens,
    lengths,
    norm_attn,
    w_query,
    w_key,
    w_value,
    w_out,
    norm_ffn,
    w_gate,
    w_up,
    w_down,
    cotangent,
):
    band_rows, items, width = tokens.shape
    per = items // bands
    seq = bands * band_rows
    band = lax.axis_index("band")
    cos, sin = rope_tables(seq)
    gain_attn, gain_ffn = norm_attn.reshape(1, width), norm_ffn.reshape(1, width)
    (
        x, query, key, value, attended_t, log_total, grad_resid, grad_attended_t, out_last, home_early,
        g_gate, g_up, g_down, g_out, g_norm_ffn,
    ) = front(
        bands, lengths, tokens, cotangent, (gain_attn, gain_ffn), (cos, sin),
        (w_query, w_key, w_value, w_out, w_gate, w_up, w_down),
    )
    fused = axis if width // axis % 16 == 0 and w_gate.shape[1] // axis % 16 == 0 else 0
    home_last, home_grad, *sums = rear(
        bands, fused, lengths, gain_attn, (cos, sin),
        (x, query, key, value, attended_t, log_total, grad_resid, grad_attended_t),
        out_last, (w_query, w_key, w_value), (g_gate, g_up, g_down, g_out), g_norm_ffn,
    )
    ahead = per - 1
    output = [home_early[k * ahead + j] if j < ahead else home_last[k] for k in range(bands) for j in range(per)]
    output = merge_items(output, band, bands)
    grad_tokens = merge_items([home_grad[at] for at in range(items)], band, bands)
    if fused:
        g_gate, g_up, g_down, g_out, rest = sums[:5]
        g_norm_attn, g_norm_ffn = rest[:, 3 * width], rest[:, 3 * width + 128]
        g_weights = rest[:, : 3 * width]
    else:
        axes = ("items", "band")
        total = lambda a: lax.psum_scatter(a, axes, scatter_dimension=0, tiled=True).astype(F32)
        norms = total(jnp.concatenate([sums[1].T, g_norm_ffn.T], 1))
        g_norm_attn, g_norm_ffn = norms[:, 0], norms[:, 1]
        g_gate, g_up, g_down, g_out, g_weights = (total(a) for a in (g_gate, g_up, g_down, g_out, sums[0]))
    return (
        output,
        grad_tokens,
        g_norm_attn,
        g_weights[:, :width],
        g_weights[:, width : 2 * width],
        g_weights[:, 2 * width : 3 * width],
        g_out,
        g_norm_ffn,
        g_gate,
        g_up,
        g_down,
    )


def solution(mesh):
    split = P("band", "items", None)
    rows = P(("items", "band"), None)
    flat = P(("items", "band"))
    return jax.shard_map(
        functools.partial(per_device, mesh.shape["band"], mesh.shape["items"]),
        mesh=mesh,
        in_specs=(split, P("items")) + (P(),) * 9 + (split,),
        out_specs=(split, split, flat, rows, rows, rows, rows, flat, rows, rows, rows),
        check_vma=False,
    )
```

```python
import functools

import jax
import jax.numpy as jnp
import numpy as np
from jax import lax
from jax.experimental import pallas as pl
from jax.experimental.pallas import tpu as pltpu
from jax.sharding import PartitionSpec as P

HEAD_DIM = 64
HALF = HEAD_DIM // 2
EPS = 1e-05
NEG = -1e30
ROPE_BASE = 10000.0
LOG2E = 1.4426950408889634
SCALE = HEAD_DIM**-0.5
BLOCK = 256
F32 = jnp.float32
LOW = jnp.bfloat16
MESH = pl.DeviceIdType.MESH


def dot_nn(left, right):
    return lax.dot_general(left, right, (((1,), (0,)), ((), ())), preferred_element_type=F32)


def dot_nt(left, right):
    return lax.dot_general(left, right, (((1,), (1,)), ((), ())), preferred_element_type=F32)


def dot_tn(left, right):
    return lax.dot_general(left, right, (((0,), (0,)), ((), ())), preferred_element_type=F32)


def vmem(count):
    return [pl.BlockSpec(memory_space=pltpu.VMEM)] * count


def smem():
    return pl.BlockSpec(memory_space=pltpu.SMEM)


def params(mib):
    return pltpu.CompilerParams(vmem_limit_bytes=mib * 2**20)


def log2_of(number):
    return number.bit_length() - 1


def split_order(items, chunk, first):
    size = items * chunk
    row = lax.broadcasted_iota(jnp.int32, (size, size), 0)
    col = lax.broadcasted_iota(jnp.int32, (size, size), 1)
    item = (row >> log2_of(chunk)) + first
    item = jnp.where(item >= items, item - items, item)
    return jnp.where(col == (row & (chunk - 1)) * items + item, 1.0, 0.0).astype(LOW)


def merge_kernel(items, per, chunk, band_ref, *refs):
    ins, out = refs[:-1], refs[-1]
    size, bands = items * chunk, items // per
    row = lax.broadcasted_iota(jnp.int32, (size, size), 0)
    col = lax.broadcasted_iota(jnp.int32, (size, size), 1)
    number = col >> log2_of(chunk)
    source = band_ref[0] - (number >> log2_of(per))
    source = jnp.where(source < 0, source + bands, source)
    item = source * per + (number & (per - 1))
    order = jnp.where(row == (col & (chunk - 1)) * items + item, 1.0, 0.0).astype(LOW)
    for block in range(out.shape[0] // size):
        parts = jnp.concatenate([part[block * chunk : (block + 1) * chunk, :] for part in ins], 0)
        out[block * size : (block + 1) * size, :] = dot_nn(order, parts).astype(LOW)


def merge_items(parts, band, bands):
    items = len(parts)
    band_rows, width = parts[0].shape
    chunk = 32 if band_rows % 32 == 0 else 16
    return pl.pallas_call(
        functools.partial(merge_kernel, items, items // bands, chunk),
        name="merge_items",
        out_shape=jax.ShapeDtypeStruct((band_rows * items, width), LOW),
        in_specs=[smem()] + vmem(items),
        out_specs=vmem(1)[0],
        compiler_params=params(32),
    )(jnp.reshape(band, (1,)), *parts).reshape(band_rows, items, width)


def rope(vector, cos, sin):
    parts = []
    for at in range(0, vector.shape[0], HEAD_DIM):
        lower, upper = vector[at : at + HALF], vector[at + HALF : at + HEAD_DIM]
        parts += [lower * cos - upper * sin, lower * sin + upper * cos]
    return jnp.concatenate(parts, 0)


def query_blocks(seq):
    return [(start, min(start + BLOCK, seq)) for start in range(0, seq, BLOCK)]


def limits(start, stop, length):
    position = start + lax.broadcasted_iota(jnp.int32, (1, stop - start), 1)
    return jnp.minimum(position, length - 1)


def score_parts(keys, queries, start, stop, length):
    parts = []
    if start:
        parts.append((0, BLOCK, dot_tn(keys[:, :BLOCK], queries)))
    first = min(start, BLOCK)
    late = dot_tn(keys[:, first:stop], queries)
    position = first + lax.broadcasted_iota(jnp.int32, late.shape, 0)
    late = jnp.where(position <= limits(start, stop, length), late, NEG)
    parts.append((first, stop, late))
    return parts


def norm_rows(inputs):
    return lax.rsqrt(jnp.mean(inputs * inputs, -1, keepdims=True) + EPS)


def attend_item(length, x, weights, gain, cos, sin, query, key, value, attended_t, attended, log_total, normed, ready):
    seq, width = x.shape
    tile = 128
    for at in range(0, seq, tile):
        inputs = x[at : at + tile, :].astype(F32)
        normed[at : at + tile, :] = (inputs * norm_rows(inputs) * gain).astype(LOW)

    project = 256

    def project_tile(at, _):
        rows = pl.ds(pl.multiple_of(at * project, project), project)
        for part, out, scaled in ((0, query, SCALE * LOG2E), (1, key, 1.0)):
            source = pl.ds(pl.multiple_of(part * width + at * project, project), project)
            out[rows, :] = (rope(dot_nt(weights[source, :], normed[...]), cos[...], sin[...]) * scaled).astype(LOW)
        source = pl.ds(pl.multiple_of(2 * width + at * project, project), project)
        value[rows, :] = dot_nt(weights[source, :], normed[...]).astype(LOW)
        return 0

    lax.fori_loop(0, width // project, project_tile, 0)
    ready()

    def head(at, _):
        for which in range(2):
            number = at * 2 + which
            rows = pl.ds(pl.multiple_of(number * HEAD_DIM, HEAD_DIM), HEAD_DIM)
            keys, values = key[rows, :], value[rows, :]
            for start, stop in query_blocks(seq):
                parts = score_parts(keys, query[rows, start:stop], start, stop, length)
                top = functools.reduce(jnp.maximum, [jnp.max(s, 0, keepdims=True) for _, _, s in parts])
                total = jnp.zeros_like(top)
                acc = jnp.zeros((HEAD_DIM, stop - start), F32)
                for first, last, scores in parts:
                    prob = jnp.exp2(scores - top)
                    total += jnp.sum(prob, 0, keepdims=True)
                    acc += dot_nn(values[:, first:last], prob.astype(LOW))
                attended_t[rows, start:stop] = (acc / total).astype(LOW)
                log_total[number, :, start:stop] = top + jnp.log2(total)
        return 0

    lax.fori_loop(0, width // HEAD_DIM // 2, head, 0)
    for at in range(0, width, project):
        attended[:, at : at + project] = attended_t[at : at + project, :].T


WIDE = 512


def feed_item(follows, x, attended, attended_t, cot, w_out, w_feed, w_down, gain, g_feed, g_down, g_out, g_norm, out, grad_attended_t, scratch, tick, before_out):
    normed, normed_t, resid, out_acc, back_acc = scratch
    seq, width = x.shape
    ff = w_down.shape[0]
    tile = 128

    def put(ref, at, grad):
        if follows:
            grad += ref[at].astype(F32)
        ref[at] = grad.astype(LOW)

    for at in range(0, seq, tile):
        rows = slice(at, at + tile)
        total = x[rows, :].astype(F32) + dot_nn(attended[rows, :], w_out[...])
        resid[rows, :] = total.astype(LOW)
        out_acc[rows, :] = total
        low = (total * norm_rows(total) * gain).astype(LOW)
        normed[rows, :] = low
        normed_t[:, rows] = low.T
    back_acc[...] = jnp.zeros_like(back_acc)

    def chunk(step, _):
        tick(step)
        span = pl.ds(pl.multiple_of(step * WIDE, WIDE), WIDE)
        up_span = pl.ds(pl.multiple_of(ff + step * WIDE, WIDE), WIDE)
        lows = []
        for at in range(0, seq, seq // 2):
            rows = slice(at, at + seq // 2)
            gate = dot_nn(normed[rows, :], w_feed[:, span])
            upward = dot_nn(normed[rows, :], w_feed[:, up_span])
            grad_hidden = dot_nt(cot[rows, :], w_down[span, :])
            sig = 0.5 * jnp.tanh(0.5 * gate) + 0.5
            silu = gate * sig
            hidden = (silu * upward).astype(LOW)
            grad_gate = (grad_hidden * upward * (sig + silu * (1.0 - sig))).astype(LOW)
            grad_upward = (grad_hidden * silu).astype(LOW)
            out_acc[rows, :] += dot_nn(hidden, w_down[span, :])
            back_acc[rows, :] += dot_nt(grad_gate, w_feed[:, span])
            back_acc[rows, :] += dot_nt(grad_upward, w_feed[:, up_span])
            lows.append((hidden, grad_gate, grad_upward))
        hidden, grad_gate, grad_upward = (jnp.concatenate(parts, 0) for parts in zip(*lows))
        put(g_down, (span, slice(None)), dot_nn(hidden.T, cot[...]))
        first = pl.ds(pl.multiple_of(step * 2 * WIDE, WIDE), WIDE)
        second = pl.ds(pl.multiple_of(step * 2 * WIDE + WIDE, WIDE), WIDE)
        put(g_feed, (slice(None), first), dot_nn(normed_t[...], grad_gate))
        put(g_feed, (slice(None), second), dot_nn(normed_t[...], grad_upward))
        return 0

    lax.fori_loop(0, ff // WIDE, chunk, 0)
    norm_sum = jnp.zeros((1, width), F32)
    for at in range(0, seq, tile):
        rows = slice(at, at + tile)
        out[rows, :] = out_acc[rows, :].astype(LOW)
        total, incoming = resid[rows, :].astype(F32), back_acc[rows, :]
        inv = norm_rows(total)
        scaled = total * inv
        norm_sum += jnp.sum(incoming * scaled, 0, keepdims=True)
        weighted = incoming * gain
        grad = cot[rows, :].astype(F32) + inv * (weighted - scaled * jnp.mean(weighted * scaled, -1, keepdims=True))
        cot[rows, :] = grad.astype(LOW)
    g_norm[...] = g_norm[...] + norm_sum if follows else norm_sum
    grad_attended_t[...] = dot_nt(w_out[...], cot[...]).astype(LOW)
    before_out()
    put(g_out, (slice(None), slice(None)), dot_nn(attended_t[...], cot[...]))


GROUP = 256
PAIRS = GROUP // (2 * HEAD_DIM)


def back_item(
    follows, length, x, grad_resid, grad_attended, attended, query, key, value, log_total, weights, gain, cos, sin,
    g_weights, g_norm, grads, normed_t, back, tick, heads_done,
):
    seq, width = x.shape
    blocks = query_blocks(seq)
    tile = 128
    for at in range(0, seq, tile):
        inputs = x[at : at + tile, :].astype(F32)
        normed_t[:, at : at + tile] = (inputs * norm_rows(inputs) * gain).astype(LOW).T
    back[...] = jnp.zeros_like(back)

    def group(number, _):
        def pair(at, _):
            tick(number * PAIRS + at)
            for which in range(2):
                local = at * 2 + which
                head = number * (2 * PAIRS) + local
                rows = pl.ds(pl.multiple_of(head * HEAD_DIM, HEAD_DIM), HEAD_DIM)
                keys, values = key[rows, :], value[rows, :]
                delta_all = jnp.sum(grad_attended[rows, :].astype(F32) * attended[rows, :].astype(F32), 0, keepdims=True)
                key_grads = [0.0] * len(blocks)
                value_grads = [0.0] * len(blocks)
                at_query, at_key, at_value = (
                    pl.ds(pl.multiple_of(part * GROUP + local * HEAD_DIM, HEAD_DIM), HEAD_DIM) for part in range(3)
                )
                for start, stop in blocks:
                    queries, incoming = query[rows, start:stop], grad_attended[rows, start:stop]
                    total = log_total[head, :, start:stop]
                    delta = delta_all[:, start:stop]
                    query_grad = 0.0
                    for first, last, scores in score_parts(keys, queries, start, stop, length):
                        prob = jnp.exp2(scores - total)
                        grad_prob = dot_tn(values[:, first:last], incoming)
                        grad_score = (prob * (grad_prob - delta)).astype(LOW)
                        query_grad += dot_nn(keys[:, first:last], grad_score)
                        key_grad = dot_nt(queries, grad_score)
                        value_grad = dot_nt(incoming, prob.astype(LOW))
                        for piece, (low, high) in enumerate(blocks):
                            if first <= low and high <= last:
                                key_grads[piece] += key_grad[:, low - first : high - first]
                                value_grads[piece] += value_grad[:, low - first : high - first]
                    grads[at_query, start:stop] = (
                        rope(query_grad, cos[:, start:stop], -sin[:, start:stop]) * SCALE
                    ).astype(LOW)
                for (start, stop), key_grad, value_grad in zip(blocks, key_grads, value_grads):
                    grads[at_key, start:stop] = (
                        rope(key_grad, cos[:, start:stop], -sin[:, start:stop]) * (1.0 / LOG2E)
                    ).astype(LOW)
                    grads[at_value, start:stop] = value_grad.astype(LOW)
            return 0

        lax.fori_loop(0, PAIRS, pair, 0)
        turned = grads[...].T
        columns = pl.ds(pl.multiple_of(number * 3 * GROUP, GROUP), 3 * GROUP)
        for at in range(0, width, GROUP):
            rows = slice(at, at + GROUP)
            grad = dot_nn(normed_t[rows, :], turned)
            if follows:
                grad += g_weights[rows, columns].astype(F32)
            g_weights[rows, columns] = grad.astype(LOW)
        total = back[...]
        for part in range(3):
            source = pl.ds(pl.multiple_of(part * width + number * GROUP, GROUP), GROUP)
            total += dot_nn(turned[:, part * GROUP : (part + 1) * GROUP], weights[source, :])
        back[...] = total
        return 0

    lax.fori_loop(0, width // GROUP, group, 0)
    heads_done()
    norm_sum = jnp.zeros((1, width), F32)
    for at in range(0, seq, tile):
        rows = slice(at, at + tile)
        inputs, incoming = x[rows, :].astype(F32), back[rows, :]
        inv = norm_rows(inputs)
        scaled = inputs * inv
        norm_sum += jnp.sum(incoming * scaled, 0, keepdims=True)
        weighted = incoming * gain
        grad = grad_resid[rows, :].astype(F32) + inv * (
            weighted - scaled * jnp.mean(weighted * scaled, -1, keepdims=True)
        )
        grad_resid[rows, :] = grad.astype(LOW)
    g_norm[...] = g_norm[...] + norm_sum if follows else norm_sum


class Links:
    def __init__(self, bands, send, receive):
        self.send, self.receive, self.bands = send, receive, bands
        self.band, self.items = lax.axis_index("band"), lax.axis_index("items")
        self.count = 0

    def take(self, count):
        first = self.count
        self.count += count
        return first

    def other(self, shift):
        return lax.rem(self.band + shift + self.bands, self.bands)

    def greet(self, axis):
        barrier = pltpu.get_barrier_semaphore()
        others = [(self.items, self.other(shift)) for shift in range(1, self.bands)]
        if axis:
            others += [(flipped(self.items, at), self.band) for at in range(log2_of(axis))]
        for other in others:
            pl.semaphore_signal(barrier, inc=1, device_id=other, device_id_type=MESH)
        pl.semaphore_wait(barrier, len(others))

    def copy(self, number, source, target, device):
        return pltpu.make_async_remote_copy(
            src_ref=source,
            dst_ref=target,
            send_sem=self.send.at[number],
            recv_sem=self.receive.at[number],
            device_id=device,
            device_id_type=MESH,
        )


class Exchange:
    def __init__(self, links, source, target, arrival):
        self.links, self.first = links, links.take(links.bands - 1)
        self.source, self.target, self.arrival = source, target, arrival

    def each(self, place):
        for shift in range(1, self.links.bands):
            yield self.links.copy(
                self.first + shift - 1, self.source(shift), place(shift), (self.links.items, self.links.other(shift))
            )

    def start(self):
        for copy in self.each(self.target):
            copy.start()

    def arrived(self):
        for copy in self.each(self.arrival):
            copy.wait_recv()

    def left(self):
        for copy in self.each(self.target):
            copy.wait_send()


def bit(number, at):
    return lax.rem(lax.div(number, 2**at), 2)


def flipped(number, at):
    return number + (1 - 2 * bit(number, at)) * 2**at


def replaced(number, bits, choice):
    for order, at in enumerate(bits):
        number = number + ((choice >> order & 1) - bit(number, at)) * 2**at
    return number


def sum_lanes(axis, stage, columns):
    left = list(range(log2_of(axis)))
    right = [0] + left[:0:-1]
    half = columns // 2
    if stage == 0:
        return [(left[0], left[1:], 0, columns)]
    return [(left[stage], left[stage + 1 :], 0, half), (right[stage], right[stage + 1 :], half, half)]


def band_shape(axis, bands, shape):
    rows = shape[0] // axis // bands
    return (rows, shape[1]) if rows % 16 == 0 else (2 * rows, shape[1] // 2)


def sum_scratch(axis, bands, shape):
    low = lambda *dims: pltpu.VMEM(dims, LOW)
    out = []
    for stage in range(log2_of(axis)):
        for _, bits, _, columns in sum_lanes(axis, stage, shape[1]):
            out.append(low(2 ** len(bits), shape[0] // axis, columns))
    part = band_shape(axis, bands, shape)
    out.append(low(bands, *part))
    for stage in range(log2_of(bands)):
        out.append(low(bands >> stage + 1, *part))
    return out


def sum_links(axis, bands):
    return axis // 2 + 2 * (axis // 2 - 1) + bands - 1


class Summing:
    def __init__(self, links, axis, array, first, columns, scratch, finish):
        self.links, self.axis, self.array, self.finish = links, axis, array, finish
        self.first, self.columns = first, columns
        self.count = log2_of(axis)
        self.stages = self.count + log2_of(links.bands)
        self.scratch = scratch
        self.base = links.take(sum_links(axis, links.bands))
        self.state = 0

    def piece(self, number, first, columns):
        rows = self.array.shape[0] // self.axis
        return self.array.at[pl.ds(pl.multiple_of(number * rows, rows), rows), pl.ds(self.first + first, columns)]

    def flights(self, stage):
        me, band = self.links.items, self.links.band
        number, out = self.base, []
        for at in range(self.stages):
            if at < self.count:
                taken = [0] if at == 0 else [2 * at - 1, 2 * at]
                lanes = sum_lanes(self.axis, at, self.columns)
            else:
                taken = [self.count + at]
                lanes = [(at - self.count, list(range(at - self.count + 1, log2_of(self.links.bands))), 0, 0)]
            for (axis_bit, bits, first, columns), buffer in zip(lanes, taken):
                for choice in range(2 ** len(bits)):
                    if at == stage:
                        came = self.scratch[buffer].at[choice]
                        if at < self.count:
                            other = flipped(me, axis_bit)
                            device = (other, band)
                            sent = self.piece(replaced(other, bits, choice), first, columns)
                            kept = self.piece(replaced(me, bits, choice), first, columns)
                        else:
                            other = flipped(band, axis_bit)
                            device = (me, other)
                            parts = self.scratch[2 * self.count - 1]
                            sent, kept = parts.at[replaced(other, bits, choice)], parts.at[replaced(band, bits, choice)]
                        out.append((self.links.copy(number, sent, came, device), kept, came))
                    number += 1
        return out

    def begin(self, stage):
        for copy, _, _ in self.flights(stage):
            copy.start()

    def end(self, stage):
        flights = self.flights(stage)
        for copy, _, _ in flights:
            copy.wait_recv()
        for _, kept, came in flights:
            if stage == self.stages - 1:
                self.finish(kept[...].astype(F32) + came[...].astype(F32))
                continue
            tile = 16

            def add(step, _, kept=kept, came=came):
                rows = pl.ds(pl.multiple_of(step * tile, tile), tile)
                kept[rows, :] = (kept[rows, :].astype(F32) + came[rows, :].astype(F32)).astype(LOW)
                return 0

            lax.fori_loop(0, kept.shape[0] // tile, add, 0)
        if stage == self.count - 1:
            self.stack()

    def stack(self):
        bands = self.links.bands
        parts = self.scratch[2 * self.count - 1]
        whole = self.piece(self.links.items, 0, self.columns)
        rows = whole.shape[0] // bands
        if parts.shape[1] == rows:
            for number in range(bands):
                parts[number] = whole[number * rows : (number + 1) * rows, :]
            return
        half = self.columns // 2
        left, right = whole[:, :half].astype(F32), whole[:, half:].astype(F32)
        for number in range(bands):
            span = slice(number * rows, (number + 1) * rows)
            parts[number] = jnp.concatenate([left[span], right[span]], 0).astype(LOW)

    def advance(self):
        if self.state > self.stages:
            return
        if self.state > 0:
            self.end(self.state - 1)
        if self.state < self.stages:
            self.begin(self.state)
        self.state += 1

    def close(self):
        for stage in range(self.stages):
            for copy, _, _ in self.flights(stage):
                copy.wait_send()


def block_kernel(bands, per, axis, *refs):
    fused = axis > 0
    lengths, norm_attn, norm_ffn, cos, sin = refs[:5]
    tokens, cotangent, w_query, w_key, w_value, w_out_from, w_gate, w_up, w_down_from = refs[5:14]
    refs = refs[14:]
    home_out, home_grad = refs[:2]
    query_far, key_far, value_far, attended_t_far, grad_attended_t_far, cot_far = refs[2:8]
    refs = refs[8:]
    sums, refs = (refs[:8], refs[8:]) if fused else (refs[:5], refs[5:])
    weights_t, w_out, w_feed, w_down, g_feed, g_down, g_out = refs[:7]
    x, cot, attended, attended_t, query, key, value, grad_attended_t = refs[7:15]
    normed, normed_t, resid, out_acc, back_acc, log_total, g_norm, g_norm_ffn = refs[15:23]
    local, send, receive = refs[23:26]
    sum_refs = refs[26:]
    seq, width = x.shape[1:]
    ff = w_down.shape[0]
    band_rows, items = seq // bands, bands * per
    groups = width // GROUP
    links = Links(bands, send, receive)
    band = links.band
    gain_attn, gain_ffn = norm_attn[...][None, :], norm_ffn[...][None, :]
    started = [0]

    def bring(source, target):
        copy = pltpu.make_async_copy(source, target, local.at[started[0]])
        started[0] += 1
        copy.start()
        return copy

    token_rows = band_rows * items
    raw = g_down.at[pl.ds(0, token_rows)]
    load_tokens = bring(tokens, raw)
    qkv = (g_feed.at[:, pl.ds(0, width)], g_feed.at[:, pl.ds(width, width)], g_feed.at[:, pl.ds(2 * width, width)])
    load_qkv = [bring(source, target) for source, target in zip((w_query, w_key, w_value), qkv)]
    links.greet(axis)

    def own_rows(shift):
        return pl.ds(pl.multiple_of(links.other(shift) * band_rows, band_rows), band_rows)

    chunk = 32 if band_rows % 32 == 0 else 16
    size = items * chunk
    order = split_order(items, chunk, band * per)
    token_send = [attended.at[item] for item in range(per)]
    stages = [normed, resid]
    cot_send = [g_out] + [cot_far.at[item] for item in range(per - 1)]

    def split(kept, sent):
        for block in range(band_rows // chunk):
            moved = dot_nn(order, raw[block * size : (block + 1) * size, :]).astype(LOW)
            rows = pl.ds(pl.multiple_of(band * band_rows + block * chunk, 16), chunk)
            for at in range(items):
                part = moved[at * chunk : (at + 1) * chunk]
                shift, item = at // per, at % per
                if shift == 0:
                    kept[item, rows, :] = part
                else:
                    place = (shift - 1) * band_rows + block * chunk
                    sent[item][place : place + chunk, :] = part

    def scattering(sent, kept, item):
        return Exchange(
            links,
            lambda shift: sent[item].at[pl.ds((shift - 1) * band_rows, band_rows)],
            lambda shift: kept.at[item, own_rows(0)],
            lambda shift: kept.at[item, own_rows(-shift)],
        )

    def returning(source, home, item):
        slot = lambda shift: home.at[shift * per + item]
        return Exchange(links, lambda shift: source.at[item, own_rows(shift)], slot, slot)

    token_links = [scattering(token_send, x, item) for item in range(per)]
    cot_links = [scattering(cot_send, cot, item) for item in range(per)]
    out_links = [returning(attended, home_out, item) for item in range(per)]
    grad_links = [returning(cot, home_grad, item) for item in range(per)]

    load_tokens.wait()
    split(x, token_send)
    token_links[0].start()
    load_cot = bring(cotangent, raw)
    load_rest = [
        bring(w_out_from, w_out),
        bring(w_gate, w_feed.at[:, pl.ds(0, ff)]),
        bring(w_up, w_feed.at[:, pl.ds(ff, ff)]),
        bring(w_down_from, w_down),
    ]
    for part in range(3):
        load_qkv[part].wait()
        for at in range(0, width, 256):
            weights_t[part * width + at : part * width + at + 256, :] = qkv[part][:, at : at + 256].T
    load_cot.wait()
    split(cot, [g_out] + stages[: per - 1])
    late = pl.ds(0, (bands - 1) * band_rows)
    to_far = [bring(stages[item].at[late], cot_far.at[item]) for item in range(per - 1)]

    sums_of = {}
    schedule = {}
    if fused:
        scratch_each = len(sum_scratch(axis, bands, (axis * bands * 16, 256)))
        taken = [0]
        o_gate, o_up, o_down, o_out, o_query, o_key, o_value, o_norm = sums

        def summing(name, array, first, columns, finish):
            sums_of[name] = Summing(
                links, axis, array, first, columns, sum_refs[taken[0] : taken[0] + scratch_each], finish
            )
            taken[0] += scratch_each

        def halves(total):
            rows = total.shape[0] // 2
            return total[:rows], total[rows:]

        for step in range(ff // WIDE):

            def finish_feed(total, step=step):
                span = slice(step * WIDE, (step + 1) * WIDE)
                o_gate[:, span], o_up[:, span] = halves(total)

            summing(("feed", step), g_feed, step * 2 * WIDE, 2 * WIDE, finish_feed)

        def finish_down(total):
            o_down[...] = total

        def finish_out(total):
            o_out[:, : width // 2], o_out[:, width // 2 :] = halves(total)

        def finish_norm(total):
            o_norm[:, :128], o_norm[:, 128:] = halves(total)

        summing("down", g_down, 0, width, finish_down)
        summing("out", g_out, 0, width, finish_out)
        for number in range(groups):

            def finish_group(total, number=number):
                left, right = halves(total)
                at, half = number * GROUP, GROUP // 2
                o_query[:, at : at + GROUP] = left[:, :GROUP]
                o_key[:, at : at + half] = left[:, GROUP:]
                o_key[:, at + half : at + GROUP] = right[:, :half]
                o_value[:, at : at + GROUP] = right[:, half:]

            summing(("back", number), w_feed, number * 3 * GROUP, 3 * GROUP, finish_group)
        summing("norm", w_feed, 3 * width, 256, finish_norm)

    def advance(*names):
        for name in names:
            sums_of[name].advance()

    spills = []

    def spill(pairs):
        spills.extend(bring(source, target) for source, target in pairs)

    def settle():
        while spills:
            spills.pop().wait()

    g_weights = w_feed
    grads = w_feed.at[pl.ds(0, 3 * GROUP), pl.ds(3 * width + 256, seq)]
    for item in range(per):
        last = item == per - 1
        if item == 0:
            token_links[0].arrived()
            cot_links[0].start()
            for copy in to_far:
                copy.wait()
        settle()

        def projected(item=item):
            token_links[item].left()
            if item < per - 1:
                spill(
                    (source, target.at[item])
                    for source, target in ((query, query_far), (key, key_far), (value, value_far))
                )

        attend_item(
            lengths[band * per + item], x.at[item], weights_t, gain_attn, cos, sin, query, key, value, attended_t,
            attended.at[item], log_total.at[item], normed, projected,
        )
        if item == 0:
            for load in load_rest:
                load.wait()
        cot_links[item].arrived()
        if last:
            for ahead in range(per - 1):
                out_links[ahead].start()
        else:
            token_links[item + 1].start()

        def feed_tick(step, item=item, last=last):
            if not last:

                @pl.when(step == ff // WIDE - 1)
                def _():
                    token_links[item + 1].arrived()
                    cot_links[item + 1].start()

            elif fused:
                for at in range(1, ff // WIDE):

                    @pl.when(step == at)
                    def _(at=at):
                        advance(*[("feed", number) for number in range(at)])

        def before_out(item=item):
            if item == 0:
                cot_links[0].left()

        feed_item(
            item > 0, x.at[item], attended.at[item], attended_t, cot.at[item], w_out, w_feed, w_down, gain_ffn,
            g_feed, g_down, g_out, g_norm_ffn, attended.at[item], grad_attended_t,
            (normed, normed_t, resid, out_acc, back_acc), feed_tick, before_out,
        )
        if not last:
            spill(
                (source, target.at[item])
                for source, target in ((attended_t, attended_t_far), (grad_attended_t, grad_attended_t_far))
            )
    out_links[per - 1].start()
    feeds = [("feed", step) for step in range(ff // WIDE)]
    if fused:
        advance(*feeds, "down", "out")
    turns = list(reversed(range(per)))
    reloads = []
    for turn, item in enumerate(turns):
        last = turn == per - 1

        def back_tick(at, turn=turn, last=last):
            if not fused:
                return
            for place, names in plan(turn, last).items():

                @pl.when(at == place)
                def _(names=names):
                    advance(*names)

        def plan(turn, last):
            out = {}
            for place in range(groups * PAIRS):
                names = []
                if turn == 0 and place % 2 == 1:
                    names += feeds
                if turn == 0 and place in (2, 5) or turn == 1 and place in (1, 3, 5):
                    names += ["down", "out"]
                if turn == 1 and place == 0:
                    names += feeds
                if last and place >= PAIRS:
                    names += [("back", number) for number in range(place // PAIRS)]
                if names:
                    out[place] = names
            return out

        def heads_done(turn=turn, last=last):
            if not last:
                following = turns[turn + 1]
                for source, target in (
                    (query_far, query), (key_far, key), (value_far, value), (attended_t_far, attended_t),
                    (grad_attended_t_far, grad_attended_t),
                ):
                    reloads.append(bring(source.at[following], target))
            elif fused:
                advance(*[("back", number) for number in range(groups)])

        back_item(
            turn > 0, lengths[band * per + item], x.at[item], cot.at[item], grad_attended_t, attended_t, query, key,
            value, log_total.at[item], weights_t, gain_attn, cos, sin, g_weights, g_norm, grads, normed_t, back_acc,
            back_tick, heads_done,
        )
        grad_links[item].start()
        while reloads:
            reloads.pop().wait()
    own = []
    for item in range(per):
        own.append(bring(attended.at[item, own_rows(0)], home_out.at[item]))
        own.append(bring(cot.at[item, own_rows(0)], home_grad.at[item]))
    if fused:
        lanes = 128
        pad = jnp.zeros((lanes - 1, width), F32)
        for at, total in enumerate((g_norm, g_norm_ffn)):
            spread = jnp.concatenate([total[...], pad], 0).T
            w_feed[:, 3 * width + at * lanes : 3 * width + (at + 1) * lanes] = spread.astype(LOW)
        every = feeds + ["down", "out"] + [("back", number) for number in range(groups)] + ["norm"]
        while any(sums_of[name].state <= sums_of[name].stages for name in every):
            advance(*every)
        for name in every:
            sums_of[name].close()
    else:
        own += [
            bring(source, target)
            for source, target in zip((g_feed, g_down, g_out, g_weights.at[:, pl.ds(0, 3 * width)]), sums[:4])
        ]
        sums[4][0:1, :] = g_norm[...]
        sums[4][1:2, :] = g_norm_ffn[...]
    for copy in own:
        copy.wait()
    for item in range(per):
        for exchange in (out_links[item], grad_links[item]):
            exchange.arrived()
            exchange.left()
        if item:
            cot_links[item].left()


def block(bands, axis, lengths, tokens, cotangent, gains, tables, weights):
    band_rows, items, width = tokens.shape
    per, seq, ff = items // bands, bands * band_rows, weights[4].shape[1]
    fused = axis > 0
    low = lambda *shape: jax.ShapeDtypeStruct(shape, LOW)
    full = lambda *shape: jax.ShapeDtypeStruct(shape, F32)
    scratch = lambda *shape: pltpu.VMEM(shape, LOW)
    wide = lambda *shape: pltpu.VMEM(shape, F32)
    outside = pl.BlockSpec(memory_space=pl.ANY)
    inside = pl.BlockSpec(memory_space=pltpu.VMEM)
    out_shape = [low(items, band_rows, width)] * 2 + [low(max(per - 1, 1), width, seq)] * 5
    out_shape += [low(max(per - 1, 1), (bands - 1) * band_rows, width)]
    out_specs = [outside] * 8
    extra, links = [], 4 * per * (bands - 1)
    if fused:
        devices = axis * bands
        rows, ff_rows = width // devices, ff // devices
        out_shape += [full(rows, ff), full(rows, ff), full(ff_rows, width)] + [full(rows, width)] * 4 + [full(rows, 256)]
        out_specs += [inside] * 8
        shapes = [(width, 2 * WIDE)] * (ff // WIDE) + [(ff, width), (width, width)]
        shapes += [(width, 3 * GROUP)] * (width // GROUP) + [(width, 256)]
        for shape in shapes:
            extra += sum_scratch(axis, bands, shape)
        links += len(shapes) * sum_links(axis, bands)
    else:
        out_shape += [low(width, 2 * ff), low(ff, width), low(width, width), low(width, 3 * width), full(2, width)]
        out_specs += [outside] * 4 + [inside]
    return pl.pallas_call(
        functools.partial(block_kernel, bands, per, axis),
        name="block",
        out_shape=out_shape,
        in_specs=[smem()] + [inside] * 4 + [outside] * 9,
        out_specs=out_specs,
        scratch_shapes=[
            scratch(3 * width, width), scratch(width, width), scratch(width, 2 * ff), scratch(ff, width),
            scratch(width, 2 * ff), scratch(ff, width), scratch(width, width),
            scratch(per, seq, width), scratch(per, seq, width), scratch(per, seq, width), scratch(width, seq),
            scratch(width, seq), scratch(width, seq), scratch(width, seq), scratch(width, seq),
            scratch(seq, width), scratch(width, seq), scratch(seq, width), wide(seq, width), wide(seq, width),
            wide(per, width // HEAD_DIM, 1, seq), wide(1, width), wide(1, width),
            pltpu.SemaphoreType.DMA((16 + 12 * per,)),
            pltpu.SemaphoreType.DMA((links,)),
            pltpu.SemaphoreType.DMA((links,)),
        ]
        + extra,
        compiler_params=pltpu.CompilerParams(vmem_limit_bytes=64 * 2**20 - 2**16, collective_id=0, has_side_effects=True),
    )(
        lengths, *gains, *tables, tokens.reshape(band_rows * items, width), cotangent.reshape(band_rows * items, width),
        *weights,
    )


def rope_tables(seq):
    frequency = np.exp(-np.log(ROPE_BASE) * (2.0 * np.arange(HALF) / HEAD_DIM))
    angles = frequency[:, None] * np.arange(seq)[None, :]
    return jnp.asarray(np.cos(angles), F32), jnp.asarray(np.sin(angles), F32)


def per_device(
    bands,
    axis,
    tokens,
    lengths,
    norm_attn,
    w_query,
    w_key,
    w_value,
    w_out,
    norm_ffn,
    w_gate,
    w_up,
    w_down,
    cotangent,
):
    band_rows, items, width = tokens.shape
    per = items // bands
    seq = bands * band_rows
    band = lax.axis_index("band")
    fused = axis if width // axis % 16 == 0 and w_gate.shape[1] // axis % 16 == 0 else 0
    home_out, home_grad, *sums = block(
        bands, fused, lengths, tokens, cotangent, (norm_attn, norm_ffn), rope_tables(seq),
        (w_query, w_key, w_value, w_out, w_gate, w_up, w_down),
    )
    sums = sums[6:]
    output = merge_items([home_out[at] for at in range(items)], band, bands)
    grad_tokens = merge_items([home_grad[at] for at in range(items)], band, bands)
    if fused:
        g_gate, g_up, g_down, g_out, g_query, g_key, g_value, norms = sums
        g_norm_attn, g_norm_ffn = norms[:, 0], norms[:, 128]
    else:
        axes = ("items", "band")
        total = lambda a: lax.psum_scatter(a, axes, scatter_dimension=0, tiled=True).astype(F32)
        g_feed, g_down, g_out, g_weights = (total(a) for a in sums[:4])
        norms = total(sums[4].T)
        g_norm_attn, g_norm_ffn = norms[:, 0], norms[:, 1]
        g_gate, g_up = jnp.moveaxis(g_feed.reshape(-1, w_gate.shape[1] // WIDE, 2, WIDE), 2, 0).reshape(2, -1, w_gate.shape[1])
        g_query, g_key, g_value = jnp.moveaxis(g_weights.reshape(-1, width // GROUP, 3, GROUP), 2, 0).reshape(3, -1, width)
    return (
        output,
        grad_tokens,
        g_norm_attn,
        g_query,
        g_key,
        g_value,
        g_out,
        g_norm_ffn,
        g_gate,
        g_up,
        g_down,
    )


def solution(mesh):
    split = P("band", "items", None)
    rows = P(("items", "band"), None)
    flat = P(("items", "band"))
    return jax.shard_map(
        functools.partial(per_device, mesh.shape["band"], mesh.shape["items"]),
        mesh=mesh,
        in_specs=(split, P("items")) + (P(),) * 9 + (split,),
        out_specs=(split, split, flat, rows, rows, rows, rows, flat, rows, rows, rows),
        check_vma=False,
    )
```

```python
import functools

import jax
import jax.numpy as jnp
import numpy as np
from jax import lax
from jax.experimental import pallas as pl
from jax.experimental.pallas import tpu as pltpu
from jax.sharding import PartitionSpec as P

HEAD_DIM = 64
HALF = HEAD_DIM // 2
EPS = 1e-05
NEG = -1e30
ROPE_BASE = 10000.0
LOG2E = 1.4426950408889634
SCALE = HEAD_DIM**-0.5
BLOCK = 256
F32 = jnp.float32
LOW = jnp.bfloat16
MESH = pl.DeviceIdType.MESH


def dot_nn(left, right):
    return lax.dot_general(left, right, (((1,), (0,)), ((), ())), preferred_element_type=F32)


def dot_nt(left, right):
    return lax.dot_general(left, right, (((1,), (1,)), ((), ())), preferred_element_type=F32)


def dot_tn(left, right):
    return lax.dot_general(left, right, (((0,), (0,)), ((), ())), preferred_element_type=F32)


def vmem(count):
    return [pl.BlockSpec(memory_space=pltpu.VMEM)] * count


def smem():
    return pl.BlockSpec(memory_space=pltpu.SMEM)


def params(mib):
    return pltpu.CompilerParams(vmem_limit_bytes=mib * 2**20)


def log2_of(number):
    return number.bit_length() - 1


def split_order(items, chunk, first):
    size = items * chunk
    row = lax.broadcasted_iota(jnp.int32, (size, size), 0)
    col = lax.broadcasted_iota(jnp.int32, (size, size), 1)
    item = (row >> log2_of(chunk)) + first
    item = jnp.where(item >= items, item - items, item)
    return jnp.where(col == (row & (chunk - 1)) * items + item, 1.0, 0.0).astype(LOW)


def merge_kernel(per, chunk, band_ref, *refs):
    count = (len(refs) - 1) // 4
    ins, outs, held, made, sem = refs[:count], refs[count : 2 * count], refs[2 * count : 3 * count], refs[3 * count : -1], refs[-1]
    loads = [pltpu.make_async_copy(ins[at], held[at], sem.at[at]) for at in range(count)]
    for load in loads:
        load.start()
    items, band_rows, width = ins[0].shape
    size, bands = items * chunk, items // per
    row = lax.broadcasted_iota(jnp.int32, (size, size), 0)
    col = lax.broadcasted_iota(jnp.int32, (size, size), 1)
    number = col >> log2_of(chunk)
    source = band_ref[0] - (number >> log2_of(per))
    source = jnp.where(source < 0, source + bands, source)
    item = source * per + (number & (per - 1))
    order = jnp.where(row == (col & (chunk - 1)) * items + item, 1.0, 0.0).astype(LOW)
    stores = []
    for at in range(count):
        loads[at].wait()
        for block in range(band_rows // chunk):
            rows = slice(block * size, (block + 1) * size)
            parts = held[at][:, block * chunk : (block + 1) * chunk, :].reshape(size, width)
            made[at][rows, :] = dot_nn(order, parts).astype(LOW)
        stores.append(pltpu.make_async_copy(made[at], outs[at], sem.at[count + at]))
        stores[-1].start()
    for store in stores:
        store.wait()


def merge_items(arrays, band, bands):
    items, band_rows, width = arrays[0].shape
    chunk = 32 if band_rows % 32 == 0 else 16
    count = len(arrays)
    outside = pl.BlockSpec(memory_space=pl.ANY)
    merged = pl.pallas_call(
        functools.partial(merge_kernel, items // bands, chunk),
        name="merge_items",
        out_shape=[jax.ShapeDtypeStruct((band_rows * items, width), LOW)] * count,
        in_specs=[smem()] + [outside] * count,
        out_specs=[outside] * count,
        scratch_shapes=[pltpu.VMEM((items, band_rows, width), LOW)] * count
        + [pltpu.VMEM((band_rows * items, width), LOW)] * count
        + [pltpu.SemaphoreType.DMA((2 * count,))],
        compiler_params=params(60),
    )(jnp.reshape(band, (1,)), *arrays)
    return [array.reshape(band_rows, items, width) for array in merged]


def rope(vector, cos, sin):
    parts = []
    for at in range(0, vector.shape[0], HEAD_DIM):
        lower, upper = vector[at : at + HALF], vector[at + HALF : at + HEAD_DIM]
        parts += [lower * cos - upper * sin, lower * sin + upper * cos]
    return jnp.concatenate(parts, 0)


def query_blocks(seq):
    return [(start, min(start + BLOCK, seq)) for start in range(0, seq, BLOCK)]


def limits(start, stop, length):
    position = start + lax.broadcasted_iota(jnp.int32, (1, stop - start), 1)
    return jnp.minimum(position, length - 1)


def score_parts(keys, queries, start, stop, length):
    parts = []
    if start:
        parts.append((0, BLOCK, dot_tn(keys[:, :BLOCK], queries)))
    first = min(start, BLOCK)
    late = dot_tn(keys[:, first:stop], queries)
    position = first + lax.broadcasted_iota(jnp.int32, late.shape, 0)
    late = jnp.where(position <= limits(start, stop, length), late, NEG)
    parts.append((first, stop, late))
    return parts


def norm_rows(inputs):
    return lax.rsqrt(jnp.mean(inputs * inputs, -1, keepdims=True) + EPS)


def attend_item(length, x, weights, gain, cos, sin, query, key, value, attended_t, attended, log_total, normed, ready):
    seq, width = x.shape
    tile = 128
    for at in range(0, seq, tile):
        inputs = x[at : at + tile, :].astype(F32)
        normed[at : at + tile, :] = (inputs * norm_rows(inputs) * gain).astype(LOW)

    project = 256

    def project_tile(at, _):
        rows = pl.ds(pl.multiple_of(at * project, project), project)
        for part, out, scaled in ((0, query, SCALE * LOG2E), (1, key, 1.0)):
            source = pl.ds(pl.multiple_of(part * width + at * project, project), project)
            out[rows, :] = (rope(dot_nt(weights[source, :], normed[...]), cos[...], sin[...]) * scaled).astype(LOW)
        source = pl.ds(pl.multiple_of(2 * width + at * project, project), project)
        value[rows, :] = dot_nt(weights[source, :], normed[...]).astype(LOW)
        return 0

    lax.fori_loop(0, width // project, project_tile, 0)
    ready()

    def head(at, _):
        for which in range(2):
            number = at * 2 + which
            rows = pl.ds(pl.multiple_of(number * HEAD_DIM, HEAD_DIM), HEAD_DIM)
            keys, values = key[rows, :], value[rows, :]
            for start, stop in query_blocks(seq):
                parts = score_parts(keys, query[rows, start:stop], start, stop, length)
                top = functools.reduce(jnp.maximum, [jnp.max(s, 0, keepdims=True) for _, _, s in parts])
                total = jnp.zeros_like(top)
                acc = jnp.zeros((HEAD_DIM, stop - start), F32)
                for first, last, scores in parts:
                    prob = jnp.exp2(scores - top)
                    total += jnp.sum(prob, 0, keepdims=True)
                    acc += dot_nn(values[:, first:last], prob.astype(LOW))
                attended_t[rows, start:stop] = (acc / total).astype(LOW)
                log_total[number, :, start:stop] = top + jnp.log2(total)
        return 0

    lax.fori_loop(0, width // HEAD_DIM // 2, head, 0)
    for at in range(0, width, project):
        attended[:, at : at + project] = attended_t[at : at + project, :].T


LANES = 128
GROUP = 256
WIDE = 512


def feed_item(follows, x, attended, attended_t, cot, w_out, w_feed, w_down, gain, g_feed, g_down, g_out, g_norm, out, grad_attended_t, scratch, tick):
    normed, normed_t, resid, out_acc, back_acc = scratch
    seq, width = x.shape
    ff = w_down.shape[0]
    tile = 128

    def put(ref, at, grad):
        if follows:
            grad += ref[at].astype(F32)
        ref[at] = grad.astype(LOW)

    for at in range(0, seq, tile):
        rows = slice(at, at + tile)
        total = x[rows, :].astype(F32) + dot_nn(attended[rows, :], w_out[...])
        resid[rows, :] = total.astype(LOW)
        out_acc[rows, :] = total
        low = (total * norm_rows(total) * gain).astype(LOW)
        normed[rows, :] = low
        normed_t[:, rows] = low.T
    back_acc[...] = jnp.zeros_like(back_acc)

    def chunk(step, _):
        tick(step)
        span = pl.ds(pl.multiple_of(step * WIDE, WIDE), WIDE)
        up_span = pl.ds(pl.multiple_of(ff + step * WIDE, WIDE), WIDE)
        lows = []
        for at in range(0, seq, seq // 2):
            rows = slice(at, at + seq // 2)
            parts = []
            for first in range(0, WIDE, WIDE // 2):
                columns = pl.ds(pl.multiple_of(step * WIDE + first, WIDE // 2), WIDE // 2)
                up_columns = pl.ds(pl.multiple_of(ff + step * WIDE + first, WIDE // 2), WIDE // 2)
                gate = dot_nn(normed[rows, :], w_feed[:, columns])
                upward = dot_nn(normed[rows, :], w_feed[:, up_columns])
                grad_hidden = dot_nt(cot[rows, :], w_down[columns, :])
                sig = 0.5 * jnp.tanh(0.5 * gate) + 0.5
                silu = gate * sig
                hidden = (silu * upward).astype(LOW)
                grad_gate = (grad_hidden * upward * (sig + silu * (1.0 - sig))).astype(LOW)
                grad_upward = (grad_hidden * silu).astype(LOW)
                parts.append((hidden, grad_gate, grad_upward))
            hidden, grad_gate, grad_upward = (jnp.concatenate(both, 1) for both in zip(*parts))
            out_acc[rows, :] += dot_nn(hidden, w_down[span, :])
            back_acc[rows, :] += dot_nt(grad_gate, w_feed[:, span])
            back_acc[rows, :] += dot_nt(grad_upward, w_feed[:, up_span])
            lows.append((hidden, grad_gate, grad_upward))
        hidden, grad_gate, grad_upward = (jnp.concatenate(parts, 0) for parts in zip(*lows))
        half = WIDE // 2
        for at in range(0, WIDE, half):
            part = pl.ds(pl.multiple_of(step * WIDE + at, half), half)
            put(g_down, (part, slice(None)), dot_nn(hidden[:, at : at + half].T, cot[...]))
        first = pl.ds(pl.multiple_of(step * 2 * WIDE, WIDE), WIDE)
        second = pl.ds(pl.multiple_of(step * 2 * WIDE + WIDE, WIDE), WIDE)
        half = width // 2
        for at in range(0, width, half):
            part = slice(at, at + half)
            put(g_feed, (part, first), dot_nn(normed_t[part, :], grad_gate))
            put(g_feed, (part, second), dot_nn(normed_t[part, :], grad_upward))
        return 0

    lax.fori_loop(0, ff // WIDE, chunk, 0)
    norm_sum = jnp.zeros((1, width), F32)
    for at in range(0, seq, tile):
        rows = slice(at, at + tile)
        out[rows, :] = out_acc[rows, :].astype(LOW)
        total, incoming = resid[rows, :].astype(F32), back_acc[rows, :]
        inv = norm_rows(total)
        scaled = total * inv
        norm_sum += jnp.sum(incoming * scaled, 0, keepdims=True)
        weighted = incoming * gain
        grad = cot[rows, :].astype(F32) + inv * (weighted - scaled * jnp.mean(weighted * scaled, -1, keepdims=True))
        cot[rows, :] = grad.astype(LOW)
    g_norm[...] = g_norm[...] + norm_sum if follows else norm_sum
    for at in range(0, width, GROUP):
        rows = slice(at, at + GROUP)
        grad_attended_t[rows, :] = dot_nt(w_out[rows, :], cot[...]).astype(LOW)
    for at in range(0, width, GROUP):
        rows = slice(at, at + GROUP)
        put(g_out, (rows, slice(0, width)), dot_nn(attended_t[rows, :], cot[...]))


PAIRS = GROUP // (2 * HEAD_DIM)


def back_item(
    follows, length, x, grad_resid, grad_attended, attended, query, key, value, log_total, weights, gain, cos, sin,
    g_weights, g_norm, grads, normed_t, back, tick, heads_done,
):
    seq, width = x.shape
    blocks = query_blocks(seq)
    tile = 128
    for at in range(0, seq, tile):
        inputs = x[at : at + tile, :].astype(F32)
        normed_t[:, at : at + tile] = (inputs * norm_rows(inputs) * gain).astype(LOW).T
    back[...] = jnp.zeros_like(back)

    def group(number, _):
        def pair(at, _):
            tick(number * PAIRS + at)
            for which in range(2):
                local = at * 2 + which
                head = number * (2 * PAIRS) + local
                rows = pl.ds(pl.multiple_of(head * HEAD_DIM, HEAD_DIM), HEAD_DIM)
                keys, values = key[rows, :], value[rows, :]
                delta_all = jnp.sum(grad_attended[rows, :].astype(F32) * attended[rows, :].astype(F32), 0, keepdims=True)
                key_grads = [0.0] * len(blocks)
                value_grads = [0.0] * len(blocks)
                at_query, at_key, at_value = (
                    pl.ds(pl.multiple_of(part * GROUP + local * HEAD_DIM, HEAD_DIM), HEAD_DIM) for part in range(3)
                )
                for start, stop in blocks:
                    queries, incoming = query[rows, start:stop], grad_attended[rows, start:stop]
                    total = log_total[head, :, start:stop]
                    delta = delta_all[:, start:stop]
                    query_grad = 0.0
                    for first, last, scores in score_parts(keys, queries, start, stop, length):
                        prob = jnp.exp2(scores - total)
                        grad_prob = dot_tn(values[:, first:last], incoming)
                        grad_score = (prob * (grad_prob - delta)).astype(LOW)
                        query_grad += dot_nn(keys[:, first:last], grad_score)
                        key_grad = dot_nt(queries, grad_score)
                        value_grad = dot_nt(incoming, prob.astype(LOW))
                        for piece, (low, high) in enumerate(blocks):
                            if first <= low and high <= last:
                                key_grads[piece] += key_grad[:, low - first : high - first]
                                value_grads[piece] += value_grad[:, low - first : high - first]
                    grads[at_query, start:stop] = (
                        rope(query_grad, cos[:, start:stop], -sin[:, start:stop]) * SCALE
                    ).astype(LOW)
                for (start, stop), key_grad, value_grad in zip(blocks, key_grads, value_grads):
                    grads[at_key, start:stop] = (
                        rope(key_grad, cos[:, start:stop], -sin[:, start:stop]) * (1.0 / LOG2E)
                    ).astype(LOW)
                    grads[at_value, start:stop] = value_grad.astype(LOW)
            return 0

        lax.fori_loop(0, PAIRS, pair, 0)
        turned = grads[...].T
        columns = pl.ds(pl.multiple_of(number * 3 * GROUP, GROUP), 3 * GROUP)
        for at in range(0, width, GROUP):
            rows = slice(at, at + GROUP)
            grad = dot_nn(normed_t[rows, :], turned)
            if follows:
                grad += g_weights[rows, columns].astype(F32)
            g_weights[rows, columns] = grad.astype(LOW)
        for at in range(0, seq, seq // 2):
            rows = slice(at, at + seq // 2)
            total = back[rows, :]
            for part in range(3):
                source = pl.ds(pl.multiple_of(part * width + number * GROUP, GROUP), GROUP)
                total += dot_nn(turned[rows, part * GROUP : (part + 1) * GROUP], weights[source, :])
            back[rows, :] = total
        return 0

    lax.fori_loop(0, width // GROUP, group, 0)
    heads_done()
    norm_sum = jnp.zeros((1, width), F32)
    for at in range(0, seq, tile):
        rows = slice(at, at + tile)
        inputs, incoming = x[rows, :].astype(F32), back[rows, :]
        inv = norm_rows(inputs)
        scaled = inputs * inv
        norm_sum += jnp.sum(incoming * scaled, 0, keepdims=True)
        weighted = incoming * gain
        grad = grad_resid[rows, :].astype(F32) + inv * (
            weighted - scaled * jnp.mean(weighted * scaled, -1, keepdims=True)
        )
        grad_resid[rows, :] = grad.astype(LOW)
    g_norm[...] = g_norm[...] + norm_sum if follows else norm_sum


class Links:
    def __init__(self, bands, axis, send, receive):
        self.send, self.receive, self.bands = send, receive, bands
        self.band, self.items = lax.axis_index("band"), lax.axis_index("items")
        self.item_bits, self.item_partners = bits_of(self.items, axis) if axis else ((), ())
        self.band_bits, self.band_partners = bits_of(self.band, bands)
        self.count = 0

    def take(self, count):
        first = self.count
        self.count += count
        return first

    def other(self, shift):
        return lax.rem(self.band + shift + self.bands, self.bands)

    def greet(self):
        barrier = pltpu.get_barrier_semaphore()
        others = [(self.items, self.other(shift)) for shift in range(1, self.bands)]
        others += [(partner, self.band) for partner in self.item_partners]
        for other in others:
            pl.semaphore_signal(barrier, inc=1, device_id=other, device_id_type=MESH)
        return lambda: pl.semaphore_wait(barrier, len(others))

    def copy(self, number, source, target, device):
        return pltpu.make_async_remote_copy(
            src_ref=source,
            dst_ref=target,
            send_sem=self.send.at[number],
            recv_sem=self.receive.at[number],
            device_id=device,
            device_id_type=MESH,
        )


class Exchange:
    def __init__(self, links, source, target, arrival):
        self.links, self.first = links, links.take(links.bands - 1)
        self.source, self.target, self.arrival = source, target, arrival

    def each(self, place):
        for shift in range(1, self.links.bands):
            yield self.links.copy(
                self.first + shift - 1, self.source(shift), place(shift), (self.links.items, self.links.other(shift))
            )

    def start(self):
        for copy in self.each(self.target):
            copy.start()

    def arrived(self):
        for copy in self.each(self.arrival):
            copy.wait_recv()

    def left(self):
        for copy in self.each(self.target):
            copy.wait_send()


def bits_of(number, size):
    bits = [lax.rem(lax.div(number, 2**at), 2) for at in range(log2_of(size))]
    return bits, [number + (1 - 2 * bit) * 2**at for at, bit in enumerate(bits)]


def sum_lanes(axis, stage, columns):
    left = list(range(log2_of(axis)))
    right = [0] + left[:0:-1]
    half = columns // 2
    if stage == 0:
        return [(left[0], left[1:], 0, columns)]
    return [(left[stage], left[stage + 1 :], 0, half), (right[stage], right[stage + 1 :], half, half)]


def band_shape(axis, bands, shape):
    rows = shape[0] // axis // bands
    return (rows, shape[1]) if rows % 16 == 0 else (2 * rows, shape[1] // 2)


def sum_scratch(axis, bands, shape):
    low = lambda *dims: pltpu.VMEM(dims, LOW)
    out = []
    for stage in range(log2_of(axis)):
        for _, bits, _, columns in sum_lanes(axis, stage, shape[1]):
            out.append(low(*(2,) * len(bits), shape[0] // axis, columns))
    part = band_shape(axis, bands, shape)
    out.append(low(*(2,) * log2_of(bands), *part))
    for stage in range(log2_of(bands)):
        out.append(low(*(2,) * (log2_of(bands) - stage - 1), *part))
    return out


def sum_links(axis, bands):
    return 2 * log2_of(axis) + log2_of(bands)


class Summing:
    def __init__(self, links, axis, array, first, columns, scratch, finish):
        self.links, self.array, self.finish = links, array, finish
        self.first, self.columns, self.scratch = first, columns, scratch
        self.axis, self.count = axis, log2_of(axis)
        self.stages = self.count + log2_of(links.bands)
        self.base = links.take(sum_links(axis, links.bands))
        self.state = 0

    def flights(self, stage):
        links = self.links
        if stage < self.count:
            rows, wide = self.array.shape
            view = self.array.reshape(*(2,) * self.count, rows // self.axis, wide)
            bits, partners, used = links.item_bits, links.item_partners, [0] if stage == 0 else [2 * stage - 1, 2 * stage]
            lanes = sum_lanes(self.axis, stage, self.columns)
            first = self.first
        else:
            view, first = self.scratch[2 * self.count - 1], 0
            bits, partners, used = links.band_bits, links.band_partners, [self.count + stage]
            at = stage - self.count
            lanes = [(at, list(range(at + 1, len(bits))), 0, view.shape[-1])]
        out = []
        for (now, later, start, columns), number in zip(lanes, used):
            place = lambda own: tuple(
                slice(None) if at in later else 1 - bits[at] if at == now and not own else bits[at]
                for at in reversed(range(len(bits)))
            ) + (slice(None), pl.ds(first + start, columns))
            partner = partners[now]
            device = (partner, links.band) if stage < self.count else (links.items, partner)
            came = self.scratch[number]
            out.append((links.copy(self.base + number, view.at[place(False)], came, device), view.at[place(True)], came))
        return out

    def begin(self, stage):
        for copy, _, _ in self.flights(stage):
            copy.start()

    def end(self, stage):
        flights = self.flights(stage)
        for copy, _, _ in flights:
            copy.wait_recv()
        for _, kept, came in flights:
            if stage == self.stages - 1:
                self.finish(kept[...].astype(F32) + came[...].astype(F32))
                continue
            rows = came.shape[-2]
            tile = 48 if rows % 48 == 0 else 32 if rows % 32 == 0 else 16
            for choice in np.ndindex(*came.shape[:-2]):

                def add(step, _, kept=kept, came=came, choice=choice):
                    span = choice + (pl.ds(pl.multiple_of(step * tile, tile), tile), slice(None))
                    kept[span] = (kept[span].astype(F32) + came[span].astype(F32)).astype(LOW)
                    return 0

                lax.fori_loop(0, rows // tile, add, 0)
        if stage == self.count - 1:
            self.stack()

    def stack(self):
        bands, parts = self.links.bands, self.scratch[2 * self.count - 1]
        rows = self.array.shape[0] // self.axis
        start = pl.multiple_of(self.links.items * rows, rows)
        whole = self.array.at[pl.ds(start, rows), pl.ds(self.first, self.columns)]
        rows = rows // bands
        spans = [slice(number * rows, (number + 1) * rows) for number in range(bands)]
        places = list(np.ndindex(*parts.shape[:-2]))
        if parts.shape[-2] == rows:
            for place, span in zip(places, spans):
                parts[place] = whole[span, :]
            return
        half = self.columns // 2
        left, right = whole[:, :half].astype(F32), whole[:, half:].astype(F32)
        for place, span in zip(places, spans):
            parts[place] = jnp.concatenate([left[span], right[span]], 0).astype(LOW)

    def advance(self):
        if self.state > self.stages:
            return
        if self.state > 0:
            self.end(self.state - 1)
        if self.state < self.stages:
            self.begin(self.state)
        self.state += 1

    def close(self):
        for stage in range(self.stages):
            for copy, _, _ in self.flights(stage):
                copy.wait_send()


def block_kernel(bands, per, axis, *refs):
    fused = axis > 0
    lengths, norm_attn, norm_ffn, cos, sin = refs[:5]
    tokens, cotangent, w_query, w_key, w_value, w_out_from, w_gate, w_up, w_down_from = refs[5:14]
    refs = refs[14:]
    home_out, home_grad = refs[:2]
    query_far, key_far, value_far, attended_t_far, grad_attended_t_far, cot_far = refs[2:8]
    refs = refs[8:]
    sums, refs = (refs[:9], refs[9:]) if fused else (refs[:5], refs[5:])
    weights_t, w_out, w_feed, w_down, g_feed, g_down, g_out = refs[:7]
    x, cot, attended, attended_t, query, key, value, grad_attended_t = refs[7:15]
    normed, normed_t, resid, out_acc, back_acc, log_total, g_norm, g_norm_ffn = refs[15:23]
    w_own, w_total, local, send, receive = refs[23:28]
    sum_refs = refs[28:]
    seq, width = x.shape[1:]
    ff = w_down.shape[0]
    band_rows, items = seq // bands, bands * per
    groups = width // GROUP
    links = Links(bands, axis, send, receive)
    band = links.band
    gain_attn, gain_ffn = norm_attn[...][None, :], norm_ffn[...][None, :]
    started = [0]

    def bring(source, target):
        copy = pltpu.make_async_copy(source, target, local.at[started[0]])
        started[0] += 1
        copy.start()
        return copy

    token_rows = band_rows * items
    raw = g_down.at[pl.ds(0, token_rows)]
    load_tokens = bring(tokens, raw)
    qkv = (g_feed.at[:, pl.ds(0, width)], g_feed.at[:, pl.ds(width, width)], g_feed.at[:, pl.ds(2 * width, width)])
    load_qkv = [bring(source, target) for source, target in zip((w_query, w_key, w_value), qkv)]
    all_here = links.greet()

    def own_rows(shift):
        return pl.ds(pl.multiple_of(links.other(shift) * band_rows, band_rows), band_rows)

    chunk = 32 if band_rows % 32 == 0 else 16
    size = items * chunk
    order = split_order(items, chunk, band * per)
    token_send = [attended.at[item] for item in range(per)]
    stages = [normed, resid]
    cot_send = [g_out.at[:, pl.ds(0, width)]] + [cot_far.at[item] for item in range(per - 1)]

    def split(kept, sent):
        for block in range(band_rows // chunk):
            moved = dot_nn(order, raw[block * size : (block + 1) * size, :]).astype(LOW)
            rows = pl.ds(pl.multiple_of(band * band_rows + block * chunk, 16), chunk)
            for at in range(items):
                part = moved[at * chunk : (at + 1) * chunk]
                shift, item = at // per, at % per
                if shift == 0:
                    kept[item, rows, :] = part
                else:
                    place = (shift - 1) * band_rows + block * chunk
                    sent[item][place : place + chunk, :] = part

    def scattering(sent, kept, item):
        return Exchange(
            links,
            lambda shift: sent[item].at[pl.ds((shift - 1) * band_rows, band_rows)],
            lambda shift: kept.at[item, own_rows(0)],
            lambda shift: kept.at[item, own_rows(-shift)],
        )

    def returning(source, home, item):
        slot = lambda shift: home.at[shift * per + item]
        return Exchange(links, lambda shift: source.at[item, own_rows(shift)], slot, slot)

    token_links = [scattering(token_send, x, item) for item in range(per)]
    cot_links = [scattering(cot_send, cot, item) for item in range(per)]
    out_links = [returning(attended, home_out, item) for item in range(per)]
    grad_links = [returning(cot, home_grad, item) for item in range(per)]

    load_tokens.wait()
    split(x, token_send)
    all_here()
    token_links[0].start()
    load_cot = bring(cotangent, raw)
    load_rest = [
        bring(w_out_from, w_out),
        bring(w_gate, w_feed.at[:, pl.ds(0, ff)]),
        bring(w_up, w_feed.at[:, pl.ds(ff, ff)]),
        bring(w_down_from, w_down),
    ]
    for part in range(3):
        load_qkv[part].wait()
        for at in range(0, width, 256):
            weights_t[part * width + at : part * width + at + 256, :] = qkv[part][:, at : at + 256].T
        if fused:
            own = w_own.shape[0]
            device = links.items * bands + band
            if part == 0:
                halves_of = axis * bands // 2
                column = jnp.concatenate([gain_attn, jnp.zeros((LANES - 1, width), F32)], 0).T
                out_acc[: width // 2, :LANES] = column[: width // 2]
                out_acc[: width // 2, LANES : 2 * LANES] = column[width // 2 :]
                at = pl.multiple_of(lax.rem(device, halves_of) * own, 8)
                both = out_acc[pl.ds(at, own), : 2 * LANES]
                own_gain = 1.0 / jnp.where(device < halves_of, both[:, :1], both[:, LANES : LANES + 1])
            both = qkv[part][pl.ds(pl.multiple_of(lax.div(device, 2) * (2 * own), 16), 2 * own), :].astype(F32)
            mine = jnp.where(lax.rem(device, 2) == 0, both[:own], both[own:]) * own_gain
            for number in range(groups):
                at = (number * 3 + part) * GROUP
                w_own[:, at : at + GROUP] = mine[:, number * GROUP : (number + 1) * GROUP]
    load_cot.wait()
    split(cot, cot_send[:1] + stages[: per - 1])
    late = pl.ds(0, (bands - 1) * band_rows)
    to_far = [bring(stages[item].at[late], cot_far.at[item]) for item in range(per - 1)]

    sums_of = {}
    schedule = {}
    if fused:
        scratch_each = len(sum_scratch(axis, bands, (axis * bands * 16, 256)))
        taken = [0]
        o_gate, o_up, o_down, o_out, o_query, o_key, o_value, o_norm_ffn, o_norm_attn = sums
        w_total[...] = jnp.zeros_like(w_total)

        def summing(name, array, first, columns, finish):
            sums_of[name] = Summing(
                links, axis, array, first, columns, sum_refs[taken[0] : taken[0] + scratch_each], finish
            )
            taken[0] += scratch_each

        def halves(total):
            rows = total.shape[0] // 2
            return total[:rows], total[rows:]

        for step in range(ff // WIDE):

            def finish_feed(total, step=step):
                span = slice(step * WIDE, (step + 1) * WIDE)
                o_gate[:, span], o_up[:, span] = halves(total)

            summing(("feed", step), g_feed, step * 2 * WIDE, 2 * WIDE, finish_feed)

        def finish_down(total):
            o_down[...] = total

        def finish_out(total):
            left, right = halves(total)
            half = left.shape[1]
            o_out[:, :half] = left
            o_out[:, half:] = right[:, : width - half]
            o_norm_ffn[...] = right[:, width - half : width - half + LANES].T[:1, :]

        summing("down", g_down, 0, width, finish_down)
        summing("out", g_out, 0, width + 2 * LANES, finish_out)
        for number in range(groups):

            def finish_group(total, number=number):
                left, right = halves(total)
                at, half = number * GROUP, GROUP // 2
                own = w_own[:, 3 * at : 3 * at + 3 * GROUP]
                middle = left.shape[1]
                w_total[...] += jnp.sum(left * own[:, :middle] + right * own[:, middle:], -1, keepdims=True)
                o_query[:, at : at + GROUP] = left[:, :GROUP]
                o_key[:, at : at + half] = left[:, GROUP:]
                o_key[:, at + half : at + GROUP] = right[:, :half]
                o_value[:, at : at + GROUP] = right[:, half:]

            summing(("back", number), w_feed, number * 3 * GROUP, 3 * GROUP, finish_group)

    def advance(*names):
        for name in names:
            sums_of[name].advance()

    spills = []

    def spill(pairs):
        spills.extend(bring(source, target) for source, target in pairs)

    def settle():
        while spills:
            spills.pop().wait()

    g_weights = w_feed
    grads = w_feed.at[pl.ds(0, 3 * GROUP), pl.ds(3 * width, seq)]
    for item in range(per):
        last = item == per - 1
        if item == 0:
            token_links[0].arrived()
            cot_links[0].start()
            for copy in to_far:
                copy.wait()
        settle()

        def projected(item=item):
            token_links[item].left()
            if item < per - 1:
                spill(
                    (source, target.at[item])
                    for source, target in ((query, query_far), (key, key_far), (value, value_far))
                )

        attend_item(
            lengths[band * per + item], x.at[item], weights_t, gain_attn, cos, sin, query, key, value, attended_t,
            attended.at[item], log_total.at[item], normed, projected,
        )
        if item == 0:
            for load in load_rest:
                load.wait()
        cot_links[item].arrived()
        if not last:
            token_links[item + 1].start()
        elif per > 1:
            out_links[item - 1].start()

        def feed_tick(step, item=item, last=last):
            if not last:

                @pl.when(step == ff // WIDE - 1)
                def _():
                    token_links[item + 1].arrived()
                    cot_links[item + 1].start()

            elif fused:
                for at in range(1, ff // WIDE):

                    @pl.when(step == at)
                    def _(at=at):
                        advance(*[("feed", number) for number in range(at)])

        cot_links[item].left()
        feed_item(
            item > 0, x.at[item], attended.at[item], attended_t, cot.at[item], w_out, w_feed, w_down, gain_ffn,
            g_feed, g_down, g_out, g_norm_ffn, attended.at[item], grad_attended_t,
            (normed, normed_t, resid, out_acc, back_acc), feed_tick,
        )
        if not last:
            spill(
                (source, target.at[item])
                for source, target in ((attended_t, attended_t_far), (grad_attended_t, grad_attended_t_far))
            )
    feeds = [("feed", step) for step in range(ff // WIDE)]
    backs = [("back", number) for number in range(groups)]
    if fused:
        column = jnp.concatenate([g_norm_ffn[...], jnp.zeros((LANES - 1, width), F32)], 0).T
        g_out[:, width : width + LANES] = column.astype(LOW)
        g_out[:, width + LANES :] = jnp.zeros((width, LANES), LOW)
        advance(*feeds, "down", "out")
    out_links[per - 1].start()
    turns = list(reversed(range(per)))
    reloads = []
    for turn, item in enumerate(turns):
        last = turn == per - 1

        def back_tick(at, turn=turn, last=last):
            if not fused:
                return
            for place, names in plan(turn, last).items():

                @pl.when(at == place)
                def _(names=names):
                    advance(*names)

        def plan(turn, last):
            out = {place: [] for place in range(groups * PAIRS)}
            if turn == 0:
                out[1] = feeds[1:]
                out[3] = feeds[2:] + ["down", "out"]
                out[5] = feeds[3:]
            if turn == 1:
                out[2] = feeds + ["down", "out"]
                out[4] = ["down", "out"]
            if last:
                for number in range(groups - 1):
                    for place in range((number + 1) * PAIRS, groups * PAIRS):
                        out[place].append(backs[number])
            return {place: names for place, names in out.items() if names}

        def heads_done(turn=turn, last=last):
            if not last:
                following = turns[turn + 1]
                for source, target in (
                    (query_far, query), (key_far, key), (value_far, value), (attended_t_far, attended_t),
                    (grad_attended_t_far, grad_attended_t),
                ):
                    reloads.append(bring(source.at[following], target))
            elif fused:
                advance(*backs[1:])

        back_item(
            turn > 0, lengths[band * per + item], x.at[item], cot.at[item], grad_attended_t, attended_t, query, key,
            value, log_total.at[item], weights_t, gain_attn, cos, sin, g_weights, g_norm, grads, normed_t, back_acc,
            back_tick, heads_done,
        )
        grad_links[item].start()
        while reloads:
            reloads.pop().wait()
    own = []
    for item in range(per):
        own.append(bring(attended.at[item, own_rows(0)], home_out.at[item]))
        own.append(bring(cot.at[item, own_rows(0)], home_grad.at[item]))
    if fused:
        every = feeds + ["down", "out"] + backs
        first, *_, last = backs
        for names in ([last] + backs[1:-1], [last], ["down", "out", first], [last], backs[1:-1], [last]):
            advance(*names)
        while any(sums_of[name].state <= sums_of[name].stages for name in every):
            least = min(sums_of[name].state for name in every)
            advance(*[name for name in every if sums_of[name].state == least])
        o_norm_attn[...] = w_total[...].T[:1, :]
        for name in every:
            sums_of[name].close()
    else:
        own += [
            bring(source, target)
            for source, target in zip(
                (g_feed, g_down, g_out.at[:, pl.ds(0, width)], g_weights.at[:, pl.ds(0, 3 * width)]), sums[:4]
            )
        ]
        sums[4][0:1, :] = g_norm[...]
        sums[4][1:2, :] = g_norm_ffn[...]
    for copy in own:
        copy.wait()
    for item in range(per):
        for exchange in (out_links[item], grad_links[item]):
            exchange.arrived()
            exchange.left()


def block(bands, axis, lengths, tokens, cotangent, gains, tables, weights):
    band_rows, items, width = tokens.shape
    per, seq, ff = items // bands, bands * band_rows, weights[4].shape[1]
    fused = axis > 0
    low = lambda *shape: jax.ShapeDtypeStruct(shape, LOW)
    full = lambda *shape: jax.ShapeDtypeStruct(shape, F32)
    scratch = lambda *shape: pltpu.VMEM(shape, LOW)
    wide = lambda *shape: pltpu.VMEM(shape, F32)
    outside = pl.BlockSpec(memory_space=pl.ANY)
    inside = pl.BlockSpec(memory_space=pltpu.VMEM)
    out_shape = [low(items, band_rows, width)] * 2 + [low(max(per - 1, 1), width, seq)] * 5
    out_shape += [low(max(per - 1, 1), (bands - 1) * band_rows, width)]
    out_specs = [outside] * 8
    extra, links = [], 4 * per * (bands - 1)
    if fused:
        devices = axis * bands
        rows, ff_rows = width // devices, ff // devices
        out_shape += [full(rows, ff), full(rows, ff), full(ff_rows, width)] + [full(rows, width)] * 4 + [full(1, rows)] * 2
        out_specs += [inside] * 9
        shapes = [(width, 2 * WIDE)] * (ff // WIDE) + [(ff, width), (width, width + 2 * LANES)]
        shapes += [(width, 3 * GROUP)] * (width // GROUP)
        for shape in shapes:
            extra += sum_scratch(axis, bands, shape)
        links += len(shapes) * sum_links(axis, bands)
    else:
        out_shape += [low(width, 2 * ff), low(ff, width), low(width, width), low(width, 3 * width), full(2, width)]
        out_specs += [outside] * 4 + [inside]
    return pl.pallas_call(
        functools.partial(block_kernel, bands, per, axis),
        name="block",
        out_shape=out_shape,
        in_specs=[smem()] + [inside] * 4 + [outside] * 9,
        out_specs=out_specs,
        scratch_shapes=[
            scratch(3 * width, width), scratch(width, width), scratch(width, 2 * ff), scratch(ff, width),
            scratch(width, 2 * ff), scratch(ff, width), scratch(width, width + 2 * LANES),
            scratch(per, seq, width), scratch(per, seq, width), scratch(per, seq, width), scratch(width, seq),
            scratch(width, seq), scratch(width, seq), scratch(width, seq), scratch(width, seq),
            scratch(seq, width), scratch(width, seq), scratch(seq, width), wide(seq, width), wide(seq, width),
            wide(per, width // HEAD_DIM, 1, seq), wide(1, width), wide(1, width),
            wide(max(width // (max(axis, 1) * bands), 8), 3 * width), wide(max(width // (max(axis, 1) * bands), 8), LANES),
            pltpu.SemaphoreType.DMA((16 + 12 * per,)),
            pltpu.SemaphoreType.DMA((links,)),
            pltpu.SemaphoreType.DMA((links,)),
        ]
        + extra,
        compiler_params=pltpu.CompilerParams(vmem_limit_bytes=64 * 2**20 - 2**16, collective_id=0, has_side_effects=True),
    )(
        lengths, *gains, *tables, tokens.reshape(band_rows * items, width), cotangent.reshape(band_rows * items, width),
        *weights,
    )


def rope_tables(seq):
    frequency = np.exp(-np.log(ROPE_BASE) * (2.0 * np.arange(HALF) / HEAD_DIM))
    angles = frequency[:, None] * np.arange(seq)[None, :]
    return jnp.asarray(np.cos(angles), F32), jnp.asarray(np.sin(angles), F32)


def per_device(
    bands,
    axis,
    tokens,
    lengths,
    norm_attn,
    w_query,
    w_key,
    w_value,
    w_out,
    norm_ffn,
    w_gate,
    w_up,
    w_down,
    cotangent,
):
    band_rows, items, width = tokens.shape
    per = items // bands
    seq = bands * band_rows
    band = lax.axis_index("band")
    whole_tiles = width // axis % 16 == 0 and width // axis // bands % 16 == 8 and w_gate.shape[1] // axis // bands % 16 == 0
    fused = axis if whole_tiles else 0
    home_out, home_grad, *sums = block(
        bands, fused, lengths, tokens, cotangent, (norm_attn, norm_ffn), rope_tables(seq),
        (w_query, w_key, w_value, w_out, w_gate, w_up, w_down),
    )
    sums = sums[6:]
    output, grad_tokens = merge_items([home_out, home_grad], band, bands)
    if fused:
        g_gate, g_up, g_down, g_out, g_query, g_key, g_value, g_norm_ffn, g_norm_attn = sums
        g_norm_attn, g_norm_ffn = g_norm_attn.reshape(-1), g_norm_ffn.reshape(-1)
    else:
        axes = ("items", "band")
        total = lambda a: lax.psum_scatter(a, axes, scatter_dimension=0, tiled=True).astype(F32)
        g_feed, g_down, g_out, g_weights = (total(a) for a in sums[:4])
        norms = total(sums[4].T)
        g_norm_attn, g_norm_ffn = norms[:, 0], norms[:, 1]
        g_gate, g_up = jnp.moveaxis(g_feed.reshape(-1, w_gate.shape[1] // WIDE, 2, WIDE), 2, 0).reshape(2, -1, w_gate.shape[1])
        g_query, g_key, g_value = jnp.moveaxis(g_weights.reshape(-1, width // GROUP, 3, GROUP), 2, 0).reshape(3, -1, width)
    return (
        output,
        grad_tokens,
        g_norm_attn,
        g_query,
        g_key,
        g_value,
        g_out,
        g_norm_ffn,
        g_gate,
        g_up,
        g_down,
    )


def solution(mesh):
    split = P("band", "items", None)
    rows = P(("items", "band"), None)
    flat = P(("items", "band"))
    return jax.shard_map(
        functools.partial(per_device, mesh.shape["band"], mesh.shape["items"]),
        mesh=mesh,
        in_specs=(split, P("items")) + (P(),) * 9 + (split,),
        out_specs=(split, split, flat, rows, rows, rows, rows, flat, rows, rows, rows),
        check_vma=False,
    )
```

```python
import functools

import jax
import jax.numpy as jnp
import numpy as np
from jax import lax
from jax.experimental import pallas as pl
from jax.experimental.pallas import tpu as pltpu
from jax.sharding import PartitionSpec as P

HEAD_DIM = 64
HALF = HEAD_DIM // 2
EPS = 1e-05
NEG = -1e30
ROPE_BASE = 10000.0
LOG2E = 1.4426950408889634
SCALE = HEAD_DIM**-0.5
BLOCK = 256
F32 = jnp.float32
LOW = jnp.bfloat16
MESH = pl.DeviceIdType.MESH


def dot_nn(left, right):
    return lax.dot_general(left, right, (((1,), (0,)), ((), ())), preferred_element_type=F32)


def dot_nt(left, right):
    return lax.dot_general(left, right, (((1,), (1,)), ((), ())), preferred_element_type=F32)


def dot_tn(left, right):
    return lax.dot_general(left, right, (((0,), (0,)), ((), ())), preferred_element_type=F32)


def vmem(count):
    return [pl.BlockSpec(memory_space=pltpu.VMEM)] * count


def smem():
    return pl.BlockSpec(memory_space=pltpu.SMEM)


def params(mib):
    return pltpu.CompilerParams(vmem_limit_bytes=mib * 2**20)


def log2_of(number):
    return number.bit_length() - 1


def split_order(items, chunk, first):
    size = items * chunk
    row = lax.broadcasted_iota(jnp.int32, (size, size), 0)
    col = lax.broadcasted_iota(jnp.int32, (size, size), 1)
    item = (row >> log2_of(chunk)) + first
    item = jnp.where(item >= items, item - items, item)
    return jnp.where(col == (row & (chunk - 1)) * items + item, 1.0, 0.0).astype(LOW)


def merge_kernel(per, chunk, passed, flat, band_ref, *refs):
    count = passed + flat + 2
    ins, outs, refs = refs[:count], refs[count : 2 * count], refs[2 * count :]
    held, made, sem, through = refs[:2], refs[2:4], refs[4], refs[5:]
    items, band_rows, width = ins[0].shape
    size, bands, blocks = items * chunk, items // per, band_rows // chunk
    started = []

    def bring(source, target):
        copy = pltpu.make_async_copy(source, target, sem.at[len(started)])
        started.append(copy)
        copy.start()
        return copy

    loads = [bring(ins[at], held[at]) for at in range(2)]
    passing = [bring(source, place) for source, place in zip(ins[2 : 2 + passed], through)]
    stores = []
    for at in range(2 + passed, count):
        outs[at][...] = ins[at][0, :]
    row = lax.broadcasted_iota(jnp.int32, (size, size), 0)
    col = lax.broadcasted_iota(jnp.int32, (size, size), 1)
    number = col >> log2_of(chunk)
    source = band_ref[0] - (number >> log2_of(per))
    source = jnp.where(source < 0, source + bands, source)
    item = source * per + (number & (per - 1))
    order = jnp.where(row == (col & (chunk - 1)) * items + item, 1.0, 0.0).astype(LOW)
    for at in range(2):
        loads[at].wait()
        for block in range(blocks):
            parts = held[at][:, block * chunk : (block + 1) * chunk, :].reshape(size, width)
            made[at][block * size : (block + 1) * size, :] = dot_nn(order, parts).astype(LOW)
        stores.append(bring(made[at], outs[at]))
        if at == 0:
            for copy, place, out in zip(passing, through, outs[2 : 2 + passed]):
                copy.wait()
                stores.append(bring(place, out))
    for store in stores:
        store.wait()


def merge_items(arrays, passed, flat, band, bands):
    items, band_rows, width = arrays[0].shape
    chunk = 32 if band_rows % 32 == 0 else 16
    outside = pl.BlockSpec(memory_space=pl.ANY)
    inside = pl.BlockSpec(memory_space=pltpu.VMEM)
    merged = pl.pallas_call(
        functools.partial(merge_kernel, items // bands, chunk, len(passed), len(flat)),
        name="merge_items",
        out_shape=[jax.ShapeDtypeStruct((band_rows * items, width), LOW)] * 2
        + [jax.ShapeDtypeStruct(array.shape, array.dtype) for array in passed]
        + [jax.ShapeDtypeStruct(array.shape[1:], array.dtype) for array in flat],
        in_specs=[smem()] + [outside] * (2 + len(passed)) + [inside] * len(flat),
        out_specs=[outside] * (2 + len(passed)) + [inside] * len(flat),
        scratch_shapes=[pltpu.VMEM((items, band_rows, width), LOW)] * 2
        + [pltpu.VMEM((band_rows * items, width), LOW)] * 2
        + [pltpu.SemaphoreType.DMA((4 * (band_rows // chunk) + 2 * len(passed),))]
        + [pltpu.VMEM(array.shape, array.dtype) for array in passed],
        compiler_params=params(60),
    )(jnp.reshape(band, (1,)), *arrays, *passed, *flat)
    return [array.reshape(band_rows, items, width) for array in merged[:2]], merged[2:]


def rope(vector, cos, sin):
    parts = []
    for at in range(0, vector.shape[0], HEAD_DIM):
        lower, upper = vector[at : at + HALF], vector[at + HALF : at + HEAD_DIM]
        parts += [lower * cos - upper * sin, lower * sin + upper * cos]
    return jnp.concatenate(parts, 0)


def query_blocks(seq):
    return [(start, min(start + BLOCK, seq)) for start in range(0, seq, BLOCK)]


def limits(start, stop, length):
    position = start + lax.broadcasted_iota(jnp.int32, (1, stop - start), 1)
    return jnp.minimum(position, length - 1)


def score_parts(keys, queries, start, stop, length):
    parts = []
    if start:
        parts.append((0, BLOCK, dot_tn(keys[:, :BLOCK], queries)))
    first = min(start, BLOCK)
    late = dot_tn(keys[:, first:stop], queries)
    position = first + lax.broadcasted_iota(jnp.int32, late.shape, 0)
    late = jnp.where(position <= limits(start, stop, length), late, NEG)
    parts.append((first, stop, late))
    return parts


def norm_rows(inputs):
    return lax.rsqrt(jnp.mean(inputs * inputs, -1, keepdims=True) + EPS)


def attend_item(length, x, weights, gain, cos, sin, query, key, value, attended_t, attended, log_total, normed, ready):
    seq, width = x.shape
    tile = 128
    for at in range(0, seq, tile):
        inputs = x[at : at + tile, :].astype(F32)
        normed[at : at + tile, :] = (inputs * norm_rows(inputs) * gain).astype(LOW)

    project = 256

    def project_tile(at, _):
        rows = pl.ds(pl.multiple_of(at * project, project), project)
        for part, out, scaled in ((0, query, SCALE * LOG2E), (1, key, 1.0)):
            source = pl.ds(pl.multiple_of(part * width + at * project, project), project)
            out[rows, :] = (rope(dot_nt(weights[source, :], normed[...]), cos[...], sin[...]) * scaled).astype(LOW)
        source = pl.ds(pl.multiple_of(2 * width + at * project, project), project)
        value[rows, :] = dot_nt(weights[source, :], normed[...]).astype(LOW)
        return 0

    lax.fori_loop(0, width // project, project_tile, 0)
    ready()

    def head(at, _):
        for which in range(2):
            number = at * 2 + which
            rows = pl.ds(pl.multiple_of(number * HEAD_DIM, HEAD_DIM), HEAD_DIM)
            keys, values = key[rows, :], value[rows, :]
            for start, stop in query_blocks(seq):
                parts = score_parts(keys, query[rows, start:stop], start, stop, length)
                top = functools.reduce(jnp.maximum, [jnp.max(s, 0, keepdims=True) for _, _, s in parts])
                total = jnp.zeros_like(top)
                acc = jnp.zeros((HEAD_DIM, stop - start), F32)
                for first, last, scores in parts:
                    prob = jnp.exp2(scores - top)
                    total += jnp.sum(prob, 0, keepdims=True)
                    acc += dot_nn(values[:, first:last], prob.astype(LOW))
                attended_t[rows, start:stop] = (acc / total).astype(LOW)
                log_total[number, :, start:stop] = top + jnp.log2(total)
        return 0

    lax.fori_loop(0, width // HEAD_DIM // 2, head, 0)
    for at in range(0, width, project):
        attended[:, at : at + project] = attended_t[at : at + project, :].T


LANES = 128
GROUP = 256
WIDE = 512


def feed_item(follows, x, attended, attended_t, cot, w_out, w_feed, w_down, gain, g_feed, g_down, g_out, g_norm, out, grad_attended_t, scratch, tick):
    normed, normed_t, resid, out_acc, back_acc = scratch
    seq, width = x.shape
    ff = w_down.shape[0]
    tile = 128

    def put(ref, at, grad):
        if follows:
            grad += ref[at].astype(F32)
        ref[at] = grad.astype(LOW)

    for at in range(0, seq, tile):
        rows = slice(at, at + tile)
        total = x[rows, :].astype(F32) + dot_nn(attended[rows, :], w_out[...])
        resid[rows, :] = total.astype(LOW)
        out_acc[rows, :] = total
        low = (total * norm_rows(total) * gain).astype(LOW)
        normed[rows, :] = low
        normed_t[:, rows] = low.T
    back_acc[...] = jnp.zeros_like(back_acc)

    def chunk(step, _):
        tick(step)
        span = pl.ds(pl.multiple_of(step * WIDE, WIDE), WIDE)
        up_span = pl.ds(pl.multiple_of(ff + step * WIDE, WIDE), WIDE)
        lows = []
        for at in range(0, seq, seq // 2):
            rows = slice(at, at + seq // 2)
            parts = []
            for first in range(0, WIDE, WIDE // 2):
                columns = pl.ds(pl.multiple_of(step * WIDE + first, WIDE // 2), WIDE // 2)
                up_columns = pl.ds(pl.multiple_of(ff + step * WIDE + first, WIDE // 2), WIDE // 2)
                gate = dot_nn(normed[rows, :], w_feed[:, columns])
                upward = dot_nn(normed[rows, :], w_feed[:, up_columns])
                grad_hidden = dot_nt(cot[rows, :], w_down[columns, :])
                sig = 0.5 * jnp.tanh(0.5 * gate) + 0.5
                silu = gate * sig
                hidden = (silu * upward).astype(LOW)
                grad_gate = (grad_hidden * upward * (sig + silu * (1.0 - sig))).astype(LOW)
                grad_upward = (grad_hidden * silu).astype(LOW)
                parts.append((hidden, grad_gate, grad_upward))
            hidden, grad_gate, grad_upward = (jnp.concatenate(both, 1) for both in zip(*parts))
            out_acc[rows, :] += dot_nn(hidden, w_down[span, :])
            back_acc[rows, :] += dot_nt(grad_gate, w_feed[:, span])
            back_acc[rows, :] += dot_nt(grad_upward, w_feed[:, up_span])
            lows.append((hidden, grad_gate, grad_upward))
        hidden, grad_gate, grad_upward = (jnp.concatenate(parts, 0) for parts in zip(*lows))
        half = WIDE // 2
        for at in range(0, WIDE, half):
            part = pl.ds(pl.multiple_of(step * WIDE + at, half), half)
            put(g_down, (part, slice(None)), dot_nn(hidden[:, at : at + half].T, cot[...]))
        first = pl.ds(pl.multiple_of(step * 2 * WIDE, WIDE), WIDE)
        second = pl.ds(pl.multiple_of(step * 2 * WIDE + WIDE, WIDE), WIDE)
        half = width // 2
        for at in range(0, width, half):
            part = slice(at, at + half)
            put(g_feed, (part, first), dot_nn(normed_t[part, :], grad_gate))
            put(g_feed, (part, second), dot_nn(normed_t[part, :], grad_upward))
        return 0

    lax.fori_loop(0, ff // WIDE, chunk, 0)
    norm_sum = jnp.zeros((1, width), F32)
    for at in range(0, seq, tile):
        rows = slice(at, at + tile)
        out[rows, :] = out_acc[rows, :].astype(LOW)
        total, incoming = resid[rows, :].astype(F32), back_acc[rows, :]
        inv = norm_rows(total)
        scaled = total * inv
        norm_sum += jnp.sum(incoming * scaled, 0, keepdims=True)
        weighted = incoming * gain
        grad = cot[rows, :].astype(F32) + inv * (weighted - scaled * jnp.mean(weighted * scaled, -1, keepdims=True))
        cot[rows, :] = grad.astype(LOW)
    g_norm[...] = g_norm[...] + norm_sum if follows else norm_sum
    for at in range(0, width, GROUP):
        rows = slice(at, at + GROUP)
        grad_attended_t[rows, :] = dot_nt(w_out[rows, :], cot[...]).astype(LOW)
    for at in range(0, width, GROUP):
        rows = slice(at, at + GROUP)
        put(g_out, (rows, slice(0, width)), dot_nn(attended_t[rows, :], cot[...]))


PAIRS = GROUP // (2 * HEAD_DIM)


def back_item(
    follows, length, x, grad_resid, grad_attended, attended, query, key, value, log_total, weights, gain, cos, sin,
    g_weights, g_norm, grads, normed_t, back, tick, heads_done,
):
    seq, width = x.shape
    blocks = query_blocks(seq)
    tile = 128
    for at in range(0, seq, tile):
        inputs = x[at : at + tile, :].astype(F32)
        normed_t[:, at : at + tile] = (inputs * norm_rows(inputs) * gain).astype(LOW).T
    back[...] = jnp.zeros_like(back)

    def group(number, _):
        def pair(at, _):
            tick(number * PAIRS + at)
            for which in range(2):
                local = at * 2 + which
                head = number * (2 * PAIRS) + local
                rows = pl.ds(pl.multiple_of(head * HEAD_DIM, HEAD_DIM), HEAD_DIM)
                keys, values = key[rows, :], value[rows, :]
                delta_all = jnp.sum(grad_attended[rows, :].astype(F32) * attended[rows, :].astype(F32), 0, keepdims=True)
                key_grads = [0.0] * len(blocks)
                value_grads = [0.0] * len(blocks)
                at_query, at_key, at_value = (
                    pl.ds(pl.multiple_of(part * GROUP + local * HEAD_DIM, HEAD_DIM), HEAD_DIM) for part in range(3)
                )
                for start, stop in blocks:
                    queries, incoming = query[rows, start:stop], grad_attended[rows, start:stop]
                    total = log_total[head, :, start:stop]
                    delta = delta_all[:, start:stop]
                    query_grad = 0.0
                    for first, last, scores in score_parts(keys, queries, start, stop, length):
                        prob = jnp.exp2(scores - total)
                        grad_prob = dot_tn(values[:, first:last], incoming)
                        grad_score = (prob * (grad_prob - delta)).astype(LOW)
                        query_grad += dot_nn(keys[:, first:last], grad_score)
                        key_grad = dot_nt(queries, grad_score)
                        value_grad = dot_nt(incoming, prob.astype(LOW))
                        for piece, (low, high) in enumerate(blocks):
                            if first <= low and high <= last:
                                key_grads[piece] += key_grad[:, low - first : high - first]
                                value_grads[piece] += value_grad[:, low - first : high - first]
                    grads[at_query, start:stop] = (
                        rope(query_grad, cos[:, start:stop], -sin[:, start:stop]) * SCALE
                    ).astype(LOW)
                for (start, stop), key_grad, value_grad in zip(blocks, key_grads, value_grads):
                    grads[at_key, start:stop] = (
                        rope(key_grad, cos[:, start:stop], -sin[:, start:stop]) * (1.0 / LOG2E)
                    ).astype(LOW)
                    grads[at_value, start:stop] = value_grad.astype(LOW)
            return 0

        lax.fori_loop(0, PAIRS, pair, 0)
        turned = grads[...].T
        columns = pl.ds(pl.multiple_of(number * 3 * GROUP, GROUP), 3 * GROUP)
        for at in range(0, width, GROUP):
            rows = slice(at, at + GROUP)
            grad = dot_nn(normed_t[rows, :], turned)
            if follows:
                grad += g_weights[rows, columns].astype(F32)
            g_weights[rows, columns] = grad.astype(LOW)
        for at in range(0, seq, seq // 2):
            rows = slice(at, at + seq // 2)
            total = back[rows, :]
            for part in range(3):
                source = pl.ds(pl.multiple_of(part * width + number * GROUP, GROUP), GROUP)
                total += dot_nn(turned[rows, part * GROUP : (part + 1) * GROUP], weights[source, :])
            back[rows, :] = total
        return 0

    lax.fori_loop(0, width // GROUP, group, 0)
    heads_done()
    norm_sum = jnp.zeros((1, width), F32)
    for at in range(0, seq, tile):
        rows = slice(at, at + tile)
        inputs, incoming = x[rows, :].astype(F32), back[rows, :]
        inv = norm_rows(inputs)
        scaled = inputs * inv
        norm_sum += jnp.sum(incoming * scaled, 0, keepdims=True)
        weighted = incoming * gain
        grad = grad_resid[rows, :].astype(F32) + inv * (
            weighted - scaled * jnp.mean(weighted * scaled, -1, keepdims=True)
        )
        grad_resid[rows, :] = grad.astype(LOW)
    g_norm[...] = g_norm[...] + norm_sum if follows else norm_sum


class Links:
    def __init__(self, bands, axis, send, receive):
        self.send, self.receive, self.bands = send, receive, bands
        self.band, self.items = lax.axis_index("band"), lax.axis_index("items")
        self.item_bits, self.item_partners = bits_of(self.items, axis) if axis else ((), ())
        self.band_bits, self.band_partners = bits_of(self.band, bands)
        self.count = 0

    def take(self, count):
        first = self.count
        self.count += count
        return first

    def other(self, shift):
        return lax.rem(self.band + shift + self.bands, self.bands)

    def greet(self):
        barrier = pltpu.get_barrier_semaphore()
        others = [(self.items, self.other(shift)) for shift in range(1, self.bands)]
        others += [(partner, self.band) for partner in self.item_partners]
        for other in others:
            pl.semaphore_signal(barrier, inc=1, device_id=other, device_id_type=MESH)
        return lambda: pl.semaphore_wait(barrier, len(others))

    def copy(self, number, source, target, device):
        return pltpu.make_async_remote_copy(
            src_ref=source,
            dst_ref=target,
            send_sem=self.send.at[number],
            recv_sem=self.receive.at[number],
            device_id=device,
            device_id_type=MESH,
        )


class Exchange:
    def __init__(self, links, source, target, arrival):
        self.links, self.first = links, links.take(links.bands - 1)
        self.source, self.target, self.arrival = source, target, arrival

    def each(self, place):
        for shift in range(1, self.links.bands):
            yield self.links.copy(
                self.first + shift - 1, self.source(shift), place(shift), (self.links.items, self.links.other(shift))
            )

    def start(self):
        for copy in self.each(self.target):
            copy.start()

    def arrived(self):
        for copy in self.each(self.arrival):
            copy.wait_recv()

    def left(self):
        for copy in self.each(self.target):
            copy.wait_send()


def bits_of(number, size):
    bits = [lax.rem(lax.div(number, 2**at), 2) for at in range(log2_of(size))]
    return bits, [number + (1 - 2 * bit) * 2**at for at, bit in enumerate(bits)]


def sum_lanes(axis, stage, columns):
    left = list(range(log2_of(axis)))
    right = [0] + left[:0:-1]
    half = columns // 2
    if stage == 0:
        return [(left[0], left[1:], 0, columns)]
    return [(left[stage], left[stage + 1 :], 0, half), (right[stage], right[stage + 1 :], half, half)]


def band_shape(axis, bands, shape):
    rows = shape[0] // axis // bands
    return (rows, shape[1]) if rows % 16 == 0 else (2 * rows, shape[1] // 2)


def sum_scratch(axis, bands, shape):
    low = lambda *dims: pltpu.VMEM(dims, LOW)
    out = []
    for stage in range(log2_of(axis)):
        for _, bits, _, columns in sum_lanes(axis, stage, shape[1]):
            out.append(low(*(2,) * len(bits), shape[0] // axis, columns))
    part = band_shape(axis, bands, shape)
    out.append(low(*(2,) * log2_of(bands), *part))
    for stage in range(log2_of(bands)):
        out.append(low(*(2,) * (log2_of(bands) - stage - 1), *part))
    return out


def sum_links(axis, bands):
    return 2 * log2_of(axis) + log2_of(bands)


class Summing:
    def __init__(self, links, axis, array, first, columns, scratch, finish):
        self.links, self.array, self.finish = links, array, finish
        self.first, self.columns, self.scratch = first, columns, scratch
        self.axis, self.count = axis, log2_of(axis)
        self.stages = self.count + log2_of(links.bands)
        self.base = links.take(sum_links(axis, links.bands))
        self.state = 0

    def flights(self, stage):
        links = self.links
        if stage < self.count:
            rows, wide = self.array.shape
            view = self.array.reshape(*(2,) * self.count, rows // self.axis, wide)
            bits, partners, used = links.item_bits, links.item_partners, [0] if stage == 0 else [2 * stage - 1, 2 * stage]
            lanes = sum_lanes(self.axis, stage, self.columns)
            first = self.first
        else:
            view, first = self.scratch[2 * self.count - 1], 0
            bits, partners, used = links.band_bits, links.band_partners, [self.count + stage]
            at = stage - self.count
            lanes = [(at, list(range(at + 1, len(bits))), 0, view.shape[-1])]
        out = []
        for (now, later, start, columns), number in zip(lanes, used):
            place = lambda own: tuple(
                slice(None) if at in later else 1 - bits[at] if at == now and not own else bits[at]
                for at in reversed(range(len(bits)))
            ) + (slice(None), pl.ds(first + start, columns))
            partner = partners[now]
            device = (partner, links.band) if stage < self.count else (links.items, partner)
            came = self.scratch[number]
            out.append((links.copy(self.base + number, view.at[place(False)], came, device), view.at[place(True)], came))
        return out

    def begin(self, stage):
        for copy, _, _ in self.flights(stage):
            copy.start()

    def end(self, stage):
        flights = self.flights(stage)
        for copy, _, _ in flights:
            copy.wait_recv()
        for _, kept, came in flights:
            if stage == self.stages - 1:
                self.finish(kept[...].astype(F32) + came[...].astype(F32))
                continue
            rows = came.shape[-2]
            tile = 48 if rows % 48 == 0 else 32 if rows % 32 == 0 else 16
            for choice in np.ndindex(*came.shape[:-2]):

                def add(step, _, kept=kept, came=came, choice=choice):
                    span = choice + (pl.ds(pl.multiple_of(step * tile, tile), tile), slice(None))
                    kept[span] = (kept[span].astype(F32) + came[span].astype(F32)).astype(LOW)
                    return 0

                lax.fori_loop(0, rows // tile, add, 0)
        if stage == self.count - 1:
            self.stack()

    def stack(self):
        bands, parts = self.links.bands, self.scratch[2 * self.count - 1]
        rows = self.array.shape[0] // self.axis
        start = pl.multiple_of(self.links.items * rows, rows)
        whole = self.array.at[pl.ds(start, rows), pl.ds(self.first, self.columns)]
        rows = rows // bands
        spans = [slice(number * rows, (number + 1) * rows) for number in range(bands)]
        places = list(np.ndindex(*parts.shape[:-2]))
        if parts.shape[-2] == rows:
            for place, span in zip(places, spans):
                parts[place] = whole[span, :]
            return
        half = self.columns // 2
        left, right = whole[:, :half].astype(F32), whole[:, half:].astype(F32)
        for place, span in zip(places, spans):
            parts[place] = jnp.concatenate([left[span], right[span]], 0).astype(LOW)

    def advance(self):
        if self.state > self.stages:
            return
        if self.state > 0:
            self.end(self.state - 1)
        if self.state < self.stages:
            self.begin(self.state)
        self.state += 1

    def close(self):
        for stage in range(self.stages):
            for copy, _, _ in self.flights(stage):
                copy.wait_send()


def block_kernel(bands, per, axis, *refs):
    fused = axis > 0
    lengths, norm_attn, norm_ffn, cos, sin = refs[:5]
    tokens, cotangent, w_query, w_key, w_value, w_out_from, w_gate, w_up, w_down_from = refs[5:14]
    refs = refs[14:]
    home_out, home_grad = refs[:2]
    query_far, key_far, value_far, attended_t_far, grad_attended_t_far, cot_far = refs[2:8]
    refs = refs[8:]
    sums, refs = (refs[:9], refs[9:]) if fused else (refs[:6], refs[6:])
    weights_t, w_out, w_feed, w_down, g_feed, g_down, g_out = refs[:7]
    x, cot, attended, attended_t, query, key, value, grad_attended_t = refs[7:15]
    normed, normed_t, resid, out_acc, back_acc, log_total, g_norm, g_norm_ffn = refs[15:23]
    w_own, w_total, local, send, receive = refs[23:28]
    sum_refs = refs[28:]
    seq, width = x.shape[1:]
    ff = w_down.shape[0]
    band_rows, items = seq // bands, bands * per
    groups = width // GROUP
    links = Links(bands, axis, send, receive)
    band = links.band
    gain_attn, gain_ffn = norm_attn[...][None, :], norm_ffn[...][None, :]
    started = [0]

    def bring(source, target):
        copy = pltpu.make_async_copy(source, target, local.at[started[0]])
        started[0] += 1
        copy.start()
        return copy

    token_rows = band_rows * items
    raw = g_down.at[pl.ds(0, token_rows)]
    load_tokens = bring(tokens, raw)
    qkv = (g_feed.at[:, pl.ds(0, width)], g_feed.at[:, pl.ds(width, width)], g_feed.at[:, pl.ds(2 * width, width)])
    load_qkv = [bring(source, target) for source, target in zip((w_query, w_key, w_value), qkv)]
    all_here = links.greet()

    def own_rows(shift):
        return pl.ds(pl.multiple_of(links.other(shift) * band_rows, band_rows), band_rows)

    chunk = 32 if band_rows % 32 == 0 else 16
    size = items * chunk
    order = split_order(items, chunk, band * per)
    token_send = [attended.at[item] for item in range(per)]
    stages = [normed, resid]
    cot_send = [g_out.at[:, pl.ds(0, width)]] + [cot_far.at[item] for item in range(per - 1)]

    def split(kept, sent):
        for block in range(band_rows // chunk):
            moved = dot_nn(order, raw[block * size : (block + 1) * size, :]).astype(LOW)
            rows = pl.ds(pl.multiple_of(band * band_rows + block * chunk, 16), chunk)
            for at in range(items):
                part = moved[at * chunk : (at + 1) * chunk]
                shift, item = at // per, at % per
                if shift == 0:
                    kept[item, rows, :] = part
                else:
                    place = (shift - 1) * band_rows + block * chunk
                    sent[item][place : place + chunk, :] = part

    def scattering(sent, kept, item):
        return Exchange(
            links,
            lambda shift: sent[item].at[pl.ds((shift - 1) * band_rows, band_rows)],
            lambda shift: kept.at[item, own_rows(0)],
            lambda shift: kept.at[item, own_rows(-shift)],
        )

    def returning(source, home, item):
        slot = lambda shift: home.at[shift * per + item]
        return Exchange(links, lambda shift: source.at[item, own_rows(shift)], slot, slot)

    token_links = [scattering(token_send, x, item) for item in range(per)]
    cot_links = [scattering(cot_send, cot, item) for item in range(per)]
    out_links = [returning(attended, home_out, item) for item in range(per)]
    grad_links = [returning(cot, home_grad, item) for item in range(per)]

    load_tokens.wait()
    split(x, token_send)
    all_here()
    token_links[0].start()
    load_cot = bring(cotangent, raw)
    load_rest = [
        bring(w_out_from, w_out),
        bring(w_gate, w_feed.at[:, pl.ds(0, ff)]),
        bring(w_up, w_feed.at[:, pl.ds(ff, ff)]),
        bring(w_down_from, w_down),
    ]
    for part in range(3):
        load_qkv[part].wait()
        for at in range(0, width, 256):
            weights_t[part * width + at : part * width + at + 256, :] = qkv[part][:, at : at + 256].T
        if fused:
            own = w_own.shape[0]
            device = links.items * bands + band
            if part == 0:
                halves_of = axis * bands // 2
                column = jnp.concatenate([gain_attn, jnp.zeros((LANES - 1, width), F32)], 0).T
                out_acc[: width // 2, :LANES] = column[: width // 2]
                out_acc[: width // 2, LANES : 2 * LANES] = column[width // 2 :]
                at = pl.multiple_of(lax.rem(device, halves_of) * own, 8)
                both = out_acc[pl.ds(at, own), : 2 * LANES]
                own_gain = 1.0 / jnp.where(device < halves_of, both[:, :1], both[:, LANES : LANES + 1])
            both = qkv[part][pl.ds(pl.multiple_of(lax.div(device, 2) * (2 * own), 16), 2 * own), :].astype(F32)
            mine = jnp.where(lax.rem(device, 2) == 0, both[:own], both[own:]) * own_gain
            for number in range(groups):
                at = (number * 3 + part) * GROUP
                w_own[:, at : at + GROUP] = mine[:, number * GROUP : (number + 1) * GROUP]
    load_cot.wait()
    split(cot, cot_send[:1] + stages[: per - 1])
    late = pl.ds(0, (bands - 1) * band_rows)
    to_far = [bring(stages[item].at[late], cot_far.at[item]) for item in range(per - 1)]

    sums_of = {}
    schedule = {}
    if fused:
        scratch_each = len(sum_scratch(axis, bands, (axis * bands * 16, 256)))
        taken = [0]
        o_gate, o_up, o_down, o_out, o_query, o_key, o_value, o_norm_ffn, o_norm_attn = sums
        w_total[...] = jnp.zeros_like(w_total)

        def summing(name, array, first, columns, finish):
            sums_of[name] = Summing(
                links, axis, array, first, columns, sum_refs[taken[0] : taken[0] + scratch_each], finish
            )
            taken[0] += scratch_each

        def halves(total):
            rows = total.shape[0] // 2
            return total[:rows], total[rows:]

        for step in range(ff // WIDE):

            def finish_feed(total, step=step):
                span = slice(step * WIDE, (step + 1) * WIDE)
                o_gate[:, span], o_up[:, span] = halves(total)

            summing(("feed", step), g_feed, step * 2 * WIDE, 2 * WIDE, finish_feed)

        def finish_down(total):
            o_down[...] = total

        def finish_out(total):
            left, right = halves(total)
            half = left.shape[1]
            o_out[:, :half] = left
            o_out[:, half:] = right[:, : width - half]
            o_norm_ffn[...] = right[:, width - half : width - half + LANES].T[:1, :]

        summing("down", g_down, 0, width, finish_down)
        summing("out", g_out, 0, width + 2 * LANES, finish_out)
        for number in range(groups):

            def finish_group(total, number=number):
                left, right = halves(total)
                at, half = number * GROUP, GROUP // 2
                own = w_own[:, 3 * at : 3 * at + 3 * GROUP]
                middle = left.shape[1]
                w_total[...] += jnp.sum(left * own[:, :middle] + right * own[:, middle:], -1, keepdims=True)
                o_query[:, at : at + GROUP] = left[:, :GROUP]
                o_key[:, at : at + half] = left[:, GROUP:]
                o_key[:, at + half : at + GROUP] = right[:, :half]
                o_value[:, at : at + GROUP] = right[:, half:]

            summing(("back", number), w_feed, number * 3 * GROUP, 3 * GROUP, finish_group)

    def advance(*names):
        for name in names:
            sums_of[name].advance()

    spills = []

    def spill(pairs):
        spills.extend(bring(source, target) for source, target in pairs)

    def settle():
        while spills:
            spills.pop().wait()

    g_weights = w_feed
    grads = w_feed.at[pl.ds(0, 3 * GROUP), pl.ds(3 * width, seq)]
    for item in range(per):
        last = item == per - 1
        if item == 0:
            token_links[0].arrived()
            cot_links[0].start()
            for copy in to_far:
                copy.wait()
        settle()

        def projected(item=item):
            token_links[item].left()
            if item < per - 1:
                spill(
                    (source, target.at[item])
                    for source, target in ((query, query_far), (key, key_far), (value, value_far))
                )

        attend_item(
            lengths[band * per + item], x.at[item], weights_t, gain_attn, cos, sin, query, key, value, attended_t,
            attended.at[item], log_total.at[item], normed, projected,
        )
        if item == 0:
            for load in load_rest:
                load.wait()
        cot_links[item].arrived()
        if not last:
            token_links[item + 1].start()
        elif per > 1:
            out_links[item - 1].start()

        def feed_tick(step, item=item, last=last):
            if not last:

                @pl.when(step == ff // WIDE - 1)
                def _():
                    token_links[item + 1].arrived()
                    cot_links[item + 1].start()

            elif fused:
                for at in range(1, ff // WIDE):

                    @pl.when(step == at)
                    def _(at=at):
                        advance(*[("feed", number) for number in range(at)])

        cot_links[item].left()
        feed_item(
            item > 0, x.at[item], attended.at[item], attended_t, cot.at[item], w_out, w_feed, w_down, gain_ffn,
            g_feed, g_down, g_out, g_norm_ffn, attended.at[item], grad_attended_t,
            (normed, normed_t, resid, out_acc, back_acc), feed_tick,
        )
        if not last:
            spill(
                (source, target.at[item])
                for source, target in ((attended_t, attended_t_far), (grad_attended_t, grad_attended_t_far))
            )
    feeds = [("feed", step) for step in range(ff // WIDE)]
    backs = [("back", number) for number in range(groups)]
    if fused:
        column = jnp.concatenate([g_norm_ffn[...], jnp.zeros((LANES - 1, width), F32)], 0).T
        g_out[:, width : width + LANES] = column.astype(LOW)
        g_out[:, width + LANES :] = jnp.zeros((width, LANES), LOW)
        advance(*feeds, "down", "out")
    out_links[per - 1].start()
    turns = list(reversed(range(per)))
    reloads = []
    for turn, item in enumerate(turns):
        last = turn == per - 1

        def back_tick(at, turn=turn, last=last):
            if not fused:
                return
            for place, names in plan(turn, last).items():

                @pl.when(at == place)
                def _(names=names):
                    advance(*names)

        def plan(turn, last):
            out = {place: [] for place in range(groups * PAIRS)}
            if turn == 0:
                out[1] = feeds[1:]
                out[3] = feeds[2:] + ["down", "out"]
                out[5] = feeds[3:]
            if turn == 1:
                out[2] = feeds + ["down", "out"]
                out[4] = ["down", "out"]
            if last:
                for number in range(groups - 1):
                    for place in range((number + 1) * PAIRS, groups * PAIRS):
                        out[place].append(backs[number])
            return {place: names for place, names in out.items() if names}

        def heads_done(turn=turn, last=last):
            if not last:
                following = turns[turn + 1]
                for source, target in (
                    (query_far, query), (key_far, key), (value_far, value), (attended_t_far, attended_t),
                    (grad_attended_t_far, grad_attended_t),
                ):
                    reloads.append(bring(source.at[following], target))
            elif fused:
                advance(*backs[1:])

        back_item(
            turn > 0, lengths[band * per + item], x.at[item], cot.at[item], grad_attended_t, attended_t, query, key,
            value, log_total.at[item], weights_t, gain_attn, cos, sin, g_weights, g_norm, grads, normed_t, back_acc,
            back_tick, heads_done,
        )
        grad_links[item].start()
        while reloads:
            reloads.pop().wait()
    own = []
    for item in range(per):
        own.append(bring(attended.at[item, own_rows(0)], home_out.at[item]))
        own.append(bring(cot.at[item, own_rows(0)], home_grad.at[item]))
    if fused:
        every = feeds + ["down", "out"] + backs
        first, *_, last = backs
        for names in ([last] + backs[1:-1], [last], ["down", "out", first], [last], backs[1:-1], [last]):
            advance(*names)
        while any(sums_of[name].state <= sums_of[name].stages for name in every):
            least = min(sums_of[name].state for name in every)
            advance(*[name for name in every if sums_of[name].state == least])
        o_norm_attn[...] = w_total[...].T[:1, :]
        for name in every:
            sums_of[name].close()
    else:
        own += [
            bring(source, target)
            for source, target in zip(
                (g_feed, g_down, g_out.at[:, pl.ds(0, width)], g_weights.at[:, pl.ds(0, 3 * width)]), sums[:4]
            )
        ]
        sums[4][...] = g_norm_ffn[...]
        sums[5][...] = g_norm[...]
    for copy in own:
        copy.wait()
    for item in range(per):
        for exchange in (out_links[item], grad_links[item]):
            exchange.arrived()
            exchange.left()


def block(bands, axis, lengths, tokens, cotangent, gains, tables, weights):
    band_rows, items, width = tokens.shape
    per, seq, ff = items // bands, bands * band_rows, weights[4].shape[1]
    fused = axis > 0
    low = lambda *shape: jax.ShapeDtypeStruct(shape, LOW)
    full = lambda *shape: jax.ShapeDtypeStruct(shape, F32)
    scratch = lambda *shape: pltpu.VMEM(shape, LOW)
    wide = lambda *shape: pltpu.VMEM(shape, F32)
    outside = pl.BlockSpec(memory_space=pl.ANY)
    inside = pl.BlockSpec(memory_space=pltpu.VMEM)
    out_shape = [low(items, band_rows, width)] * 2 + [low(max(per - 1, 1), width, seq)] * 5
    out_shape += [low(max(per - 1, 1), (bands - 1) * band_rows, width)]
    out_specs = [outside] * 8
    extra, links = [], 4 * per * (bands - 1)
    if fused:
        devices = axis * bands
        rows, ff_rows = width // devices, ff // devices
        out_shape += [full(rows, ff), full(rows, ff), full(ff_rows, width)] + [full(rows, width)] * 4 + [full(1, rows)] * 2
        out_specs += [inside] * 9
        shapes = [(width, 2 * WIDE)] * (ff // WIDE) + [(ff, width), (width, width + 2 * LANES)]
        shapes += [(width, 3 * GROUP)] * (width // GROUP)
        for shape in shapes:
            extra += sum_scratch(axis, bands, shape)
        links += len(shapes) * sum_links(axis, bands)
    else:
        out_shape += [low(width, 2 * ff), low(ff, width), low(width, width), low(width, 3 * width)] + [full(1, width)] * 2
        out_specs += [outside] * 4 + [inside] * 2
    return pl.pallas_call(
        functools.partial(block_kernel, bands, per, axis),
        name="block",
        out_shape=out_shape,
        in_specs=[smem()] + [inside] * 4 + [outside] * 9,
        out_specs=out_specs,
        scratch_shapes=[
            scratch(3 * width, width), scratch(width, width), scratch(width, 2 * ff), scratch(ff, width),
            scratch(width, 2 * ff), scratch(ff, width), scratch(width, width + 2 * LANES),
            scratch(per, seq, width), scratch(per, seq, width), scratch(per, seq, width), scratch(width, seq),
            scratch(width, seq), scratch(width, seq), scratch(width, seq), scratch(width, seq),
            scratch(seq, width), scratch(width, seq), scratch(seq, width), wide(seq, width), wide(seq, width),
            wide(per, width // HEAD_DIM, 1, seq), wide(1, width), wide(1, width),
            wide(max(width // (max(axis, 1) * bands), 8), 3 * width), wide(max(width // (max(axis, 1) * bands), 8), LANES),
            pltpu.SemaphoreType.DMA((16 + 12 * per,)),
            pltpu.SemaphoreType.DMA((links,)),
            pltpu.SemaphoreType.DMA((links,)),
        ]
        + extra,
        compiler_params=pltpu.CompilerParams(vmem_limit_bytes=64 * 2**20 - 2**16, collective_id=0, has_side_effects=True),
    )(
        lengths, *gains, *tables, tokens.reshape(band_rows * items, width), cotangent.reshape(band_rows * items, width),
        *weights,
    )


def rope_tables(seq):
    frequency = np.exp(-np.log(ROPE_BASE) * (2.0 * np.arange(HALF) / HEAD_DIM))
    angles = frequency[:, None] * np.arange(seq)[None, :]
    return jnp.asarray(np.cos(angles), F32), jnp.asarray(np.sin(angles), F32)


def per_device(
    bands,
    axis,
    tokens,
    lengths,
    norm_attn,
    w_query,
    w_key,
    w_value,
    w_out,
    norm_ffn,
    w_gate,
    w_up,
    w_down,
    cotangent,
):
    band_rows, items, width = tokens.shape
    per = items // bands
    seq = bands * band_rows
    band = lax.axis_index("band")
    whole_tiles = width // axis % 16 == 0 and width // axis // bands % 16 == 8 and w_gate.shape[1] // axis // bands % 16 == 0
    fused = axis if whole_tiles else 0
    home_out, home_grad, *sums = block(
        bands, fused, lengths, tokens, cotangent, (norm_attn, norm_ffn), rope_tables(seq),
        (w_query, w_key, w_value, w_out, w_gate, w_up, w_down),
    )
    sums = sums[6:]
    if fused:
        (output, grad_tokens), sums = merge_items([home_out, home_grad], sums[:-2], sums[-2:], band, bands)
        g_gate, g_up, g_down, g_out, g_query, g_key, g_value, g_norm_ffn, g_norm_attn = sums
    else:
        (output, grad_tokens), norms = merge_items([home_out, home_grad], [], sums[-2:], band, bands)
        axes = ("items", "band")
        total = lambda a: lax.psum_scatter(a, axes, scatter_dimension=0, tiled=True).astype(F32)
        g_feed, g_down, g_out, g_weights = (total(a) for a in sums[:4])
        norms = total(jnp.stack(norms, 1))
        g_norm_ffn, g_norm_attn = norms[:, 0], norms[:, 1]
        g_gate, g_up = jnp.moveaxis(g_feed.reshape(-1, w_gate.shape[1] // WIDE, 2, WIDE), 2, 0).reshape(2, -1, w_gate.shape[1])
        g_query, g_key, g_value = jnp.moveaxis(g_weights.reshape(-1, width // GROUP, 3, GROUP), 2, 0).reshape(3, -1, width)
    return (
        output,
        grad_tokens,
        g_norm_attn,
        g_query,
        g_key,
        g_value,
        g_out,
        g_norm_ffn,
        g_gate,
        g_up,
        g_down,
    )


def solution(mesh):
    split = P("band", "items", None)
    rows = P(("items", "band"), None)
    flat = P(("items", "band"))
    return jax.shard_map(
        functools.partial(per_device, mesh.shape["band"], mesh.shape["items"]),
        mesh=mesh,
        in_specs=(split, P("items")) + (P(),) * 9 + (split,),
        out_specs=(split, split, flat, rows, rows, rows, rows, flat, rows, rows, rows),
        check_vma=False,
    )
```

```python
import functools

import jax
import jax.numpy as jnp
import numpy as np
from jax import lax
from jax.experimental import pallas as pl
from jax.experimental.pallas import tpu as pltpu
from jax.sharding import PartitionSpec as P

HEAD_DIM = 64
HALF = HEAD_DIM // 2
EPS = 1e-05
NEG = -1e30
ROPE_BASE = 10000.0
LOG2E = 1.4426950408889634
SCALE = HEAD_DIM**-0.5
BLOCK = 256
F32 = jnp.float32
LOW = jnp.bfloat16
MESH = pl.DeviceIdType.MESH


def dot_nn(left, right):
    return lax.dot_general(left, right, (((1,), (0,)), ((), ())), preferred_element_type=F32)


def dot_nt(left, right):
    return lax.dot_general(left, right, (((1,), (1,)), ((), ())), preferred_element_type=F32)


def dot_tn(left, right):
    return lax.dot_general(left, right, (((0,), (0,)), ((), ())), preferred_element_type=F32)


def vmem(count):
    return [pl.BlockSpec(memory_space=pltpu.VMEM)] * count


def smem():
    return pl.BlockSpec(memory_space=pltpu.SMEM)


def params(mib):
    return pltpu.CompilerParams(vmem_limit_bytes=mib * 2**20)


def log2_of(number):
    return number.bit_length() - 1


def split_order(bands, per, chunk, band, item):
    items = bands * per
    row = lax.broadcasted_iota(jnp.int32, (bands * chunk, items * chunk), 0)
    col = lax.broadcasted_iota(jnp.int32, (bands * chunk, items * chunk), 1)
    other = (row >> log2_of(chunk)) + band
    other = jnp.where(other >= bands, other - bands, other)
    return jnp.where(col == (row & (chunk - 1)) * items + other * per + item, 1.0, 0.0).astype(LOW)


def merge_kernel(per, chunk, passed, flat, band_ref, *refs):
    count = passed + flat + 2
    ins, outs, refs = refs[:count], refs[count : 2 * count], refs[2 * count :]
    held, made, sem, through = refs[:2], refs[2:4], refs[4], refs[5:]
    items, band_rows, width = ins[0].shape
    size, bands, blocks = items * chunk, items // per, band_rows // chunk
    started = []

    def bring(source, target):
        copy = pltpu.make_async_copy(source, target, sem.at[len(started)])
        started.append(copy)
        copy.start()
        return copy

    loads = [bring(ins[at], held[at]) for at in range(2)]
    passing = [bring(source, place) for source, place in zip(ins[2 : 2 + passed], through)]
    stores = []
    for at in range(2 + passed, count):
        outs[at][...] = ins[at][0, :]
    row = lax.broadcasted_iota(jnp.int32, (size, size), 0)
    col = lax.broadcasted_iota(jnp.int32, (size, size), 1)
    number = col >> log2_of(chunk)
    source = band_ref[0] - (number >> log2_of(per))
    source = jnp.where(source < 0, source + bands, source)
    item = source * per + (number & (per - 1))
    order = jnp.where(row == (col & (chunk - 1)) * items + item, 1.0, 0.0).astype(LOW)
    for at in range(2):
        loads[at].wait()
        for block in range(blocks):
            parts = held[at][:, block * chunk : (block + 1) * chunk, :].reshape(size, width)
            made[at][block * size : (block + 1) * size, :] = dot_nn(order, parts).astype(LOW)
        stores.append(bring(made[at], outs[at]))
        if at == 0:
            for copy, place, out in zip(passing, through, outs[2 : 2 + passed]):
                copy.wait()
                stores.append(bring(place, out))
    for store in stores:
        store.wait()


def merge_items(arrays, passed, flat, band, bands):
    items, band_rows, width = arrays[0].shape
    chunk = 32 if band_rows % 32 == 0 else 16
    outside = pl.BlockSpec(memory_space=pl.ANY)
    inside = pl.BlockSpec(memory_space=pltpu.VMEM)
    merged = pl.pallas_call(
        functools.partial(merge_kernel, items // bands, chunk, len(passed), len(flat)),
        name="merge_items",
        out_shape=[jax.ShapeDtypeStruct((band_rows * items, width), LOW)] * 2
        + [jax.ShapeDtypeStruct(array.shape, array.dtype) for array in passed]
        + [jax.ShapeDtypeStruct(array.shape[1:], array.dtype) for array in flat],
        in_specs=[smem()] + [outside] * (2 + len(passed)) + [inside] * len(flat),
        out_specs=[outside] * (2 + len(passed)) + [inside] * len(flat),
        scratch_shapes=[pltpu.VMEM((items, band_rows, width), LOW)] * 2
        + [pltpu.VMEM((band_rows * items, width), LOW)] * 2
        + [pltpu.SemaphoreType.DMA((4 * (band_rows // chunk) + 2 * len(passed),))]
        + [pltpu.VMEM(array.shape, array.dtype) for array in passed],
        compiler_params=params(60),
    )(jnp.reshape(band, (1,)), *arrays, *passed, *flat)
    return [array.reshape(band_rows, items, width) for array in merged[:2]], merged[2:]


def rope(vector, cos, sin):
    parts = []
    for at in range(0, vector.shape[0], HEAD_DIM):
        lower, upper = vector[at : at + HALF], vector[at + HALF : at + HEAD_DIM]
        parts += [lower * cos - upper * sin, lower * sin + upper * cos]
    return jnp.concatenate(parts, 0)


def query_blocks(seq):
    return [(start, min(start + BLOCK, seq)) for start in range(0, seq, BLOCK)]


def limits(start, stop, length):
    position = start + lax.broadcasted_iota(jnp.int32, (1, stop - start), 1)
    return jnp.minimum(position, length - 1)


def score_parts(keys, queries, start, stop, length):
    parts = []
    if start:
        parts.append((0, BLOCK, dot_tn(keys[:, :BLOCK], queries)))
    first = min(start, BLOCK)
    late = dot_tn(keys[:, first:stop], queries)
    position = first + lax.broadcasted_iota(jnp.int32, late.shape, 0)
    late = jnp.where(position <= limits(start, stop, length), late, NEG)
    parts.append((first, stop, late))
    return parts


def norm_rows(inputs):
    return lax.rsqrt(jnp.mean(inputs * inputs, -1, keepdims=True) + EPS)


def attend_item(length, x, weights, gain, cos, sin, query, key, value, attended_t, attended, log_total, normed, ready):
    seq, width = x.shape
    tile = 128
    for at in range(0, seq, tile):
        inputs = x[at : at + tile, :].astype(F32)
        normed[at : at + tile, :] = (inputs * norm_rows(inputs) * gain).astype(LOW)

    project = 256

    def project_tile(at, _):
        rows = pl.ds(pl.multiple_of(at * project, project), project)
        for part, out, scaled in ((0, query, SCALE * LOG2E), (1, key, 1.0)):
            source = pl.ds(pl.multiple_of(part * width + at * project, project), project)
            out[rows, :] = (rope(dot_nt(weights[source, :], normed[...]), cos[...], sin[...]) * scaled).astype(LOW)
        source = pl.ds(pl.multiple_of(2 * width + at * project, project), project)
        value[rows, :] = dot_nt(weights[source, :], normed[...]).astype(LOW)
        return 0

    lax.fori_loop(0, width // project, project_tile, 0)
    ready()

    def head(at, _):
        for which in range(4):
            number = at * 4 + which
            rows = pl.ds(pl.multiple_of(number * HEAD_DIM, HEAD_DIM), HEAD_DIM)
            keys, values = key[rows, :], value[rows, :]
            for start, stop in query_blocks(seq):
                parts = score_parts(keys, query[rows, start:stop], start, stop, length)
                top = functools.reduce(jnp.maximum, [jnp.max(s, 0, keepdims=True) for _, _, s in parts])
                total = jnp.zeros_like(top)
                acc = jnp.zeros((HEAD_DIM, stop - start), F32)
                for first, last, scores in parts:
                    prob = jnp.exp2(scores - top)
                    total += jnp.sum(prob, 0, keepdims=True)
                    acc += dot_nn(values[:, first:last], prob.astype(LOW))
                attended_t[rows, start:stop] = (acc / total).astype(LOW)
                log_total[number, :, start:stop] = top + jnp.log2(total)
        return 0

    lax.fori_loop(0, width // HEAD_DIM // 4, head, 0)
    for at in range(0, width, project):
        attended[:, at : at + project] = attended_t[at : at + project, :].T


LANES = 128
GROUP = 256
WIDE = 512


def feed_item(follows, x, attended, attended_t, cot, w_out, w_feed, w_down, gain, g_feed, g_down, g_out, g_norm, out, grad_attended_t, scratch, cot_ready, tick, out_done):
    normed, normed_t, resid, out_acc, back_acc = scratch
    seq, width = x.shape
    ff = w_down.shape[0]
    tile = 128

    def put(ref, at, grad):
        if follows:
            grad += ref[at].astype(F32)
        ref[at] = grad.astype(LOW)

    for at in range(0, seq, tile):
        rows = slice(at, at + tile)
        total = x[rows, :].astype(F32) + dot_nn(attended[rows, :], w_out[...])
        resid[rows, :] = total.astype(LOW)
        out_acc[rows, :] = total
        low = (total * norm_rows(total) * gain).astype(LOW)
        normed[rows, :] = low
        normed_t[:, rows] = low.T
    back_acc[...] = jnp.zeros_like(back_acc)
    cot_ready()

    def chunk(step, _):
        tick(step)
        span = pl.ds(pl.multiple_of(step * WIDE, WIDE), WIDE)
        up_span = pl.ds(pl.multiple_of(ff + step * WIDE, WIDE), WIDE)
        lows = []
        for at in range(0, seq, seq // 2):
            rows = slice(at, at + seq // 2)
            parts = []
            for first in range(0, WIDE, WIDE // 2):
                columns = pl.ds(pl.multiple_of(step * WIDE + first, WIDE // 2), WIDE // 2)
                up_columns = pl.ds(pl.multiple_of(ff + step * WIDE + first, WIDE // 2), WIDE // 2)
                gate = dot_nn(normed[rows, :], w_feed[:, columns])
                upward = dot_nn(normed[rows, :], w_feed[:, up_columns])
                grad_hidden = dot_nt(cot[rows, :], w_down[columns, :])
                sig = 0.5 * jnp.tanh(0.5 * gate) + 0.5
                silu = gate * sig
                hidden = (silu * upward).astype(LOW)
                grad_gate = (grad_hidden * upward * (sig + silu * (1.0 - sig))).astype(LOW)
                grad_upward = (grad_hidden * silu).astype(LOW)
                parts.append((hidden, grad_gate, grad_upward))
            hidden, grad_gate, grad_upward = (jnp.concatenate(both, 1) for both in zip(*parts))
            out_acc[rows, :] += dot_nn(hidden, w_down[span, :])
            back_acc[rows, :] += dot_nt(grad_gate, w_feed[:, span])
            back_acc[rows, :] += dot_nt(grad_upward, w_feed[:, up_span])
            lows.append((hidden, grad_gate, grad_upward))
        hidden, grad_gate, grad_upward = (jnp.concatenate(parts, 0) for parts in zip(*lows))
        half = WIDE // 2
        for at in range(0, WIDE, half):
            part = pl.ds(pl.multiple_of(step * WIDE + at, half), half)
            put(g_down, (part, slice(None)), dot_nn(hidden[:, at : at + half].T, cot[...]))
        first = pl.ds(pl.multiple_of(step * 2 * WIDE, WIDE), WIDE)
        second = pl.ds(pl.multiple_of(step * 2 * WIDE + WIDE, WIDE), WIDE)
        half = width // 2
        for at in range(0, width, half):
            part = slice(at, at + half)
            put(g_feed, (part, first), dot_nn(normed_t[part, :], grad_gate))
            put(g_feed, (part, second), dot_nn(normed_t[part, :], grad_upward))
        return 0

    lax.fori_loop(0, ff // WIDE, chunk, 0)
    for at in range(0, seq, tile):
        out[at : at + tile, :] = out_acc[at : at + tile, :].astype(LOW)
    out_done()
    norm_sum = jnp.zeros((1, width), F32)
    for at in range(0, seq, tile):
        rows = slice(at, at + tile)
        total, incoming = resid[rows, :].astype(F32), back_acc[rows, :]
        inv = norm_rows(total)
        scaled = total * inv
        norm_sum += jnp.sum(incoming * scaled, 0, keepdims=True)
        weighted = incoming * gain
        grad = cot[rows, :].astype(F32) + inv * (weighted - scaled * jnp.mean(weighted * scaled, -1, keepdims=True))
        cot[rows, :] = grad.astype(LOW)
    g_norm[...] = g_norm[...] + norm_sum if follows else norm_sum
    for at in range(0, width, GROUP):
        rows = slice(at, at + GROUP)
        grad_attended_t[rows, :] = dot_nt(w_out[rows, :], cot[...]).astype(LOW)
    for at in range(0, width, GROUP):
        rows = slice(at, at + GROUP)
        put(g_out, (rows, slice(0, width)), dot_nn(attended_t[rows, :], cot[...]))


PAIRS = GROUP // (2 * HEAD_DIM)


def back_item(
    follows, length, x, grad_resid, grad_attended, attended, query, key, value, log_total, weights, gain, cos, sin,
    g_weights, g_norm, grads, normed_t, back, tick, heads_done,
):
    seq, width = x.shape
    blocks = query_blocks(seq)
    tile = 128
    for at in range(0, seq, tile):
        inputs = x[at : at + tile, :].astype(F32)
        normed_t[:, at : at + tile] = (inputs * norm_rows(inputs) * gain).astype(LOW).T
    back[...] = jnp.zeros_like(back)

    def group(number, _):
        def pair(at, _):
            tick(number * PAIRS + at)
            for which in range(2):
                local = at * 2 + which
                head = number * (2 * PAIRS) + local
                rows = pl.ds(pl.multiple_of(head * HEAD_DIM, HEAD_DIM), HEAD_DIM)
                keys, values = key[rows, :], value[rows, :]
                delta_all = jnp.sum(grad_attended[rows, :].astype(F32) * attended[rows, :].astype(F32), 0, keepdims=True)
                key_grads = [0.0] * len(blocks)
                value_grads = [0.0] * len(blocks)
                at_query, at_key, at_value = (
                    pl.ds(pl.multiple_of(part * GROUP + local * HEAD_DIM, HEAD_DIM), HEAD_DIM) for part in range(3)
                )
                for start, stop in blocks:
                    queries, incoming = query[rows, start:stop], grad_attended[rows, start:stop]
                    total = log_total[head, :, start:stop]
                    delta = delta_all[:, start:stop]
                    query_grad = 0.0
                    for first, last, scores in score_parts(keys, queries, start, stop, length):
                        prob = jnp.exp2(scores - total)
                        grad_prob = dot_tn(values[:, first:last], incoming)
                        grad_score = (prob * (grad_prob - delta)).astype(LOW)
                        query_grad += dot_nn(keys[:, first:last], grad_score)
                        key_grad = dot_nt(queries, grad_score)
                        value_grad = dot_nt(incoming, prob.astype(LOW))
                        for piece, (low, high) in enumerate(blocks):
                            if first <= low and high <= last:
                                key_grads[piece] += key_grad[:, low - first : high - first]
                                value_grads[piece] += value_grad[:, low - first : high - first]
                    grads[at_query, start:stop] = (
                        rope(query_grad, cos[:, start:stop], -sin[:, start:stop]) * SCALE
                    ).astype(LOW)
                for (start, stop), key_grad, value_grad in zip(blocks, key_grads, value_grads):
                    grads[at_key, start:stop] = (
                        rope(key_grad, cos[:, start:stop], -sin[:, start:stop]) * (1.0 / LOG2E)
                    ).astype(LOW)
                    grads[at_value, start:stop] = value_grad.astype(LOW)
            return 0

        lax.fori_loop(0, PAIRS, pair, 0)
        turned = grads[...].T
        columns = pl.ds(pl.multiple_of(number * 3 * GROUP, GROUP), 3 * GROUP)
        for at in range(0, width, GROUP):
            rows = slice(at, at + GROUP)
            grad = dot_nn(normed_t[rows, :], turned)
            if follows:
                grad += g_weights[rows, columns].astype(F32)
            g_weights[rows, columns] = grad.astype(LOW)
        for at in range(0, seq, seq // 2):
            rows = slice(at, at + seq // 2)
            total = back[rows, :]
            for part in range(3):
                source = pl.ds(pl.multiple_of(part * width + number * GROUP, GROUP), GROUP)
                total += dot_nn(turned[rows, part * GROUP : (part + 1) * GROUP], weights[source, :])
            back[rows, :] = total
        return 0

    lax.fori_loop(0, width // GROUP, group, 0)
    heads_done()
    norm_sum = jnp.zeros((1, width), F32)
    for at in range(0, seq, tile):
        rows = slice(at, at + tile)
        inputs, incoming = x[rows, :].astype(F32), back[rows, :]
        inv = norm_rows(inputs)
        scaled = inputs * inv
        norm_sum += jnp.sum(incoming * scaled, 0, keepdims=True)
        weighted = incoming * gain
        grad = grad_resid[rows, :].astype(F32) + inv * (
            weighted - scaled * jnp.mean(weighted * scaled, -1, keepdims=True)
        )
        grad_resid[rows, :] = grad.astype(LOW)
    g_norm[...] = g_norm[...] + norm_sum if follows else norm_sum


class Links:
    def __init__(self, bands, axis, send, receive):
        self.send, self.receive, self.bands = send, receive, bands
        self.band, self.items = lax.axis_index("band"), lax.axis_index("items")
        self.item_bits, self.item_partners = bits_of(self.items, axis) if axis else ((), ())
        self.band_bits, self.band_partners = bits_of(self.band, bands)
        self.count = 0

    def take(self, count):
        first = self.count
        self.count += count
        return first

    def other(self, shift):
        return lax.rem(self.band + shift + self.bands, self.bands)

    def greet(self):
        barrier = pltpu.get_barrier_semaphore()
        others = [(self.items, self.other(shift)) for shift in range(1, self.bands)]
        others += [(partner, self.band) for partner in self.item_partners]
        for other in others:
            pl.semaphore_signal(barrier, inc=1, device_id=other, device_id_type=MESH)
        return lambda: pl.semaphore_wait(barrier, len(others))

    def copy(self, number, source, target, device):
        return pltpu.make_async_remote_copy(
            src_ref=source,
            dst_ref=target,
            send_sem=self.send.at[number],
            recv_sem=self.receive.at[number],
            device_id=device,
            device_id_type=MESH,
        )


class Exchange:
    def __init__(self, links, source, target, arrival):
        self.links, self.first = links, links.take(links.bands - 1)
        self.source, self.target, self.arrival = source, target, arrival

    def each(self, place):
        for shift in range(1, self.links.bands):
            yield self.links.copy(
                self.first + shift - 1, self.source(shift), place(shift), (self.links.items, self.links.other(shift))
            )

    def start(self):
        for copy in self.each(self.target):
            copy.start()

    def arrived(self):
        for copy in self.each(self.arrival):
            copy.wait_recv()

    def left(self):
        for copy in self.each(self.target):
            copy.wait_send()


def bits_of(number, size):
    bits = [lax.rem(lax.div(number, 2**at), 2) for at in range(log2_of(size))]
    return bits, [number + (1 - 2 * bit) * 2**at for at, bit in enumerate(bits)]


def sum_lanes(axis, stage, columns):
    left = list(range(log2_of(axis)))
    right = [0] + left[:0:-1]
    half = columns // 2
    if stage == 0:
        return [(left[0], left[1:], 0, columns)]
    return [(left[stage], left[stage + 1 :], 0, half), (right[stage], right[stage + 1 :], half, half)]


def band_shape(axis, bands, shape):
    rows = shape[0] // axis // bands
    return (rows, shape[1]) if rows % 16 == 0 else (2 * rows, shape[1] // 2)


def sum_scratch(axis, bands, shape):
    low = lambda *dims: pltpu.VMEM(dims, LOW)
    out = []
    for stage in range(log2_of(axis)):
        for _, bits, _, columns in sum_lanes(axis, stage, shape[1]):
            out.append(low(*(2,) * len(bits), shape[0] // axis, columns))
    part = band_shape(axis, bands, shape)
    out.append(low(*(2,) * log2_of(bands), *part))
    for stage in range(log2_of(bands)):
        out.append(low(*(2,) * (log2_of(bands) - stage - 1), *part))
    return out


def sum_links(axis, bands):
    return 2 * log2_of(axis) + log2_of(bands)


class Summing:
    def __init__(self, links, axis, array, first, columns, scratch, finish):
        self.links, self.array, self.finish = links, array, finish
        self.first, self.columns, self.scratch = first, columns, scratch
        self.axis, self.count = axis, log2_of(axis)
        self.stages = self.count + log2_of(links.bands)
        self.base = links.take(sum_links(axis, links.bands))
        self.state = 0

    def flights(self, stage):
        links = self.links
        if stage < self.count:
            rows, wide = self.array.shape
            view = self.array.reshape(*(2,) * self.count, rows // self.axis, wide)
            bits, partners, used = links.item_bits, links.item_partners, [0] if stage == 0 else [2 * stage - 1, 2 * stage]
            lanes = sum_lanes(self.axis, stage, self.columns)
            first = self.first
        else:
            view, first = self.scratch[2 * self.count - 1], 0
            bits, partners, used = links.band_bits, links.band_partners, [self.count + stage]
            at = stage - self.count
            lanes = [(at, list(range(at + 1, len(bits))), 0, view.shape[-1])]
        out = []
        for (now, later, start, columns), number in zip(lanes, used):
            place = lambda own: tuple(
                slice(None) if at in later else 1 - bits[at] if at == now and not own else bits[at]
                for at in reversed(range(len(bits)))
            ) + (slice(None), pl.ds(first + start, columns))
            partner = partners[now]
            device = (partner, links.band) if stage < self.count else (links.items, partner)
            came = self.scratch[number]
            out.append((links.copy(self.base + number, view.at[place(False)], came, device), view.at[place(True)], came))
        return out

    def begin(self, stage):
        for copy, _, _ in self.flights(stage):
            copy.start()

    def end(self, stage):
        flights = self.flights(stage)
        for copy, _, _ in flights:
            copy.wait_recv()
            copy.wait_send()
        for _, kept, came in flights:
            if stage == self.stages - 1:
                self.finish(kept[...].astype(F32) + came[...].astype(F32))
                continue
            rows = came.shape[-2]
            tile = 48 if rows % 48 == 0 else 32 if rows % 32 == 0 else 16
            for choice in np.ndindex(*came.shape[:-2]):

                def add(step, _, kept=kept, came=came, choice=choice):
                    span = choice + (pl.ds(pl.multiple_of(step * tile, tile), tile), slice(None))
                    kept[span] = kept[span] + came[span]
                    return 0

                lax.fori_loop(0, rows // tile, add, 0)
        if stage == self.count - 1:
            self.stack()

    def stack(self):
        bands, parts = self.links.bands, self.scratch[2 * self.count - 1]
        rows = self.array.shape[0] // self.axis
        start = pl.multiple_of(self.links.items * rows, rows)
        whole = self.array.at[pl.ds(start, rows), pl.ds(self.first, self.columns)]
        rows = rows // bands
        spans = [slice(number * rows, (number + 1) * rows) for number in range(bands)]
        places = list(np.ndindex(*parts.shape[:-2]))
        if parts.shape[-2] == rows:
            for place, span in zip(places, spans):
                parts[place] = whole[span, :]
            return
        half = self.columns // 2
        left, right = whole[:, :half].astype(F32), whole[:, half:].astype(F32)
        for place, span in zip(places, spans):
            parts[place] = jnp.concatenate([left[span], right[span]], 0).astype(LOW)

    def advance(self):
        if self.state > self.stages:
            return
        if self.state > 0:
            self.end(self.state - 1)
        if self.state < self.stages:
            self.begin(self.state)
        self.state += 1


def block_kernel(bands, per, axis, *refs):
    fused = axis > 0
    lengths, norm_attn, norm_ffn, cos, sin = refs[:5]
    tokens, cotangent, w_query, w_key, w_value, w_out_from, w_gate, w_up, w_down_from = refs[5:14]
    refs = refs[14:]
    home_out, home_grad = refs[:2]
    query_far, key_far, value_far, attended_t_far, grad_attended_t_far, cot_far = refs[2:8]
    refs = refs[8:]
    sums, refs = (refs[:9], refs[9:]) if fused else (refs[:6], refs[6:])
    weights_t, w_out, w_feed, w_down, g_feed, g_down, g_out = refs[:7]
    x, cot, attended, attended_t, query, key, value, grad_attended_t = refs[7:15]
    normed, normed_t, resid, out_acc, back_acc, log_total, g_norm, g_norm_ffn = refs[15:23]
    w_own, w_total, local, send, receive = refs[23:28]
    sum_refs = refs[28:]
    seq, width = x.shape[1:]
    ff = w_down.shape[0]
    band_rows, items = seq // bands, bands * per
    groups = width // GROUP
    links = Links(bands, axis, send, receive)
    band = links.band
    gain_attn, gain_ffn = norm_attn[...][None, :], norm_ffn[...][None, :]
    started = [0]

    def bring(source, target):
        copy = pltpu.make_async_copy(source, target, local.at[started[0]])
        started[0] += 1
        copy.start()
        return copy

    token_rows = band_rows * items
    chunk = 32 if band_rows % 32 == 0 else 16
    size = items * chunk
    raw = g_down.at[pl.ds(0, token_rows)]
    spans = [pl.ds(at, size) for at in range(0, token_rows, size)]
    load_tokens = [bring(tokens.at[span], raw.at[span]) for span in spans]
    qkv = (g_feed.at[:, pl.ds(0, width)], g_feed.at[:, pl.ds(width, width)], g_feed.at[:, pl.ds(2 * width, width)])
    load_qkv = [bring(source, target) for source, target in zip((w_query, w_key, w_value), qkv)]
    all_here = links.greet()

    def own_rows(shift):
        return pl.ds(pl.multiple_of(links.other(shift) * band_rows, band_rows), band_rows)

    token_send = [attended.at[item] for item in range(per)]
    stages = [normed, resid]
    cot_send = [g_out.at[:, pl.ds(0, width)]] + [cot_far.at[item] for item in range(per - 1)]

    def split(kept, sent, item, loads=()):
        order = split_order(bands, per, chunk, band, item)
        for block in range(band_rows // chunk):
            if loads:
                loads[block].wait()
            moved = dot_nn(order, raw[block * size : (block + 1) * size, :]).astype(LOW)
            kept[item, pl.ds(pl.multiple_of(band * band_rows + block * chunk, 16), chunk), :] = moved[:chunk]
            for shift in range(1, bands):
                place = (shift - 1) * band_rows + block * chunk
                sent[place : place + chunk, :] = moved[shift * chunk : (shift + 1) * chunk]

    def scattering(sent, kept, item):
        return Exchange(
            links,
            lambda shift: sent[item].at[pl.ds((shift - 1) * band_rows, band_rows)],
            lambda shift: kept.at[item, own_rows(0)],
            lambda shift: kept.at[item, own_rows(-shift)],
        )

    def returning(source, home, item):
        slot = lambda shift: home.at[shift * per + item]
        return Exchange(links, lambda shift: source.at[item, own_rows(shift)], slot, slot)

    token_links = [scattering(token_send, x, item) for item in range(per)]
    cot_links = [scattering(cot_send, cot, item) for item in range(per)]
    out_links = [returning(attended, home_out, item) for item in range(per)]
    grad_links = [returning(cot, home_grad, item) for item in range(per)]

    split(x, token_send[0], 0, load_tokens)
    all_here()
    token_links[0].start()
    for item in range(1, per):
        split(x, token_send[item], item)
    load_cot = bring(cotangent, raw)
    load_rest = [
        bring(w_out_from, w_out),
        bring(w_gate, w_feed.at[:, pl.ds(0, ff)]),
        bring(w_up, w_feed.at[:, pl.ds(ff, ff)]),
        bring(w_down_from, w_down),
    ]
    for part in range(3):
        load_qkv[part].wait()
        for at in range(0, width, 256):
            weights_t[part * width + at : part * width + at + 256, :] = qkv[part][:, at : at + 256].T
        if fused:
            own = w_own.shape[0]
            device = links.items * bands + band
            if part == 0:
                halves_of = axis * bands // 2
                column = jnp.concatenate([gain_attn, jnp.zeros((LANES - 1, width), F32)], 0).T
                out_acc[: width // 2, :LANES] = column[: width // 2]
                out_acc[: width // 2, LANES : 2 * LANES] = column[width // 2 :]
                at = pl.multiple_of(lax.rem(device, halves_of) * own, 8)
                both = out_acc[pl.ds(at, own), : 2 * LANES]
                own_gain = 1.0 / jnp.where(device < halves_of, both[:, :1], both[:, LANES : LANES + 1])
            both = qkv[part][pl.ds(pl.multiple_of(lax.div(device, 2) * (2 * own), 16), 2 * own), :].astype(F32)
            mine = jnp.where(lax.rem(device, 2) == 0, both[:own], both[own:]) * own_gain
            for number in range(groups):
                at = (number * 3 + part) * GROUP
                w_own[:, at : at + GROUP] = mine[:, number * GROUP : (number + 1) * GROUP]
    load_cot.wait()
    for item in range(per):
        split(cot, stages[item - 1] if item else cot_send[0], item)
    late = pl.ds(0, (bands - 1) * band_rows)
    to_far = [bring(stages[item].at[late], cot_far.at[item]) for item in range(per - 1)]

    sums_of = {}
    schedule = {}
    if fused:
        scratch_each = len(sum_scratch(axis, bands, (axis * bands * 16, 256)))
        taken = [0]
        o_gate, o_up, o_down, o_out, o_query, o_key, o_value, o_norm_ffn, o_norm_attn = sums
        w_total[...] = jnp.zeros_like(w_total)

        def summing(name, array, first, columns, finish):
            sums_of[name] = Summing(
                links, axis, array, first, columns, sum_refs[taken[0] : taken[0] + scratch_each], finish
            )
            taken[0] += scratch_each

        def halves(total):
            rows = total.shape[0] // 2
            return total[:rows], total[rows:]

        for step in range(ff // WIDE):

            def finish_feed(total, step=step):
                span = slice(step * WIDE, (step + 1) * WIDE)
                o_gate[:, span], o_up[:, span] = halves(total)

            summing(("feed", step), g_feed, step * 2 * WIDE, 2 * WIDE, finish_feed)

        def finish_down(total):
            o_down[...] = total

        def finish_out(total):
            left, right = halves(total)
            half = left.shape[1]
            o_out[:, :half] = left
            o_out[:, half:] = right[:, : width - half]
            o_norm_ffn[...] = right[:, width - half : width - half + LANES].T[:1, :]

        summing("down", g_down, 0, width, finish_down)
        summing("out", g_out, 0, width + 2 * LANES, finish_out)
        for number in range(groups):

            def finish_group(total, number=number):
                left, right = halves(total)
                at, half = number * GROUP, GROUP // 2
                own = w_own[:, 3 * at : 3 * at + 3 * GROUP]
                middle = left.shape[1]
                w_total[...] += jnp.sum(left * own[:, :middle] + right * own[:, middle:], -1, keepdims=True)
                o_query[:, at : at + GROUP] = left[:, :GROUP]
                o_key[:, at : at + half] = left[:, GROUP:]
                o_key[:, at + half : at + GROUP] = right[:, :half]
                o_value[:, at : at + GROUP] = right[:, half:]

            summing(("back", number), w_feed, number * 3 * GROUP, 3 * GROUP, finish_group)

    def advance(*names):
        for name in names:
            sums_of[name].advance()

    spills = []

    def spill(pairs):
        spills.extend(bring(source, target) for source, target in pairs)

    def settle():
        while spills:
            spills.pop().wait()

    g_weights = w_feed
    grads = w_feed.at[pl.ds(0, 3 * GROUP), pl.ds(3 * width, seq)]
    for item in range(per):
        last = item == per - 1
        if item == 0:
            token_links[0].arrived()
            cot_links[0].start()
            for copy in to_far:
                copy.wait()
        settle()

        def projected(item=item):
            token_links[item].left()
            if item < per - 1:
                spill(
                    (source, target.at[item])
                    for source, target in ((query, query_far), (key, key_far), (value, value_far))
                )

        attend_item(
            lengths[band * per + item], x.at[item], weights_t, gain_attn, cos, sin, query, key, value, attended_t,
            attended.at[item], log_total.at[item], normed, projected,
        )
        if item == 0:
            for load in load_rest:
                load.wait()
        def cot_ready(item=item, last=last):
            cot_links[item].arrived()
            if not last:
                token_links[item + 1].start()
            elif per > 1:
                out_links[item - 1].start()
            cot_links[item].left()

        def feed_tick(step, item=item, last=last):
            if not last:

                @pl.when(step == ff // WIDE - 1)
                def _():
                    token_links[item + 1].arrived()
                    cot_links[item + 1].start()

            elif fused:
                for at in range(1, ff // WIDE):

                    @pl.when(step == at)
                    def _(at=at):
                        advance(*[("feed", number) for number in range(at)])

        feed_item(
            item > 0, x.at[item], attended.at[item], attended_t, cot.at[item], w_out, w_feed, w_down, gain_ffn,
            g_feed, g_down, g_out, g_norm_ffn, attended.at[item], grad_attended_t,
            (normed, normed_t, resid, out_acc, back_acc), cot_ready, feed_tick, out_links[item].start if last else lambda: None,
        )
        if not last:
            spill(
                (source, target.at[item])
                for source, target in ((attended_t, attended_t_far), (grad_attended_t, grad_attended_t_far))
            )
    feeds = [("feed", step) for step in range(ff // WIDE)]
    backs = [("back", number) for number in range(groups)]
    if fused:
        column = jnp.concatenate([g_norm_ffn[...], jnp.zeros((LANES - 1, width), F32)], 0).T
        g_out[:, width : width + LANES] = column.astype(LOW)
        g_out[:, width + LANES :] = jnp.zeros((width, LANES), LOW)
        advance(*feeds, "down", "out")
    turns = list(reversed(range(per)))
    reloads = []
    for turn, item in enumerate(turns):
        last = turn == per - 1

        def back_tick(at, turn=turn, last=last):
            if not fused:
                return
            for place, names in plan(turn, last).items():

                @pl.when(at == place)
                def _(names=names):
                    advance(*names)

        def plan(turn, last):
            out = {place: [] for place in range(groups * PAIRS)}
            if turn == 0:
                out[1] = feeds[1:]
                out[3] = feeds[2:] + ["down", "out"]
                out[5] = feeds[3:]
            if turn == 1:
                out[2] = feeds + ["down", "out"]
                out[4] = ["down", "out"]
            if last:
                for number in range(groups - 1):
                    for place in range((number + 1) * PAIRS, groups * PAIRS):
                        out[place].append(backs[number])
            return {place: names for place, names in out.items() if names}

        def heads_done(turn=turn, last=last):
            if not last:
                following = turns[turn + 1]
                for source, target in (
                    (query_far, query), (key_far, key), (value_far, value), (attended_t_far, attended_t),
                    (grad_attended_t_far, grad_attended_t),
                ):
                    reloads.append(bring(source.at[following], target))
            elif fused:
                advance(*backs[1:])

        back_item(
            turn > 0, lengths[band * per + item], x.at[item], cot.at[item], grad_attended_t, attended_t, query, key,
            value, log_total.at[item], weights_t, gain_attn, cos, sin, g_weights, g_norm, grads, normed_t, back_acc,
            back_tick, heads_done,
        )
        grad_links[item].start()
        while reloads:
            reloads.pop().wait()
    own = []
    for item in range(per):
        own.append(bring(attended.at[item, own_rows(0)], home_out.at[item]))
        own.append(bring(cot.at[item, own_rows(0)], home_grad.at[item]))
    if fused:
        every = feeds + ["down", "out"] + backs
        first, *_, last = backs
        for names in ([last] + backs[1:-1], [last], ["down", "out", first], [last], backs[1:-1], [last]):
            advance(*names)
        while any(sums_of[name].state <= sums_of[name].stages for name in every):
            least = min(sums_of[name].state for name in every)
            advance(*[name for name in every if sums_of[name].state == least])
        o_norm_attn[...] = w_total[...].T[:1, :]
    else:
        own += [
            bring(source, target)
            for source, target in zip(
                (g_feed, g_down, g_out.at[:, pl.ds(0, width)], g_weights.at[:, pl.ds(0, 3 * width)]), sums[:4]
            )
        ]
        sums[4][...] = g_norm_ffn[...]
        sums[5][...] = g_norm[...]
    for copy in own:
        copy.wait()
    for item in range(per):
        for exchange in (out_links[item], grad_links[item]):
            exchange.arrived()
            exchange.left()


def block(bands, axis, lengths, tokens, cotangent, gains, tables, weights):
    band_rows, items, width = tokens.shape
    per, seq, ff = items // bands, bands * band_rows, weights[4].shape[1]
    fused = axis > 0
    low = lambda *shape: jax.ShapeDtypeStruct(shape, LOW)
    full = lambda *shape: jax.ShapeDtypeStruct(shape, F32)
    scratch = lambda *shape: pltpu.VMEM(shape, LOW)
    wide = lambda *shape: pltpu.VMEM(shape, F32)
    outside = pl.BlockSpec(memory_space=pl.ANY)
    inside = pl.BlockSpec(memory_space=pltpu.VMEM)
    out_shape = [low(items, band_rows, width)] * 2 + [low(max(per - 1, 1), width, seq)] * 5
    out_shape += [low(max(per - 1, 1), (bands - 1) * band_rows, width)]
    out_specs = [outside] * 8
    extra, links = [], 4 * per * (bands - 1)
    if fused:
        devices = axis * bands
        rows, ff_rows = width // devices, ff // devices
        out_shape += [full(rows, ff), full(rows, ff), full(ff_rows, width)] + [full(rows, width)] * 4 + [full(1, rows)] * 2
        out_specs += [inside] * 9
        shapes = [(width, 2 * WIDE)] * (ff // WIDE) + [(ff, width), (width, width + 2 * LANES)]
        shapes += [(width, 3 * GROUP)] * (width // GROUP)
        for shape in shapes:
            extra += sum_scratch(axis, bands, shape)
        links += len(shapes) * sum_links(axis, bands)
    else:
        out_shape += [low(width, 2 * ff), low(ff, width), low(width, width), low(width, 3 * width)] + [full(1, width)] * 2
        out_specs += [outside] * 4 + [inside] * 2
    return pl.pallas_call(
        functools.partial(block_kernel, bands, per, axis),
        name="block",
        out_shape=out_shape,
        in_specs=[smem()] + [inside] * 4 + [outside] * 9,
        out_specs=out_specs,
        scratch_shapes=[
            scratch(3 * width, width), scratch(width, width), scratch(width, 2 * ff), scratch(ff, width),
            scratch(width, 2 * ff), scratch(ff, width), scratch(width, width + 2 * LANES),
            scratch(per, seq, width), scratch(per, seq, width), scratch(per, seq, width), scratch(width, seq),
            scratch(width, seq), scratch(width, seq), scratch(width, seq), scratch(width, seq),
            scratch(seq, width), scratch(width, seq), scratch(seq, width), wide(seq, width), wide(seq, width),
            wide(per, width // HEAD_DIM, 1, seq), wide(1, width), wide(1, width),
            wide(max(width // (max(axis, 1) * bands), 8), 3 * width), wide(max(width // (max(axis, 1) * bands), 8), LANES),
            pltpu.SemaphoreType.DMA((32 + 12 * per,)),
            pltpu.SemaphoreType.DMA((links,)),
            pltpu.SemaphoreType.DMA((links,)),
        ]
        + extra,
        compiler_params=pltpu.CompilerParams(vmem_limit_bytes=64 * 2**20 - 2**16, collective_id=0, has_side_effects=True),
    )(
        lengths, *gains, *tables, tokens.reshape(band_rows * items, width), cotangent.reshape(band_rows * items, width),
        *weights,
    )


def rope_tables(seq):
    frequency = np.exp(-np.log(ROPE_BASE) * (2.0 * np.arange(HALF) / HEAD_DIM))
    angles = frequency[:, None] * np.arange(seq)[None, :]
    return jnp.asarray(np.cos(angles), F32), jnp.asarray(np.sin(angles), F32)


def per_device(
    bands,
    axis,
    tokens,
    lengths,
    norm_attn,
    w_query,
    w_key,
    w_value,
    w_out,
    norm_ffn,
    w_gate,
    w_up,
    w_down,
    cotangent,
):
    band_rows, items, width = tokens.shape
    per = items // bands
    seq = bands * band_rows
    band = lax.axis_index("band")
    whole_tiles = width // axis % 16 == 0 and width // axis // bands % 16 == 8 and w_gate.shape[1] // axis // bands % 16 == 0
    fused = axis if whole_tiles else 0
    home_out, home_grad, *sums = block(
        bands, fused, lengths, tokens, cotangent, (norm_attn, norm_ffn), rope_tables(seq),
        (w_query, w_key, w_value, w_out, w_gate, w_up, w_down),
    )
    sums = sums[6:]
    if fused:
        (output, grad_tokens), sums = merge_items([home_out, home_grad], sums[:-2], sums[-2:], band, bands)
        g_gate, g_up, g_down, g_out, g_query, g_key, g_value, g_norm_ffn, g_norm_attn = sums
    else:
        (output, grad_tokens), norms = merge_items([home_out, home_grad], [], sums[-2:], band, bands)
        axes = ("items", "band")
        total = lambda a: lax.psum_scatter(a, axes, scatter_dimension=0, tiled=True).astype(F32)
        g_feed, g_down, g_out, g_weights = (total(a) for a in sums[:4])
        norms = total(jnp.stack(norms, 1))
        g_norm_ffn, g_norm_attn = norms[:, 0], norms[:, 1]
        g_gate, g_up = jnp.moveaxis(g_feed.reshape(-1, w_gate.shape[1] // WIDE, 2, WIDE), 2, 0).reshape(2, -1, w_gate.shape[1])
        g_query, g_key, g_value = jnp.moveaxis(g_weights.reshape(-1, width // GROUP, 3, GROUP), 2, 0).reshape(3, -1, width)
    return (
        output,
        grad_tokens,
        g_norm_attn,
        g_query,
        g_key,
        g_value,
        g_out,
        g_norm_ffn,
        g_gate,
        g_up,
        g_down,
    )


def solution(mesh):
    split = P("band", "items", None)
    rows = P(("items", "band"), None)
    flat = P(("items", "band"))
    return jax.shard_map(
        functools.partial(per_device, mesh.shape["band"], mesh.shape["items"]),
        mesh=mesh,
        in_specs=(split, P("items")) + (P(),) * 9 + (split,),
        out_specs=(split, split, flat, rows, rows, rows, rows, flat, rows, rows, rows),
        check_vma=False,
    )
```

```python
import functools

import jax
import jax.numpy as jnp
import numpy as np
from jax import lax
from jax.experimental import pallas as pl
from jax.experimental.pallas import tpu as pltpu
from jax.sharding import PartitionSpec as P

HEAD_DIM = 64
HALF = HEAD_DIM // 2
EPS = 1e-05
NEG = -1e30
ROPE_BASE = 10000.0
LOG2E = 1.4426950408889634
SCALE = HEAD_DIM**-0.5
BLOCK = 256
F32 = jnp.float32
LOW = jnp.bfloat16
MESH = pl.DeviceIdType.MESH


def dot_nn(left, right):
    return lax.dot_general(left, right, (((1,), (0,)), ((), ())), preferred_element_type=F32)


def dot_nt(left, right):
    return lax.dot_general(left, right, (((1,), (1,)), ((), ())), preferred_element_type=F32)


def dot_tn(left, right):
    return lax.dot_general(left, right, (((0,), (0,)), ((), ())), preferred_element_type=F32)


def vmem(count):
    return [pl.BlockSpec(memory_space=pltpu.VMEM)] * count


def smem():
    return pl.BlockSpec(memory_space=pltpu.SMEM)


def params(mib):
    return pltpu.CompilerParams(vmem_limit_bytes=mib * 2**20)


def log2_of(number):
    return number.bit_length() - 1


def split_order(bands, per, chunk, band, item):
    items = bands * per
    row = lax.broadcasted_iota(jnp.int32, (bands * chunk, items * chunk), 0)
    col = lax.broadcasted_iota(jnp.int32, (bands * chunk, items * chunk), 1)
    other = (row >> log2_of(chunk)) + band
    other = jnp.where(other >= bands, other - bands, other)
    return jnp.where(col == (row & (chunk - 1)) * items + other * per + item, 1.0, 0.0).astype(LOW)


def merge_kernel(per, chunk, passed, flat, band_ref, *refs):
    count = passed + flat + 2
    ins, outs, refs = refs[:count], refs[count : 2 * count], refs[2 * count :]
    held, made, sem, through = refs[:2], refs[2:4], refs[4], refs[5:]
    items, band_rows, width = ins[0].shape
    size, bands, blocks = items * chunk, items // per, band_rows // chunk
    started = []

    def bring(source, target):
        copy = pltpu.make_async_copy(source, target, sem.at[len(started)])
        started.append(copy)
        copy.start()
        return copy

    loads = [bring(ins[at], held[at]) for at in range(2)]
    passing = [bring(source, place) for source, place in zip(ins[2 : 2 + passed], through)]
    stores = []
    for at in range(2 + passed, count):
        outs[at][...] = ins[at][0, :]
    row = lax.broadcasted_iota(jnp.int32, (size, size), 0)
    col = lax.broadcasted_iota(jnp.int32, (size, size), 1)
    number = col >> log2_of(chunk)
    source = band_ref[0] - (number >> log2_of(per))
    source = jnp.where(source < 0, source + bands, source)
    item = source * per + (number & (per - 1))
    order = jnp.where(row == (col & (chunk - 1)) * items + item, 1.0, 0.0).astype(LOW)
    for at in range(2):
        loads[at].wait()
        for block in range(blocks):
            parts = held[at][:, block * chunk : (block + 1) * chunk, :].reshape(size, width)
            made[at][block * size : (block + 1) * size, :] = dot_nn(order, parts).astype(LOW)
        stores.append(bring(made[at], outs[at]))
        if at == 0:
            for copy, place, out in zip(passing, through, outs[2 : 2 + passed]):
                copy.wait()
                stores.append(bring(place, out))
    for store in stores:
        store.wait()


def merge_items(arrays, passed, flat, band, bands):
    items, band_rows, width = arrays[0].shape
    chunk = 32 if band_rows % 32 == 0 else 16
    outside = pl.BlockSpec(memory_space=pl.ANY)
    inside = pl.BlockSpec(memory_space=pltpu.VMEM)
    merged = pl.pallas_call(
        functools.partial(merge_kernel, items // bands, chunk, len(passed), len(flat)),
        name="merge_items",
        out_shape=[jax.ShapeDtypeStruct((band_rows * items, width), LOW)] * 2
        + [jax.ShapeDtypeStruct(array.shape, array.dtype) for array in passed]
        + [jax.ShapeDtypeStruct(array.shape[1:], array.dtype) for array in flat],
        in_specs=[smem()] + [outside] * (2 + len(passed)) + [inside] * len(flat),
        out_specs=[outside] * (2 + len(passed)) + [inside] * len(flat),
        scratch_shapes=[pltpu.VMEM((items, band_rows, width), LOW)] * 2
        + [pltpu.VMEM((band_rows * items, width), LOW)] * 2
        + [pltpu.SemaphoreType.DMA((4 * (band_rows // chunk) + 2 * len(passed),))]
        + [pltpu.VMEM(array.shape, array.dtype) for array in passed],
        compiler_params=params(60),
    )(jnp.reshape(band, (1,)), *arrays, *passed, *flat)
    return [array.reshape(band_rows, items, width) for array in merged[:2]], merged[2:]


def rope(vector, cos, sin):
    parts = []
    for at in range(0, vector.shape[0], HEAD_DIM):
        lower, upper = vector[at : at + HALF], vector[at + HALF : at + HEAD_DIM]
        parts += [lower * cos - upper * sin, lower * sin + upper * cos]
    return jnp.concatenate(parts, 0)


def query_blocks(seq):
    return [(start, min(start + BLOCK, seq)) for start in range(0, seq, BLOCK)]


def limits(start, stop, length):
    position = start + lax.broadcasted_iota(jnp.int32, (1, stop - start), 1)
    return jnp.minimum(position, length - 1)


def score_parts(keys, queries, start, stop, length):
    parts = []
    if start:
        parts.append((0, BLOCK, dot_tn(keys[:, :BLOCK], queries)))
    first = min(start, BLOCK)
    late = dot_tn(keys[:, first:stop], queries)
    position = first + lax.broadcasted_iota(jnp.int32, late.shape, 0)
    late = jnp.where(position <= limits(start, stop, length), late, NEG)
    parts.append((first, stop, late))
    return parts


def norm_rows(inputs):
    return lax.rsqrt(jnp.mean(inputs * inputs, -1, keepdims=True) + EPS)


def attend_item(length, x, weights, gain, cos, sin, query, key, value, attended_t, attended, log_total, normed, ready):
    seq, width = x.shape
    tile = 128
    for at in range(0, seq, tile):
        inputs = x[at : at + tile, :].astype(F32)
        normed[at : at + tile, :] = (inputs * norm_rows(inputs) * gain).astype(LOW)

    project = 256

    def project_tile(at, _):
        rows = pl.ds(pl.multiple_of(at * project, project), project)
        for part, out, scaled in ((0, query, SCALE * LOG2E), (1, key, 1.0)):
            source = pl.ds(pl.multiple_of(part * width + at * project, project), project)
            out[rows, :] = (rope(dot_nt(weights[source, :], normed[...]), cos[...], sin[...]) * scaled).astype(LOW)
        source = pl.ds(pl.multiple_of(2 * width + at * project, project), project)
        value[rows, :] = dot_nt(weights[source, :], normed[...]).astype(LOW)
        return 0

    lax.fori_loop(0, width // project, project_tile, 0)
    ready()

    def head(at, _):
        for which in range(4):
            number = at * 4 + which
            rows = pl.ds(pl.multiple_of(number * HEAD_DIM, HEAD_DIM), HEAD_DIM)
            keys, values = key[rows, :], value[rows, :]
            for start, stop in query_blocks(seq):
                parts = score_parts(keys, query[rows, start:stop], start, stop, length)
                top = functools.reduce(jnp.maximum, [jnp.max(s, 0, keepdims=True) for _, _, s in parts])
                total = jnp.zeros_like(top)
                acc = jnp.zeros((HEAD_DIM, stop - start), F32)
                for first, last, scores in parts:
                    prob = jnp.exp2(scores - top)
                    total += jnp.sum(prob, 0, keepdims=True)
                    acc += dot_nn(values[:, first:last], prob.astype(LOW))
                attended_t[rows, start:stop] = (acc / total).astype(LOW)
                log_total[number, :, start:stop] = top + jnp.log2(total)
        return 0

    lax.fori_loop(0, width // HEAD_DIM // 4, head, 0)
    for at in range(0, width, project):
        attended[:, at : at + project] = attended_t[at : at + project, :].T


LANES = 128
GROUP = 256
WIDE = 512


def feed_item(follows, x, attended, attended_t, cot, w_out, w_feed, w_down, gain, g_feed, g_down, g_out, g_norm, out, grad_attended_t, scratch, cot_ready, tick, out_done):
    normed, normed_t, resid, out_acc, back_acc = scratch
    seq, width = x.shape
    ff = w_down.shape[0]
    tile = 128

    def put(ref, at, grad):
        if follows:
            grad += ref[at].astype(F32)
        ref[at] = grad.astype(LOW)

    for at in range(0, seq, tile):
        rows = slice(at, at + tile)
        total = x[rows, :].astype(F32) + dot_nn(attended[rows, :], w_out[...])
        resid[rows, :] = total.astype(LOW)
        out_acc[rows, :] = total
        low = (total * norm_rows(total) * gain).astype(LOW)
        normed[rows, :] = low
        normed_t[:, rows] = low.T
    back_acc[...] = jnp.zeros_like(back_acc)
    cot_ready()

    def chunk(step, _):
        tick(step)
        span = pl.ds(pl.multiple_of(step * WIDE, WIDE), WIDE)
        up_span = pl.ds(pl.multiple_of(ff + step * WIDE, WIDE), WIDE)
        lows = []
        for at in range(0, seq, seq // 2):
            rows = slice(at, at + seq // 2)
            parts = []
            for first in range(0, WIDE, WIDE // 2):
                columns = pl.ds(pl.multiple_of(step * WIDE + first, WIDE // 2), WIDE // 2)
                up_columns = pl.ds(pl.multiple_of(ff + step * WIDE + first, WIDE // 2), WIDE // 2)
                gate = dot_nn(normed[rows, :], w_feed[:, columns])
                upward = dot_nn(normed[rows, :], w_feed[:, up_columns])
                grad_hidden = dot_nt(cot[rows, :], w_down[columns, :])
                sig = 0.5 * jnp.tanh(0.5 * gate) + 0.5
                silu = gate * sig
                hidden = (silu * upward).astype(LOW)
                grad_gate = (grad_hidden * upward * (sig + silu * (1.0 - sig))).astype(LOW)
                grad_upward = (grad_hidden * silu).astype(LOW)
                parts.append((hidden, grad_gate, grad_upward))
            hidden, grad_gate, grad_upward = (jnp.concatenate(both, 1) for both in zip(*parts))
            out_acc[rows, :] += dot_nn(hidden, w_down[span, :])
            back_acc[rows, :] += dot_nt(grad_gate, w_feed[:, span])
            back_acc[rows, :] += dot_nt(grad_upward, w_feed[:, up_span])
            lows.append((hidden, grad_gate, grad_upward))
        hidden, grad_gate, grad_upward = (jnp.concatenate(parts, 0) for parts in zip(*lows))
        half = WIDE // 2
        for at in range(0, WIDE, half):
            part = pl.ds(pl.multiple_of(step * WIDE + at, half), half)
            put(g_down, (part, slice(None)), dot_nn(hidden[:, at : at + half].T, cot[...]))
        first = pl.ds(pl.multiple_of(step * 2 * WIDE, WIDE), WIDE)
        second = pl.ds(pl.multiple_of(step * 2 * WIDE + WIDE, WIDE), WIDE)
        half = width // 2
        for at in range(0, width, half):
            part = slice(at, at + half)
            put(g_feed, (part, first), dot_nn(normed_t[part, :], grad_gate))
            put(g_feed, (part, second), dot_nn(normed_t[part, :], grad_upward))
        return 0

    lax.fori_loop(0, ff // WIDE, chunk, 0)
    for at in range(0, seq, tile):
        out[at : at + tile, :] = out_acc[at : at + tile, :].astype(LOW)
    out_done()
    norm_sum = jnp.zeros((1, width), F32)
    for at in range(0, seq, tile):
        rows = slice(at, at + tile)
        total, incoming = resid[rows, :].astype(F32), back_acc[rows, :]
        inv = norm_rows(total)
        scaled = total * inv
        norm_sum += jnp.sum(incoming * scaled, 0, keepdims=True)
        weighted = incoming * gain
        grad = cot[rows, :].astype(F32) + inv * (weighted - scaled * jnp.mean(weighted * scaled, -1, keepdims=True))
        cot[rows, :] = grad.astype(LOW)
    g_norm[...] = g_norm[...] + norm_sum if follows else norm_sum
    for at in range(0, width, GROUP):
        rows = slice(at, at + GROUP)
        grad_attended_t[rows, :] = dot_nt(w_out[rows, :], cot[...]).astype(LOW)
    for at in range(0, width, GROUP):
        rows = slice(at, at + GROUP)
        put(g_out, (rows, slice(0, width)), dot_nn(attended_t[rows, :], cot[...]))


PAIRS = GROUP // (2 * HEAD_DIM)


def back_item(
    follows, length, x, grad_resid, grad_attended, attended, query, key, value, log_total, weights, gain, cos, sin,
    g_weights, g_norm, grads, normed_t, back, tick, heads_done,
):
    seq, width = x.shape
    blocks = query_blocks(seq)
    tile = 128
    for at in range(0, seq, tile):
        inputs = x[at : at + tile, :].astype(F32)
        normed_t[:, at : at + tile] = (inputs * norm_rows(inputs) * gain).astype(LOW).T
    back[...] = jnp.zeros_like(back)

    def group(number, _):
        def pair(at, _):
            tick(number * PAIRS + at)
            for which in range(2):
                local = at * 2 + which
                head = number * (2 * PAIRS) + local
                rows = pl.ds(pl.multiple_of(head * HEAD_DIM, HEAD_DIM), HEAD_DIM)
                keys, values = key[rows, :], value[rows, :]
                delta_all = jnp.sum(grad_attended[rows, :].astype(F32) * attended[rows, :].astype(F32), 0, keepdims=True)
                key_grads = [0.0] * len(blocks)
                value_grads = [0.0] * len(blocks)
                at_query, at_key, at_value = (
                    pl.ds(pl.multiple_of(part * GROUP + local * HEAD_DIM, HEAD_DIM), HEAD_DIM) for part in range(3)
                )
                for start, stop in blocks:
                    queries, incoming = query[rows, start:stop], grad_attended[rows, start:stop]
                    total = log_total[head, :, start:stop]
                    delta = delta_all[:, start:stop]
                    query_grad = 0.0
                    for first, last, scores in score_parts(keys, queries, start, stop, length):
                        prob = jnp.exp2(scores - total)
                        grad_prob = dot_tn(values[:, first:last], incoming)
                        grad_score = (prob * (grad_prob - delta)).astype(LOW)
                        query_grad += dot_nn(keys[:, first:last], grad_score)
                        key_grad = dot_nt(queries, grad_score)
                        value_grad = dot_nt(incoming, prob.astype(LOW))
                        for piece, (low, high) in enumerate(blocks):
                            if first <= low and high <= last:
                                key_grads[piece] += key_grad[:, low - first : high - first]
                                value_grads[piece] += value_grad[:, low - first : high - first]
                    grads[at_query, start:stop] = (
                        rope(query_grad, cos[:, start:stop], -sin[:, start:stop]) * SCALE
                    ).astype(LOW)
                for (start, stop), key_grad, value_grad in zip(blocks, key_grads, value_grads):
                    grads[at_key, start:stop] = (
                        rope(key_grad, cos[:, start:stop], -sin[:, start:stop]) * (1.0 / LOG2E)
                    ).astype(LOW)
                    grads[at_value, start:stop] = value_grad.astype(LOW)
            return 0

        lax.fori_loop(0, PAIRS, pair, 0)
        turned = grads[...].T
        columns = pl.ds(pl.multiple_of(number * 3 * GROUP, GROUP), 3 * GROUP)
        for at in range(0, width, GROUP):
            rows = slice(at, at + GROUP)
            grad = dot_nn(normed_t[rows, :], turned)
            if follows:
                grad += g_weights[rows, columns].astype(F32)
            g_weights[rows, columns] = grad.astype(LOW)
        for at in range(0, seq, seq // 2):
            rows = slice(at, at + seq // 2)
            total = back[rows, :]
            for part in range(3):
                source = pl.ds(pl.multiple_of(part * width + number * GROUP, GROUP), GROUP)
                total += dot_nn(turned[rows, part * GROUP : (part + 1) * GROUP], weights[source, :])
            back[rows, :] = total
        return 0

    lax.fori_loop(0, width // GROUP, group, 0)
    heads_done()
    norm_sum = jnp.zeros((1, width), F32)
    for at in range(0, seq, tile):
        rows = slice(at, at + tile)
        inputs, incoming = x[rows, :].astype(F32), back[rows, :]
        inv = norm_rows(inputs)
        scaled = inputs * inv
        norm_sum += jnp.sum(incoming * scaled, 0, keepdims=True)
        weighted = incoming * gain
        grad = grad_resid[rows, :].astype(F32) + inv * (
            weighted - scaled * jnp.mean(weighted * scaled, -1, keepdims=True)
        )
        grad_resid[rows, :] = grad.astype(LOW)
    g_norm[...] = g_norm[...] + norm_sum if follows else norm_sum


class Links:
    def __init__(self, bands, axis, send, receive):
        self.send, self.receive, self.bands = send, receive, bands
        self.band, self.items = lax.axis_index("band"), lax.axis_index("items")
        self.item_bits, self.item_partners = bits_of(self.items, axis) if axis else ((), ())
        self.band_bits, self.band_partners = bits_of(self.band, bands)
        self.count = 0

    def take(self, count):
        first = self.count
        self.count += count
        return first

    def other(self, shift):
        return lax.rem(self.band + shift + self.bands, self.bands)

    def greet(self):
        barrier = pltpu.get_barrier_semaphore()
        others = [(self.items, self.other(shift)) for shift in range(1, self.bands)]
        others += [(partner, self.band) for partner in self.item_partners]
        for other in others:
            pl.semaphore_signal(barrier, inc=1, device_id=other, device_id_type=MESH)
        return lambda: pl.semaphore_wait(barrier, len(others))

    def copy(self, number, source, target, device):
        return pltpu.make_async_remote_copy(
            src_ref=source,
            dst_ref=target,
            send_sem=self.send.at[number],
            recv_sem=self.receive.at[number],
            device_id=device,
            device_id_type=MESH,
        )


class Exchange:
    def __init__(self, links, source, target, arrival):
        self.links, self.first = links, links.take(links.bands - 1)
        self.source, self.target, self.arrival = source, target, arrival

    def each(self, place):
        for shift in range(1, self.links.bands):
            yield self.links.copy(
                self.first + shift - 1, self.source(shift), place(shift), (self.links.items, self.links.other(shift))
            )

    def start(self):
        for copy in self.each(self.target):
            copy.start()

    def arrived(self):
        for copy in self.each(self.arrival):
            copy.wait_recv()

    def left(self):
        for copy in self.each(self.target):
            copy.wait_send()


def bits_of(number, size):
    bits = [lax.rem(lax.div(number, 2**at), 2) for at in range(log2_of(size))]
    return bits, [number + (1 - 2 * bit) * 2**at for at, bit in enumerate(bits)]


def sum_lanes(axis, stage, columns):
    left = list(range(log2_of(axis)))
    right = [0] + left[:0:-1]
    half = columns // 2
    if stage == 0:
        return [(left[0], left[1:], 0, columns)]
    return [(left[stage], left[stage + 1 :], 0, half), (right[stage], right[stage + 1 :], half, half)]


def band_shape(axis, bands, shape):
    rows = shape[0] // axis // bands
    return (rows, shape[1]) if rows % 16 == 0 else (2 * rows, shape[1] // 2)


def sum_scratch(axis, bands, shape):
    low = lambda *dims: pltpu.VMEM(dims, LOW)
    out = []
    for stage in range(log2_of(axis)):
        for _, bits, _, columns in sum_lanes(axis, stage, shape[1]):
            out.append(low(*(2,) * len(bits), shape[0] // axis, columns))
    part = band_shape(axis, bands, shape)
    out.append(low(*(2,) * log2_of(bands), *part))
    for stage in range(log2_of(bands)):
        out.append(low(*(2,) * (log2_of(bands) - stage - 1), *part))
    return out


def sum_links(axis, bands):
    return 2 * log2_of(axis) + log2_of(bands)


class Summing:
    def __init__(self, links, axis, array, first, columns, scratch, finish):
        self.links, self.array, self.finish = links, array, finish
        self.first, self.columns, self.scratch = first, columns, scratch
        self.axis, self.count = axis, log2_of(axis)
        self.stages = self.count + log2_of(links.bands)
        self.base = links.take(sum_links(axis, links.bands))
        self.state = 0

    def flights(self, stage):
        links = self.links
        if stage < self.count:
            rows, wide = self.array.shape
            view = self.array.reshape(*(2,) * self.count, rows // self.axis, wide)
            bits, partners, used = links.item_bits, links.item_partners, [0] if stage == 0 else [2 * stage - 1, 2 * stage]
            lanes = sum_lanes(self.axis, stage, self.columns)
            first = self.first
        else:
            view, first = self.scratch[2 * self.count - 1], 0
            bits, partners, used = links.band_bits, links.band_partners, [self.count + stage]
            at = stage - self.count
            lanes = [(at, list(range(at + 1, len(bits))), 0, view.shape[-1])]
        out = []
        for (now, later, start, columns), number in zip(lanes, used):
            place = lambda own: tuple(
                slice(None) if at in later else 1 - bits[at] if at == now and not own else bits[at]
                for at in reversed(range(len(bits)))
            ) + (slice(None), pl.ds(first + start, columns))
            partner = partners[now]
            device = (partner, links.band) if stage < self.count else (links.items, partner)
            came = self.scratch[number]
            out.append((links.copy(self.base + number, view.at[place(False)], came, device), view.at[place(True)], came))
        return out

    def begin(self, stage):
        for copy, _, _ in self.flights(stage):
            copy.start()

    def end(self, stage):
        flights = self.flights(stage)
        for copy, _, _ in flights:
            copy.wait_recv()
            copy.wait_send()
        for _, kept, came in flights:
            if stage == self.stages - 1:
                self.finish(kept[...].astype(F32) + came[...].astype(F32))
                continue
            rows = came.shape[-2]
            tile = 48 if rows % 48 == 0 else 32 if rows % 32 == 0 else 16
            for choice in np.ndindex(*came.shape[:-2]):

                def add(step, _, kept=kept, came=came, choice=choice):
                    span = choice + (pl.ds(pl.multiple_of(step * tile, tile), tile), slice(None))
                    kept[span] = kept[span] + came[span]
                    return 0

                lax.fori_loop(0, rows // tile, add, 0)
        if stage == self.count - 1:
            self.stack()

    def stack(self):
        bands, parts = self.links.bands, self.scratch[2 * self.count - 1]
        rows = self.array.shape[0] // self.axis
        start = pl.multiple_of(self.links.items * rows, rows)
        whole = self.array.at[pl.ds(start, rows), pl.ds(self.first, self.columns)]
        rows = rows // bands
        spans = [slice(number * rows, (number + 1) * rows) for number in range(bands)]
        places = list(np.ndindex(*parts.shape[:-2]))
        if parts.shape[-2] == rows:
            for place, span in zip(places, spans):
                parts[place] = whole[span, :]
            return
        half = self.columns // 2
        left, right = whole[:, :half].astype(F32), whole[:, half:].astype(F32)
        for place, span in zip(places, spans):
            parts[place] = jnp.concatenate([left[span], right[span]], 0).astype(LOW)

    def advance(self):
        if self.state > self.stages:
            return
        if self.state > 0:
            self.end(self.state - 1)
        if self.state < self.stages:
            self.begin(self.state)
        self.state += 1


def block_kernel(bands, per, axis, *refs):
    fused = axis > 0
    lengths, norm_attn, norm_ffn, cos, sin = refs[:5]
    tokens, cotangent, w_query, w_key, w_value, w_out_from, w_gate, w_up, w_down_from = refs[5:14]
    refs = refs[14:]
    home_out, home_grad = refs[:2]
    query_far, key_far, value_far, attended_t_far, grad_attended_t_far, cot_far = refs[2:8]
    refs = refs[8:]
    sums, refs = (refs[:9], refs[9:]) if fused else (refs[:6], refs[6:])
    weights_t, w_out, w_feed, w_down, g_feed, g_down, g_out = refs[:7]
    x, cot, attended, attended_t, query, key, value, grad_attended_t = refs[7:15]
    normed, normed_t, resid, out_acc, back_acc, log_total, g_norm, g_norm_ffn = refs[15:23]
    w_own, w_total, local, send, receive = refs[23:28]
    sum_refs = refs[28:]
    seq, width = x.shape[1:]
    ff = w_down.shape[0]
    band_rows, items = seq // bands, bands * per
    groups = width // GROUP
    links = Links(bands, axis, send, receive)
    band = links.band
    gain_attn, gain_ffn = norm_attn[...][None, :], norm_ffn[...][None, :]
    started = [0]

    def bring(source, target):
        copy = pltpu.make_async_copy(source, target, local.at[started[0]])
        started[0] += 1
        copy.start()
        return copy

    token_rows = band_rows * items
    chunk = 32 if band_rows % 32 == 0 else 16
    size = items * chunk
    raw = g_down.at[pl.ds(0, token_rows)]
    spans = [pl.ds(at, size) for at in range(0, token_rows, size)]
    load_tokens = [bring(tokens.at[span], raw.at[span]) for span in spans]
    qkv = (g_feed.at[:, pl.ds(0, width)], g_feed.at[:, pl.ds(width, width)], g_feed.at[:, pl.ds(2 * width, width)])
    load_qkv = [bring(source, target) for source, target in zip((w_query, w_key, w_value), qkv)]
    all_here = links.greet()

    def own_rows(shift):
        return pl.ds(pl.multiple_of(links.other(shift) * band_rows, band_rows), band_rows)

    token_send = [attended.at[item] for item in range(per)]
    stages = [normed, resid]
    cot_send = [g_out.at[:, pl.ds(0, width)]] + [cot_far.at[item] for item in range(per - 1)]

    def split(kept, sent, item, loads=()):
        order = split_order(bands, per, chunk, band, item)
        for block in range(band_rows // chunk):
            if loads:
                loads[block].wait()
            moved = dot_nn(order, raw[block * size : (block + 1) * size, :]).astype(LOW)
            kept[item, pl.ds(pl.multiple_of(band * band_rows + block * chunk, 16), chunk), :] = moved[:chunk]
            for shift in range(1, bands):
                place = (shift - 1) * band_rows + block * chunk
                sent[place : place + chunk, :] = moved[shift * chunk : (shift + 1) * chunk]

    def scattering(sent, kept, item):
        return Exchange(
            links,
            lambda shift: sent[item].at[pl.ds((shift - 1) * band_rows, band_rows)],
            lambda shift: kept.at[item, own_rows(0)],
            lambda shift: kept.at[item, own_rows(-shift)],
        )

    def returning(source, home, item):
        slot = lambda shift: home.at[shift * per + item]
        return Exchange(links, lambda shift: source.at[item, own_rows(shift)], slot, slot)

    token_links = [scattering(token_send, x, item) for item in range(per)]
    cot_links = [scattering(cot_send, cot, item) for item in range(per)]
    out_links = [returning(attended, home_out, item) for item in range(per)]
    grad_links = [returning(cot, home_grad, item) for item in range(per)]

    split(x, token_send[0], 0, load_tokens)
    all_here()
    token_links[0].start()
    for item in range(1, per):
        split(x, token_send[item], item)
    load_cot = bring(cotangent, raw)
    load_rest = [
        bring(w_out_from, w_out),
        bring(w_gate, w_feed.at[:, pl.ds(0, ff)]),
        bring(w_up, w_feed.at[:, pl.ds(ff, ff)]),
        bring(w_down_from, w_down),
    ]
    for part in range(3):
        load_qkv[part].wait()
        for at in range(0, width, 256):
            weights_t[part * width + at : part * width + at + 256, :] = qkv[part][:, at : at + 256].T
        if fused:
            own = w_own.shape[0]
            device = links.items * bands + band
            if part == 0:
                halves_of = axis * bands // 2
                column = jnp.concatenate([gain_attn, jnp.zeros((LANES - 1, width), F32)], 0).T
                out_acc[: width // 2, :LANES] = column[: width // 2]
                out_acc[: width // 2, LANES : 2 * LANES] = column[width // 2 :]
                at = pl.multiple_of(lax.rem(device, halves_of) * own, 8)
                both = out_acc[pl.ds(at, own), : 2 * LANES]
                own_gain = 1.0 / jnp.where(device < halves_of, both[:, :1], both[:, LANES : LANES + 1])
            both = qkv[part][pl.ds(pl.multiple_of(lax.div(device, 2) * (2 * own), 16), 2 * own), :].astype(F32)
            mine = jnp.where(lax.rem(device, 2) == 0, both[:own], both[own:]) * own_gain
            for number in range(groups):
                at = (number * 3 + part) * GROUP
                w_own[:, at : at + GROUP] = mine[:, number * GROUP : (number + 1) * GROUP]
    load_cot.wait()
    for item in range(per):
        split(cot, stages[item - 1] if item else cot_send[0], item)
    late = pl.ds(0, (bands - 1) * band_rows)
    to_far = [bring(stages[item].at[late], cot_far.at[item]) for item in range(per - 1)]

    sums_of = {}
    schedule = {}
    if fused:
        scratch_each = len(sum_scratch(axis, bands, (axis * bands * 16, 256)))
        taken = [0]
        o_gate, o_up, o_down, o_out, o_query, o_key, o_value, o_norm_ffn, o_norm_attn = sums
        w_total[...] = jnp.zeros_like(w_total)

        def summing(name, array, first, columns, finish):
            sums_of[name] = Summing(
                links, axis, array, first, columns, sum_refs[taken[0] : taken[0] + scratch_each], finish
            )
            taken[0] += scratch_each

        def halves(total):
            rows = total.shape[0] // 2
            return total[:rows], total[rows:]

        for step in range(ff // WIDE):

            def finish_feed(total, step=step):
                span = slice(step * WIDE, (step + 1) * WIDE)
                o_gate[:, span], o_up[:, span] = halves(total)

            summing(("feed", step), g_feed, step * 2 * WIDE, 2 * WIDE, finish_feed)

        def finish_down(total):
            o_down[...] = total

        def finish_out(total):
            left, right = halves(total)
            half = left.shape[1]
            o_out[:, :half] = left
            o_out[:, half:] = right[:, : width - half]
            o_norm_ffn[...] = right[:, width - half : width - half + LANES].T[:1, :]

        summing("down", g_down, 0, width, finish_down)
        summing("out", g_out, 0, width + 2 * LANES, finish_out)
        for number in range(groups):

            def finish_group(total, number=number):
                left, right = halves(total)
                at, half = number * GROUP, GROUP // 2
                own = w_own[:, 3 * at : 3 * at + 3 * GROUP]
                middle = left.shape[1]
                w_total[...] += jnp.sum(left * own[:, :middle] + right * own[:, middle:], -1, keepdims=True)
                o_query[:, at : at + GROUP] = left[:, :GROUP]
                o_key[:, at : at + half] = left[:, GROUP:]
                o_key[:, at + half : at + GROUP] = right[:, :half]
                o_value[:, at : at + GROUP] = right[:, half:]

            summing(("back", number), w_feed, number * 3 * GROUP, 3 * GROUP, finish_group)

    def advance(*names):
        for name in names:
            sums_of[name].advance()

    spills = []

    def spill(pairs):
        spills.extend(bring(source, target) for source, target in pairs)

    def settle():
        while spills:
            spills.pop().wait()

    g_weights = w_feed
    grads = w_feed.at[pl.ds(0, 3 * GROUP), pl.ds(3 * width, seq)]
    for item in range(per):
        last = item == per - 1
        if item == 0:
            token_links[0].arrived()
            cot_links[0].start()
            for copy in to_far:
                copy.wait()
        settle()

        def projected(item=item):
            token_links[item].left()
            if item < per - 1:
                spill(
                    (source, target.at[item])
                    for source, target in ((query, query_far), (key, key_far), (value, value_far))
                )

        attend_item(
            lengths[band * per + item], x.at[item], weights_t, gain_attn, cos, sin, query, key, value, attended_t,
            attended.at[item], log_total.at[item], normed, projected,
        )
        if item == 0:
            for load in load_rest:
                load.wait()
        def cot_ready(item=item, last=last):
            cot_links[item].arrived()
            if not last:
                token_links[item + 1].start()
            elif per > 1:
                out_links[item - 1].start()
            cot_links[item].left()

        def feed_tick(step, item=item, last=last):
            if not last:

                @pl.when(step == ff // WIDE - 1)
                def _():
                    token_links[item + 1].arrived()
                    cot_links[item + 1].start()

            elif fused:
                for at in range(1, ff // WIDE):

                    @pl.when(step == at)
                    def _(at=at):
                        advance(*[("feed", number) for number in range(at)])

        feed_item(
            item > 0, x.at[item], attended.at[item], attended_t, cot.at[item], w_out, w_feed, w_down, gain_ffn,
            g_feed, g_down, g_out, g_norm_ffn, attended.at[item], grad_attended_t,
            (normed, normed_t, resid, out_acc, back_acc), cot_ready, feed_tick, out_links[item].start if last else lambda: None,
        )
        if not last:
            spill(
                (source, target.at[item])
                for source, target in ((attended_t, attended_t_far), (grad_attended_t, grad_attended_t_far))
            )
    feeds = [("feed", step) for step in range(ff // WIDE)]
    backs = [("back", number) for number in range(groups)]
    if fused:
        column = jnp.concatenate([g_norm_ffn[...], jnp.zeros((LANES - 1, width), F32)], 0).T
        g_out[:, width : width + LANES] = column.astype(LOW)
        g_out[:, width + LANES :] = jnp.zeros((width, LANES), LOW)
        advance(*feeds, "down", "out")
    turns = list(reversed(range(per)))
    reloads = []
    for turn, item in enumerate(turns):
        last = turn == per - 1

        def back_tick(at, turn=turn, last=last):
            if not fused:
                return
            for place, names in plan(turn, last).items():

                @pl.when(at == place)
                def _(names=names):
                    advance(*names)

        def plan(turn, last):
            out = {place: [] for place in range(groups * PAIRS)}
            if turn == 0:
                out[1] = feeds[1:]
                out[3] = feeds[2:] + ["down", "out"]
                out[5] = feeds[3:]
            if turn == 1:
                out[2] = feeds + ["down", "out"]
                out[4] = ["down", "out"]
            if last:
                for number in range(groups - 1):
                    for place in range((number + 1) * PAIRS, groups * PAIRS):
                        out[place].append(backs[number])
            return {place: names for place, names in out.items() if names}

        def heads_done(turn=turn, last=last):
            if not last:
                following = turns[turn + 1]
                for source, target in (
                    (query_far, query), (key_far, key), (value_far, value), (attended_t_far, attended_t),
                    (grad_attended_t_far, grad_attended_t),
                ):
                    reloads.append(bring(source.at[following], target))
            elif fused:
                advance(backs[-1])

        back_item(
            turn > 0, lengths[band * per + item], x.at[item], cot.at[item], grad_attended_t, attended_t, query, key,
            value, log_total.at[item], weights_t, gain_attn, cos, sin, g_weights, g_norm, grads, normed_t, back_acc,
            back_tick, heads_done,
        )
        grad_links[item].start()
        while reloads:
            reloads.pop().wait()
    own = []
    for item in range(per):
        own.append(bring(attended.at[item, own_rows(0)], home_out.at[item]))
        own.append(bring(cot.at[item, own_rows(0)], home_grad.at[item]))
    if fused:
        every = feeds + ["down", "out"] + backs
        first, *_, last = backs
        for names in ([last] + backs[1:-1], [last] + backs[1:-1], ["down", "out", first], [last], backs[1:-1], [last]):
            advance(*names)
        while any(sums_of[name].state <= sums_of[name].stages for name in every):
            least = min(sums_of[name].state for name in every)
            advance(*[name for name in every if sums_of[name].state == least])
        o_norm_attn[...] = w_total[...].T[:1, :]
    else:
        own += [
            bring(source, target)
            for source, target in zip(
                (g_feed, g_down, g_out.at[:, pl.ds(0, width)], g_weights.at[:, pl.ds(0, 3 * width)]), sums[:4]
            )
        ]
        sums[4][...] = g_norm_ffn[...]
        sums[5][...] = g_norm[...]
    for copy in own:
        copy.wait()
    for item in range(per):
        for exchange in (out_links[item], grad_links[item]):
            exchange.arrived()
            exchange.left()


def block(bands, axis, lengths, tokens, cotangent, gains, tables, weights):
    band_rows, items, width = tokens.shape
    per, seq, ff = items // bands, bands * band_rows, weights[4].shape[1]
    fused = axis > 0
    low = lambda *shape: jax.ShapeDtypeStruct(shape, LOW)
    full = lambda *shape: jax.ShapeDtypeStruct(shape, F32)
    scratch = lambda *shape: pltpu.VMEM(shape, LOW)
    wide = lambda *shape: pltpu.VMEM(shape, F32)
    outside = pl.BlockSpec(memory_space=pl.ANY)
    inside = pl.BlockSpec(memory_space=pltpu.VMEM)
    out_shape = [low(items, band_rows, width)] * 2 + [low(max(per - 1, 1), width, seq)] * 5
    out_shape += [low(max(per - 1, 1), (bands - 1) * band_rows, width)]
    out_specs = [outside] * 8
    extra, links = [], 4 * per * (bands - 1)
    if fused:
        devices = axis * bands
        rows, ff_rows = width // devices, ff // devices
        out_shape += [full(rows, ff), full(rows, ff), full(ff_rows, width)] + [full(rows, width)] * 4 + [full(1, rows)] * 2
        out_specs += [inside] * 9
        shapes = [(width, 2 * WIDE)] * (ff // WIDE) + [(ff, width), (width, width + 2 * LANES)]
        shapes += [(width, 3 * GROUP)] * (width // GROUP)
        for shape in shapes:
            extra += sum_scratch(axis, bands, shape)
        links += len(shapes) * sum_links(axis, bands)
    else:
        out_shape += [low(width, 2 * ff), low(ff, width), low(width, width), low(width, 3 * width)] + [full(1, width)] * 2
        out_specs += [outside] * 4 + [inside] * 2
    return pl.pallas_call(
        functools.partial(block_kernel, bands, per, axis),
        name="block",
        out_shape=out_shape,
        in_specs=[smem()] + [inside] * 4 + [outside] * 9,
        out_specs=out_specs,
        scratch_shapes=[
            scratch(3 * width, width), scratch(width, width), scratch(width, 2 * ff), scratch(ff, width),
            scratch(width, 2 * ff), scratch(ff, width), scratch(width, width + 2 * LANES),
            scratch(per, seq, width), scratch(per, seq, width), scratch(per, seq, width), scratch(width, seq),
            scratch(width, seq), scratch(width, seq), scratch(width, seq), scratch(width, seq),
            scratch(seq, width), scratch(width, seq), scratch(seq, width), wide(seq, width), wide(seq, width),
            wide(per, width // HEAD_DIM, 1, seq), wide(1, width), wide(1, width),
            wide(max(width // (max(axis, 1) * bands), 8), 3 * width), wide(max(width // (max(axis, 1) * bands), 8), LANES),
            pltpu.SemaphoreType.DMA((32 + 12 * per,)),
            pltpu.SemaphoreType.DMA((links,)),
            pltpu.SemaphoreType.DMA((links,)),
        ]
        + extra,
        compiler_params=pltpu.CompilerParams(vmem_limit_bytes=64 * 2**20 - 2**16, collective_id=0, has_side_effects=True),
    )(
        lengths, *gains, *tables, tokens.reshape(band_rows * items, width), cotangent.reshape(band_rows * items, width),
        *weights,
    )


def rope_tables(seq):
    frequency = np.exp(-np.log(ROPE_BASE) * (2.0 * np.arange(HALF) / HEAD_DIM))
    angles = frequency[:, None] * np.arange(seq)[None, :]
    return jnp.asarray(np.cos(angles), F32), jnp.asarray(np.sin(angles), F32)


def per_device(
    bands,
    axis,
    tokens,
    lengths,
    norm_attn,
    w_query,
    w_key,
    w_value,
    w_out,
    norm_ffn,
    w_gate,
    w_up,
    w_down,
    cotangent,
):
    band_rows, items, width = tokens.shape
    per = items // bands
    seq = bands * band_rows
    band = lax.axis_index("band")
    whole_tiles = width // axis % 16 == 0 and width // axis // bands % 16 == 8 and w_gate.shape[1] // axis // bands % 16 == 0
    fused = axis if whole_tiles else 0
    home_out, home_grad, *sums = block(
        bands, fused, lengths, tokens, cotangent, (norm_attn, norm_ffn), rope_tables(seq),
        (w_query, w_key, w_value, w_out, w_gate, w_up, w_down),
    )
    sums = sums[6:]
    if fused:
        (output, grad_tokens), sums = merge_items([home_out, home_grad], sums[:-2], sums[-2:], band, bands)
        g_gate, g_up, g_down, g_out, g_query, g_key, g_value, g_norm_ffn, g_norm_attn = sums
    else:
        (output, grad_tokens), norms = merge_items([home_out, home_grad], [], sums[-2:], band, bands)
        axes = ("items", "band")
        total = lambda a: lax.psum_scatter(a, axes, scatter_dimension=0, tiled=True).astype(F32)
        g_feed, g_down, g_out, g_weights = (total(a) for a in sums[:4])
        norms = total(jnp.stack(norms, 1))
        g_norm_ffn, g_norm_attn = norms[:, 0], norms[:, 1]
        g_gate, g_up = jnp.moveaxis(g_feed.reshape(-1, w_gate.shape[1] // WIDE, 2, WIDE), 2, 0).reshape(2, -1, w_gate.shape[1])
        g_query, g_key, g_value = jnp.moveaxis(g_weights.reshape(-1, width // GROUP, 3, GROUP), 2, 0).reshape(3, -1, width)
    return (
        output,
        grad_tokens,
        g_norm_attn,
        g_query,
        g_key,
        g_value,
        g_out,
        g_norm_ffn,
        g_gate,
        g_up,
        g_down,
    )


def solution(mesh):
    split = P("band", "items", None)
    rows = P(("items", "band"), None)
    flat = P(("items", "band"))
    return jax.shard_map(
        functools.partial(per_device, mesh.shape["band"], mesh.shape["items"]),
        mesh=mesh,
        in_specs=(split, P("items")) + (P(),) * 9 + (split,),
        out_specs=(split, split, flat, rows, rows, rows, rows, flat, rows, rows, rows),
        check_vma=False,
    )
```
